32 devices in a mesh: dp: 8 (over y, x, core), tensor: 4 (over z).
Axes of the slice: x: 2, y: 2, z: 4, core: 2. Of those that a mesh axis runs over, the one named last changes fastest.
Arguments:
- inputs: bfloat16 [8, 768, 512], P('dp', 'tensor'), may hold values from -6 to 6
- lengths: int32 [8], P('dp'), may hold values from 577 to 768, as said below
- rel_embed: bfloat16 [1535, 512], replicated, may hold values from -6 to 6
- out_grad: bfloat16 [8, 768, 512], P('dp', 'tensor'), may hold values from -6 to 6
- norm_gain: bfloat16 [5, 512], P(None, 'dp'), may hold values from 0.099609375 to 1.8984375
- norm_bias: bfloat16 [5, 512], P(None, 'dp'), may hold values from -3 to 3
- ffn1_in: bfloat16 [512, 2048], P('dp', 'tensor'), may hold values from -0.25 to 0.25
- ffn1_out: bfloat16 [2048, 512], P('tensor', 'dp'), may hold values from -0.125 to 0.125
- query_w: bfloat16 [512, 512], P('dp', 'tensor'), may hold values from -0.25 to 0.25
- key_w: bfloat16 [512, 512], P('dp', 'tensor'), may hold values from -0.25 to 0.25
- value_w: bfloat16 [512, 512], P('dp', 'tensor'), may hold values from -0.25 to 0.25
- pos_w: bfloat16 [512, 512], P('dp', 'tensor'), may hold values from -0.25 to 0.25
- attn_out: bfloat16 [512, 512], P('tensor', 'dp'), may hold values from -1.5 to 1.5
- pos_bias: bfloat16 [2, 512], P(None, 'tensor'), may hold values from -3 to 3
- conv_value: bfloat16 [512, 512], P('dp', 'tensor'), may hold values from -0.25 to 0.25
- conv_gate: bfloat16 [512, 512], P('dp', 'tensor'), may hold values from -0.25 to 0.25
- depthwise: bfloat16 [31, 512], P(None, 'tensor'), may hold values from -1 to 1
- bn_gain: bfloat16 [512], P('tensor'), may hold values from 0.099609375 to 1.8984375
- bn_bias: bfloat16 [512], P('tensor'), may hold values from -3 to 3
- conv_out: bfloat16 [512, 512], P('tensor', 'dp'), may hold values from -0.25 to 0.25
- ffn2_in: bfloat16 [512, 2048], P('dp', 'tensor'), may hold values from -0.25 to 0.25
- ffn2_out: bfloat16 [2048, 512], P('tensor', 'dp'), may hold values from -0.125 to 0.125
Outputs:
- block_out: bfloat16 [8, 768, 512], P('dp', 'tensor')
- input_grad: float32 [8, 768, 512], P('dp', 'tensor')
- norm_gain_grad: float32 [5, 512], P(None, 'dp')
- norm_bias_grad: float32 [5, 512], P(None, 'dp')
- ffn1_in_grad: float32 [512, 2048], P('dp', 'tensor')
- ffn1_out_grad: float32 [2048, 512], P('tensor', 'dp')
- query_grad: float32 [512, 512], P('dp', 'tensor')
- key_grad: float32 [512, 512], P('dp', 'tensor')
- value_grad: float32 [512, 512], P('dp', 'tensor')
- pos_grad: float32 [512, 512], P('dp', 'tensor')
- attn_out_grad: float32 [512, 512], P('tensor', 'dp')
- pos_bias_grad: float32 [2, 512], P(None, 'tensor')
- conv_value_grad: float32 [512, 512], P('dp', 'tensor')
- conv_gate_grad: float32 [512, 512], P('dp', 'tensor')
- depthwise_grad: float32 [31, 512], P(None, 'tensor')
- bn_gain_grad: float32 [512], P('tensor')
- bn_bias_grad: float32 [512], P('tensor')
- conv_out_grad: float32 [512, 512], P('tensor', 'dp')
- ffn2_in_grad: float32 [512, 2048], P('dp', 'tensor')
- ffn2_out_grad: float32 [2048, 512], P('tensor', 'dp')
The draws below stay inside these ranges and needn't reach their ends.
Inputs may be any that keep to these rules, and one draw needn't show every extreme that they name: `lengths`: every valid length is more than three quarters of 768; in every draw some sequence has exactly 768.
All inputs are finite; a program needn't handle non-finite values.
Results may differ from the reference program's by a relative error of at most 0.04.
Values may be sent and summed in bfloat16 or wider, within the bound.
No kernel may reach another device: no remote copies, remote signals or barrier semaphores. Data moves between devices by JAX's collectives and lax.ppermute only.
A program may use at most 128 MiB of HBM per device.

```python
import jax
import jax.numpy as jnp
from jax import lax

D = 512
H = 8
DH = 64
FF = 2048
KER = 31
SEQ_LEN = 768
SEQS = 8
NREL = 1535


def draw_lengths(key, part):
    key = jax.random.fold_in(key, 7)
    first_key, second_key = jax.random.split(key)
    drawn = jax.random.randint(first_key, (SEQS,), SEQ_LEN - SEQ_LEN // 4 + 1, SEQ_LEN + 1)
    chosen = jax.random.randint(second_key, (), 0, SEQS)
    return jnp.where(jnp.arange(SEQS) == chosen, SEQ_LEN, drawn).astype(jnp.int32)


def block_scale(stream_key, extent, cuts, low, top_value):
    loudness = 1.0
    for dim, blocks in cuts:
        steps = jax.random.uniform(jax.random.fold_in(jax.random.fold_in(stream_key, 6), dim), (blocks,), jnp.float32, low / len(cuts), top_value / len(cuts))
        loudness = loudness * jnp.repeat(jnp.exp(steps), extent[dim] // blocks).reshape((-1,) + (1,) * (len(extent) - 1 - dim))
    return loudness


def normal_values(stream_key, extent, width, bound, shards=(), held_as=jnp.bfloat16):
    entries = width * jax.random.normal(stream_key, extent, jnp.float32)
    if shards:
        entries = entries * block_scale(stream_key, extent, shards, -0.22, 0.18)
    return jnp.clip(entries, -bound, bound).astype(held_as)


def setup_inputs(seed: int = 0) -> dict:
    key_list = jax.random.split(jax.random.key(seed), 23)
    return {
        "inputs": normal_values(key_list[0], (SEQS, SEQ_LEN, D), 1.0, 6.0, ((0, 8), (1, 4))),
        "lengths": draw_lengths(jax.random.fold_in(key_list[22], 71), 0),
        "rel_embed": normal_values(key_list[2], (NREL, D), 1.0, 6.0),
        "out_grad": normal_values(key_list[3], (SEQS, SEQ_LEN, D), 1.0, 6.0, ((0, 8), (1, 4))),
        "norm_gain": jnp.clip(1.0 + 0.18 * jax.random.normal(key_list[4], (5, D), jnp.float32), 0.099609375, 1.8984375).astype(jnp.bfloat16),
        "norm_bias": normal_values(key_list[5], (5, D), 0.3, 3.0, ((1, 8),)),
        "ffn1_in": normal_values(key_list[6], (D, FF), D ** -0.5, 0.25, ((0, 8), (1, 4))),
        "ffn1_out": normal_values(key_list[7], (FF, D), FF ** -0.5, 0.125, ((0, 4), (1, 8))),
        "query_w": normal_values(key_list[8], (D, D), D ** -0.5, 0.25, ((0, 8), (1, 4))),
        "key_w": normal_values(key_list[9], (D, D), D ** -0.5, 0.25, ((0, 8), (1, 4))),
        "value_w": normal_values(key_list[10], (D, D), D ** -0.5, 0.25, ((0, 8), (1, 4))),
        "pos_w": normal_values(key_list[11], (D, D), D ** -0.5, 0.25, ((0, 8), (1, 4))),
        "attn_out": normal_values(key_list[12], (D, D), (D // 32) ** -0.5, 1.5, ((0, 4), (1, 8))),
        "pos_bias": normal_values(key_list[13], (2, D), 0.5, 3.0, ((1, 4),)),
        "conv_value": normal_values(key_list[14], (D, D), D ** -0.5, 0.25, ((0, 8), (1, 4))),
        "conv_gate": normal_values(key_list[15], (D, D), D ** -0.5, 0.25, ((0, 8), (1, 4))),
        "depthwise": normal_values(key_list[16], (KER, D), KER ** -0.5, 1.0, ((1, 4),)),
        "bn_gain": jnp.clip(1.0 + 0.18 * jax.random.normal(key_list[17], (D,), jnp.float32), 0.099609375, 1.8984375).astype(jnp.bfloat16),
        "bn_bias": normal_values(key_list[18], (D,), 0.3, 3.0, ((0, 4),)),
        "conv_out": normal_values(key_list[19], (D, D), D ** -0.5, 0.25, ((0, 4), (1, 8))),
        "ffn2_in": normal_values(key_list[20], (D, FF), D ** -0.5, 0.25, ((0, 8), (1, 4))),
        "ffn2_out": normal_values(key_list[21], (FF, D), FF ** -0.5, 0.125, ((0, 4), (1, 8))),
    }


EPS = 1e-05
NEG = -1000000000.0
HIGHEST = lax.Precision.HIGHEST

@jax.custom_vjp
def low(v):
    return lax.optimization_barrier(v.astype(jnp.bfloat16)).astype(jnp.float32)

@jax.custom_vjp
def low_back(v):
    return v

def low_keep(v):
    return (low(v), None)

def low_pass(kept, grad):
    return (grad,)

def back_keep(v):
    return (v, None)

def back_low(kept, grad):
    return (low(grad),)
low.defvjp(low_keep, low_pass)
low_back.defvjp(back_keep, back_low)

def matmul(left, right):
    return jnp.dot(left, right, precision=HIGHEST, preferred_element_type=jnp.float32)

def layer_norm(stream, gain, beta_row):
    centered = stream - lax.optimization_barrier(jnp.mean(stream, -1, keepdims=True))
    return centered * lax.rsqrt(lax.optimization_barrier(jnp.mean(centered * centered, -1, keepdims=True)) + EPS) * gain + beta_row

def rel_shift(pos_table):
    span_len = pos_table.shape[1]
    flattened = pos_table.reshape(pos_table.shape[0], span_len * (2 * span_len - 1))
    flattened = flattened[:, span_len - 1:span_len - 1 + span_len * (2 * span_len - 2)]
    return flattened.reshape(pos_table.shape[0], span_len, 2 * span_len - 2)[:, :, :span_len]

def feed_forward(stream, gain, beta_row, proj_in, proj_out):

    def one_seq(seq_rows):
        normed = low(layer_norm(seq_rows, gain, beta_row))
        inner_act = low_back(matmul(normed, proj_in))
        hidden = low(jax.nn.silu(inner_act))
        return low_back(matmul(hidden, proj_out))
    return lax.map(jax.checkpoint(one_seq), stream)

def attention(stream, lengths, gain, beta_row, query_mat, key_mat, value_mat, pos_mat, attn_mat, pair_bias, rel_table):
    positions = low(matmul(rel_table, pos_mat)).reshape(NREL, H, DH)
    bias_u = pair_bias[0].reshape(H, DH)
    bias_v = pair_bias[1].reshape(H, DH)

    def one_seq(seq_item):
        seq_rows, seq_length = seq_item
        normed = low(layer_norm(seq_rows, gain, beta_row))
        queries = low_back(matmul(normed, query_mat)).reshape(SEQ_LEN, H, DH)
        keys_low = low(low_back(matmul(normed, key_mat))).reshape(SEQ_LEN, H, DH)
        values_low = low(low_back(matmul(normed, value_mat))).reshape(SEQ_LEN, H, DH)
        query_u = low(queries + bias_u)
        query_v = low(queries + bias_v)
        content = jnp.einsum('ihd,jhd->hij', query_u, keys_low, precision=HIGHEST)
        pos_table = jnp.einsum('ihd,rhd->hir', query_v, positions, precision=HIGHEST)
        scores = low_back(content + rel_shift(pos_table)) * DH ** (-0.5)
        visible = jnp.arange(SEQ_LEN) < seq_length
        scores = jnp.where(visible[None, None, :], scores, NEG)
        shifted = scores - lax.optimization_barrier(jnp.max(scores, -1, keepdims=True))
        exponent = jnp.exp(shifted)
        soft_probs = low(exponent / lax.optimization_barrier(jnp.sum(exponent, -1, keepdims=True)))
        mixed = low(low_back(jnp.einsum('hij,jhd->ihd', soft_probs, values_low, precision=HIGHEST)))
        return low_back(matmul(mixed.reshape(SEQ_LEN, D), attn_mat))
    return lax.map(jax.checkpoint(one_seq), (stream, lengths))

def convolution(stream, pad_mask, gain, beta_row, conv_values, conv_gates, depth_kernel, batch_gain, batch_bias, conv_outs):
    normed = low(layer_norm(stream, gain, beta_row))
    value_half = low_back(jnp.einsum('bld,dc->blc', normed, conv_values, precision=HIGHEST))
    gate_half = low_back(jnp.einsum('bld,dc->blc', normed, conv_gates, precision=HIGHEST))
    gated = pad_mask * value_half * jax.nn.sigmoid(gate_half)
    margin = (KER - 1) // 2
    padded = jnp.pad(gated, ((0, 0), (margin, margin), (0, 0)))
    depth_out = jnp.zeros_like(gated)
    for offset in range(KER):
        depth_out = depth_out + depth_kernel[offset] * padded[:, offset:offset + SEQ_LEN]
    tokens_valid = jnp.sum(pad_mask)
    mean_depth = lax.optimization_barrier(jnp.sum(pad_mask * depth_out, (0, 1))) / tokens_valid
    var_depth = lax.optimization_barrier(jnp.sum(pad_mask * depth_out * depth_out, (0, 1))) / tokens_valid - mean_depth * mean_depth
    normal_out = (depth_out - mean_depth) * lax.rsqrt(var_depth + EPS) * batch_gain + batch_bias
    activated = low(jax.nn.silu(normal_out))
    return low_back(jnp.einsum('blc,cd->bld', activated, conv_outs, precision=HIGHEST))

def reference(inputs, lengths, rel_embed, out_grad, norm_gain, norm_bias, ffn1_in, ffn1_out, query_w, key_w, value_w, pos_w, attn_out, pos_bias, conv_value, conv_gate, depthwise, bn_gain, bn_bias, conv_out, ffn2_in, ffn2_out):
    rel_table = rel_embed.astype(jnp.float32)
    pad_mask = (jnp.arange(SEQ_LEN)[None, :] < lengths[:, None]).astype(jnp.float32)[:, :, None]

    def forward(params):
        stream, gain_rows, beta_rows, first_in, first_out, query_mat, key_mat, value_mat, pos_mat, attn_mat, pair_bias, conv_values, conv_gates, depth_kernel, batch_gain, batch_bias, conv_outs, second_in, second_out = params
        stream = stream + 0.5 * feed_forward(stream, gain_rows[0], beta_rows[0], first_in, first_out)
        stream = stream + attention(stream, lengths, gain_rows[1], beta_rows[1], query_mat, key_mat, value_mat, pos_mat, attn_mat, pair_bias, rel_table)
        stream = stream + convolution(stream, pad_mask, gain_rows[2], beta_rows[2], conv_values, conv_gates, depth_kernel, batch_gain, batch_bias, conv_outs)
        stream = stream + 0.5 * feed_forward(stream, gain_rows[3], beta_rows[3], second_in, second_out)
        return layer_norm(stream, gain_rows[4], beta_rows[4])
    params = tuple((member.astype(jnp.float32) for member in (inputs, norm_gain, norm_bias, ffn1_in, ffn1_out, query_w, key_w, value_w, pos_w, attn_out, pos_bias, conv_value, conv_gate, depthwise, bn_gain, bn_bias, conv_out, ffn2_in, ffn2_out)))
    block_out, pullback = jax.vjp(forward, params)
    gradients = pullback(out_grad.astype(jnp.float32))[0]
    return (block_out.astype(jnp.bfloat16), gradients[0], gradients[1], gradients[2], gradients[3], gradients[4], gradients[5], gradients[6], gradients[7], gradients[8], gradients[9], gradients[10], gradients[11], gradients[12], gradients[13], gradients[14], gradients[15], gradients[16], gradients[17], gradients[18])
```

```python
import jax
import jax.numpy as jnp
from jax import lax
from jax.experimental import pallas as pl
from jax.experimental.pallas import tpu as pltpu
from jax.sharding import PartitionSpec as P

DH = 64
LANES = 128
HALO = 16
EPS = 1e-05
NEG = -1000000000.0
HIGHEST = lax.Precision.HIGHEST
BF = jnp.bfloat16
F32 = jnp.float32
VMEM_LIMIT = 56 * 1024 * 1024


def dot(left, right, dims=((1,), (0,)), **kw):
    return lax.dot_general(left, right, (dims, ((), ())), preferred_element_type=F32, **kw)


def swap(values, axis, mask):
    return lax.ppermute(values, axis, [(i, i ^ mask) for i in range(lax.axis_size(axis))])


def dp_plan():
    size = lax.axis_size("dp")
    chips = [m for m in (0, 2, 4, 6) if m < size]
    doublings = [1] + [1 << b for b in range(3, 20) if 1 << b < size]
    masks = list(chips)
    for step in doublings:
        masks = masks + [m ^ step for m in masks]
    return chips, doublings, masks


def cut(values, widths):
    parts, at = [], 0
    for width in widths:
        parts.append(values[:, at : at + width])
        at += width
    return parts


def gather_tensor(parts):
    packed = jnp.concatenate(parts, 1) if len(parts) > 1 else parts[0]
    widths = [p.shape[1] for p in parts]
    blocks = [cut(packed, widths)]
    for mask in range(1, lax.axis_size("tensor")):
        blocks.append(cut(swap(packed, "tensor", mask), widths))
    return [jnp.concatenate([b[i] for b in blocks], 1) for i in range(len(parts))]


def gather_dp(block):
    chips, doublings, _ = dp_plan()
    rows = jnp.concatenate([block] + [swap(block, "dp", m) for m in chips[1:]], 0)
    for step in doublings:
        rows = jnp.concatenate([rows, swap(rows, "dp", step)], 0)
    return rows


def scatter_dp(partial):
    chips, doublings, _ = dp_plan()
    for step in doublings[::-1]:
        half = partial.shape[0] // 2
        other = swap(partial[half:], "dp", step)
        partial = (partial[:half].astype(F32) + other.astype(F32)).astype(BF)
    count = partial.shape[0] // len(chips)
    total = partial[:count].astype(F32)
    for i, mask in enumerate(chips[1:], 1):
        total = total + swap(partial[i * count : (i + 1) * count], "dp", mask).astype(F32)
    return total


def scatter_tensor(total, widths, shared=0):
    size = lax.axis_size("tensor")
    low = total.astype(BF)
    own, blocks, at = [], [[] for _ in range(size)], 0
    for width in widths:
        for mask in range(size):
            blocks[mask].append(slice(at + mask * width, at + (mask + 1) * width))
        at += size * width
    if shared:
        for mask in range(size):
            blocks[mask].append(slice(at, at + shared))
    result = jnp.concatenate([total[:, s] for s in blocks[0]], 1)
    for mask in range(1, size):
        packed = jnp.concatenate([low[:, s] for s in blocks[mask]], 1)
        result = result + swap(packed, "tensor", mask).astype(F32)
    return cut(result, list(widths) + ([shared] if shared else []))


def block_swap(values, mask):
    size = lax.axis_size("tensor")
    width = values.shape[1] // size
    return jnp.concatenate(
        [values[:, (b ^ mask) * width : ((b ^ mask) + 1) * width] for b in range(size)], 1
    )


def sum_all(rows):
    chips, doublings, _ = dp_plan()
    total = rows
    for step in doublings:
        total = total + swap(total, "dp", step)
    total = total + sum(swap(total, "dp", m) for m in chips[1:])
    return total + sum(
        block_swap(swap(total, "tensor", m), m) for m in range(1, lax.axis_size("tensor"))
    )


def edge_rows(values, swap_blocks):
    size = lax.axis_size("tensor")
    me = lax.axis_index("tensor")
    before = lax.ppermute(values[-HALO:], "tensor", [(i, i + 1) for i in range(size - 1)])
    after = lax.ppermute(values[:HALO], "tensor", [(i + 1, i) for i in range(size - 1)])
    if swap_blocks:
        def reorder(rows, mask_of):
            options = sorted({m ^ (m - 1) for m in range(1, size)})
            out = rows
            for mask in options:
                out = jnp.where(mask_of == mask, block_swap(rows, mask), out)
            return out

        before = reorder(before, me ^ (me - 1))
        after = reorder(after, me ^ (me + 1))
    return before, after


def norm_forward(stream, gain, beta_row):
    centered = stream - jnp.mean(stream, -1, keepdims=True)
    inv_std = lax.rsqrt(jnp.mean(centered * centered, -1, keepdims=True) + EPS)
    scaled = centered * inv_std
    return (scaled * gain + beta_row, (scaled, inv_std))


def norm_backward(upstream, kept_state, gain):
    scaled, inv_std = kept_state
    scaled_grad = upstream * gain
    stream_grad = inv_std * (
        scaled_grad
        - jnp.mean(scaled_grad, -1, keepdims=True)
        - scaled * jnp.mean(scaled_grad * scaled, -1, keepdims=True)
    )
    return (stream_grad, jnp.sum(upstream * scaled, 0), jnp.sum(upstream, 0))


def swish_slope(inner_act):
    logistic = jax.nn.sigmoid(inner_act)
    return logistic * (1.0 + inner_act * (1.0 - logistic))


def ffn_forward(normed, proj_in, proj_out_t):
    inner_act = dot(normed, proj_in)
    hidden = jax.nn.silu(inner_act).astype(BF)
    return dot(hidden, proj_out_t, ((1,), (1,))), (normed, inner_act, hidden)


def ffn_backward(upstream, kept_state, proj_in, proj_out_t):
    normed, inner_act, hidden = kept_state
    grad_rows = upstream.astype(BF)
    out_grad = dot(grad_rows, hidden, ((0,), (0,))).astype(BF)
    inner_grad = (dot(grad_rows, proj_out_t) * swish_slope(inner_act)).astype(BF)
    in_grad = dot(normed, inner_grad, ((0,), (0,))).astype(BF)
    return dot(inner_grad, proj_in, ((1,), (1,))), in_grad, out_grad


def head_lanes(rows):
    return lax.broadcasted_iota(jnp.int32, (rows, LANES), 1)


def attn_forward_kernel(
    place_ref, rows_ref, wq_ref, wk_ref, wv_ref, wp_ref, rel_ref, bias_ref,
    mixed_ref, probs_ref, keys_ref, vals_ref, qu_ref, qv_ref, pos_ref,
):
    me, length = place_ref[0], place_ref[1]
    blocks, rows = rows_ref.shape[0], rows_ref.shape[1]
    span = blocks * rows
    wide = rel_ref.shape[0]
    for b in range(blocks):
        at = pl.ds(pl.multiple_of((me ^ b) * rows, 64), rows)
        keys_ref[at, :] = dot(rows_ref[b], wk_ref[...]).astype(BF)
        vals_ref[at, :] = dot(rows_ref[b], wv_ref[...]).astype(BF)
    queries = dot(rows_ref[0], wq_ref[...])
    query_u = (queries + bias_ref[0:1, :]).astype(BF)
    query_v = (queries + bias_ref[1:2, :]).astype(BF)
    qu_ref[...] = query_u
    qv_ref[...] = query_v
    positions = dot(rel_ref[...], wp_ref[...]).astype(BF)
    pos_ref[...] = positions
    keys, vals = keys_ref[...], vals_ref[...]
    lane = head_lanes(rows)
    visible = lax.broadcasted_iota(jnp.int32, (rows, span), 1) < length
    mixed = jnp.zeros((rows, LANES), F32)
    for h in range(LANES // DH):
        mine = (lane >= h * DH) & (lane < (h + 1) * DH)
        zero = jnp.zeros_like(query_u)
        content = dot(jnp.where(mine, query_u, zero), keys, ((1,), (1,)))
        table = dot(jnp.where(mine, query_v, zero), positions, ((1,), (1,)))
        shifted = pltpu.roll(table, wide - (rows - 1), 1, stride=1, stride_axis=0)
        scores = jnp.where(visible, (content + shifted[:, :span]) * DH ** (-0.5), NEG)
        exponent = jnp.exp(scores - jnp.max(scores, -1, keepdims=True))
        probs = exponent / jnp.sum(exponent, -1, keepdims=True)
        probs_ref[h] = probs
        mixed = jnp.where(mine, dot(probs.astype(BF), vals), mixed)
    mixed_ref[...] = mixed.astype(BF)


def attn_forward(place, rows_stack, weights, rel_rows, pair_bias):
    blocks, rows, width = rows_stack.shape
    span, wide = blocks * rows, rel_rows.shape[0]
    groups = pair_bias.shape[1] // LANES
    pairs = LANES // DH

    def weight(i):
        return pl.BlockSpec((width, LANES), lambda g, i=i: (0, i * groups + g))

    def column(n):
        return pl.BlockSpec((n, LANES), lambda g: (0, g))

    def whole(*shape):
        return pl.BlockSpec(shape, lambda g: (0,) * len(shape))

    columns = groups * LANES
    return pl.pallas_call(
        attn_forward_kernel,
        grid=(groups,),
        in_specs=[
            pl.BlockSpec(memory_space=pltpu.SMEM),
            whole(blocks, rows, width),
            weight(0),
            weight(1),
            weight(2),
            weight(3),
            whole(wide, width),
            column(pair_bias.shape[0]),
        ],
        out_specs=[
            column(rows),
            pl.BlockSpec((pairs, rows, span), lambda g: (g, 0, 0)),
            column(span),
            column(span),
            column(rows),
            column(rows),
            column(wide),
        ],
        out_shape=[
            jax.ShapeDtypeStruct((rows, columns), BF),
            jax.ShapeDtypeStruct((groups * pairs, rows, span), F32),
            jax.ShapeDtypeStruct((span, columns), BF),
            jax.ShapeDtypeStruct((span, columns), BF),
            jax.ShapeDtypeStruct((rows, columns), BF),
            jax.ShapeDtypeStruct((rows, columns), BF),
            jax.ShapeDtypeStruct((wide, columns), BF),
        ],
        compiler_params=pltpu.CompilerParams(vmem_limit_bytes=VMEM_LIMIT),
        name="attn_forward",
    )(place, rows_stack, weights, weights, weights, weights, rel_rows, pair_bias)


def attn_backward_kernel(
    place_ref, rows_ref, wq_ref, wk_ref, wv_ref, wo_ref, rel_ref, gb_ref,
    mixed_ref, probs_ref, keys_ref, vals_ref, qu_ref, qv_ref, pos_ref,
    dq_ref, dk_ref, dv_ref, dp_ref, do_ref, bias_ref, own_ref, others_ref,
    ordered, ordered_t, rel_t, gb_t, total,
):
    me = place_ref[0]
    blocks, rows = rows_ref.shape[0], rows_ref.shape[1]
    span = blocks * rows
    wide = rel_ref.shape[0]
    step = pl.program_id(0)

    @pl.when(step == 0)
    def _():
        for b in range(blocks):
            at = pl.ds(pl.multiple_of((me ^ b) * rows, 64), rows)
            ordered[at, :] = rows_ref[b]
        ordered_t[...] = ordered[...].T
        rel_t[...] = rel_ref[...].T
        gb_t[...] = gb_ref[...].T
        total[...] = jnp.zeros_like(total)
        own_ref[...] = jnp.zeros_like(own_ref)

    lane = head_lanes(rows)
    i = lax.broadcasted_iota(jnp.int32, (rows, rows), 0)
    j = lax.broadcasted_iota(jnp.int32, (rows, rows), 1)
    flip = jnp.where(i + j == rows - 1, 1.0, 0.0)
    flip_low = flip.astype(BF)
    keys, vals, positions = keys_ref[...], vals_ref[...], pos_ref[...]
    gm = dot(gb_ref[...], wo_ref[...]).astype(BF)
    gm_t = gm.T
    qu_t = qu_ref[...].T
    qv_t = dot(flip_low, qv_ref[...]).astype(BF).T
    du = jnp.zeros((rows, LANES), F32)
    dv_rows = jnp.zeros((rows, LANES), F32)
    dk_t, dv_t, dp_t = [], [], []
    for h in range(LANES // DH):
        mine = (lane >= h * DH) & (lane < (h + 1) * DH)
        head = slice(h * DH, (h + 1) * DH)
        probs = probs_ref[h]
        dprobs = dot(jnp.where(mine, gm, jnp.zeros_like(gm)), vals, ((1,), (1,)))
        delta = jnp.sum(dprobs * probs, -1, keepdims=True)
        gp = ((DH ** (-0.5) * probs) * (dprobs - delta)).astype(BF)
        dv_t.append(dot(gm_t[head], probs.astype(BF)))
        dk_t.append(dot(qu_t[head], gp))
        du = jnp.where(mine, dot(gp, keys), du)
        flipped = dot(flip_low, gp)
        table = jnp.concatenate([flipped, jnp.zeros((rows, wide - span), F32)], 1)
        table = pltpu.roll(table, 0, 1, stride=1, stride_axis=0).astype(BF)
        dp_t.append(dot(qv_t[head], table))
        dv_rows = jnp.where(mine, dot(table, positions), dv_rows)
    dv_rows = dot(flip, dv_rows, precision=HIGHEST)
    bias_ref[...] = jnp.concatenate(
        [
            jnp.sum(du, 0, keepdims=True),
            jnp.sum(dv_rows, 0, keepdims=True),
            jnp.zeros((6, LANES), F32),
        ],
        0,
    )
    dq = (du + dv_rows).astype(BF)
    dk = jnp.concatenate(dk_t, 0).T.astype(BF)
    dv = jnp.concatenate(dv_t, 0).T.astype(BF)
    dp = jnp.concatenate(dp_t, 0).T.astype(BF)
    total[...] += dot(dk, wk_ref[...], ((1,), (1,))) + dot(dv, wv_ref[...], ((1,), (1,)))
    own_ref[...] += dot(dq, wq_ref[...], ((1,), (1,)))
    dq_ref[...] = dot(rows_ref[0].T, dq).astype(BF)
    dk_ref[...] = dot(ordered_t[...], dk).astype(BF)
    dv_ref[...] = dot(ordered_t[...], dv).astype(BF)
    dp_ref[...] = dot(rel_t[...], dp).astype(BF)
    do_ref[...] = dot(gb_t[...], mixed_ref[...]).astype(BF)

    @pl.when(step == pl.num_programs(0) - 1)
    def _():
        at = pl.ds(pl.multiple_of(me * rows, 64), rows)
        own_ref[...] += total[at, :]
        for b in range(1, blocks):
            at = pl.ds(pl.multiple_of((me ^ b) * rows, 64), rows)
            others_ref[b - 1] = total[at, :].astype(BF)


def attn_backward(place, rows_stack, weights, rel_rows, gb, kept):
    blocks, rows, width = rows_stack.shape
    span, wide = blocks * rows, rel_rows.shape[0]
    mixed = kept[0]
    columns = mixed.shape[1]
    groups = columns // LANES
    pairs = LANES // DH

    def weight(i):
        return pl.BlockSpec((width, LANES), lambda g, i=i: (0, i * groups + g))

    def column(n):
        return pl.BlockSpec((n, LANES), lambda g: (0, g))

    def whole(*shape):
        return pl.BlockSpec(shape, lambda g: (0,) * len(shape))

    return pl.pallas_call(
        attn_backward_kernel,
        grid=(groups,),
        in_specs=[
            pl.BlockSpec(memory_space=pltpu.SMEM),
            whole(blocks, rows, width),
            weight(0),
            weight(1),
            weight(2),
            weight(4),
            whole(wide, width),
            whole(rows, width),
            column(rows),
            pl.BlockSpec((pairs, rows, span), lambda g: (g, 0, 0)),
            column(span),
            column(span),
            column(rows),
            column(rows),
            column(wide),
        ],
        out_specs=[column(width)] * 5
        + [column(8), whole(rows, width), whole(blocks - 1, rows, width)],
        out_shape=[jax.ShapeDtypeStruct((width, columns), BF)] * 5
        + [
            jax.ShapeDtypeStruct((8, columns), F32),
            jax.ShapeDtypeStruct((rows, width), F32),
            jax.ShapeDtypeStruct((blocks - 1, rows, width), BF),
        ],
        scratch_shapes=[
            pltpu.VMEM((span, width), BF),
            pltpu.VMEM((width, span), BF),
            pltpu.VMEM((width, wide), BF),
            pltpu.VMEM((width, rows), BF),
            pltpu.VMEM((span, width), F32),
        ],
        compiler_params=pltpu.CompilerParams(vmem_limit_bytes=VMEM_LIMIT),
        name="attn_backward",
    )(place, rows_stack, weights, weights, weights, weights, rel_rows, gb, *kept)


def conv_forward_kernel(
    place_ref, rows_ref, wv_ref, wg_ref, taps_ref, gated_ref, value_ref, gate_ref, depth_ref, sums_ref
):
    start, length = place_ref[2], place_ref[1]
    rows = depth_ref.shape[0]
    value_half = dot(rows_ref[...], wv_ref[...])
    logistic = jax.nn.sigmoid(dot(rows_ref[...], wg_ref[...]))
    token = start - HALO + lax.broadcasted_iota(jnp.int32, value_half.shape, 0)
    mask = jnp.where((token >= 0) & (token < length), 1.0, 0.0)
    gated_ref[...] = mask * value_half * logistic
    value_ref[...] = value_half[HALO : HALO + rows]
    gate_ref[...] = logistic[HALO : HALO + rows]
    taps = taps_ref[...]
    ker = 2 * (HALO - 1) + 1
    depth = jnp.zeros((rows, LANES), F32)
    for k in range(ker):
        depth = depth + taps[k : k + 1, :] * gated_ref[k + 1 : k + 1 + rows, :]
    depth_ref[...] = depth
    masked = depth * mask[HALO : HALO + rows]
    sums_ref[...] = jnp.concatenate(
        [
            jnp.sum(masked, 0, keepdims=True),
            jnp.sum(masked * depth, 0, keepdims=True),
            jnp.sum(mask[HALO : HALO + rows], 0, keepdims=True),
            jnp.zeros((5, LANES), F32),
        ],
        0,
    )


def conv_backward_kernel(place_ref, grad_ref, gated_ref, value_ref, gate_ref, taps_ref, dv_ref, dg_ref, dtaps_ref):
    start, length = place_ref[2], place_ref[1]
    rows = value_ref.shape[0]
    taps = taps_ref[...]
    ker = 2 * (HALO - 1) + 1
    own = grad_ref[HALO : HALO + rows, :]
    total = jnp.zeros((rows, LANES), F32)
    for k in range(ker):
        total = total + taps[k : k + 1, :] * grad_ref[ker - k : ker - k + rows, :]
        dtaps_ref[k : k + 1, :] = jnp.sum(
            own * gated_ref[k + 1 : k + 1 + rows, :], 0, keepdims=True
        )
    dtaps_ref[ker:, :] = jnp.zeros_like(dtaps_ref[ker:, :])
    token = start + lax.broadcasted_iota(jnp.int32, total.shape, 0)
    total = jnp.where(token < length, total, 0.0)
    value_half, logistic = value_ref[...], gate_ref[...]
    dv_ref[...] = (total * logistic).astype(BF)
    dg_ref[...] = (total * value_half * logistic * (1.0 - logistic)).astype(BF)


def conv_forward(place, rows_ext, weights, taps):
    ext, width = rows_ext.shape
    rows = ext - 2 * HALO
    columns = taps.shape[1]
    groups = columns // LANES

    def column(n):
        return pl.BlockSpec((n, LANES), lambda g: (0, g))

    def weight(i):
        return pl.BlockSpec((width, LANES), lambda g, i=i: (0, i * groups + g))

    return pl.pallas_call(
        conv_forward_kernel,
        grid=(groups,),
        in_specs=[
            pl.BlockSpec(memory_space=pltpu.SMEM),
            pl.BlockSpec((ext, width), lambda g: (0, 0)),
            weight(0),
            weight(1),
            column(taps.shape[0]),
        ],
        out_specs=[column(ext), column(rows), column(rows), column(rows), column(8)],
        out_shape=[
            jax.ShapeDtypeStruct((ext, columns), F32),
            jax.ShapeDtypeStruct((rows, columns), F32),
            jax.ShapeDtypeStruct((rows, columns), F32),
            jax.ShapeDtypeStruct((rows, columns), F32),
            jax.ShapeDtypeStruct((8, columns), F32),
        ],
        compiler_params=pltpu.CompilerParams(vmem_limit_bytes=VMEM_LIMIT),
        name="conv_forward",
    )(place, rows_ext, weights, weights, taps)


def conv_backward(place, grad_ext, gated, value_half, logistic, taps):
    ext, columns = grad_ext.shape
    rows = ext - 2 * HALO
    groups = columns // LANES

    def column(n):
        return pl.BlockSpec((n, LANES), lambda g: (0, g))

    return pl.pallas_call(
        conv_backward_kernel,
        grid=(groups,),
        in_specs=[
            pl.BlockSpec(memory_space=pltpu.SMEM),
            column(ext),
            column(ext),
            column(rows),
            column(rows),
            column(taps.shape[0]),
        ],
        out_specs=[column(rows), column(rows), column(taps.shape[0])],
        out_shape=[
            jax.ShapeDtypeStruct((rows, columns), BF),
            jax.ShapeDtypeStruct((rows, columns), BF),
            jax.ShapeDtypeStruct((taps.shape[0], columns), F32),
        ],
        compiler_params=pltpu.CompilerParams(vmem_limit_bytes=VMEM_LIMIT),
        name="conv_backward",
    )(place, grad_ext, gated, value_half, logistic, taps)


def on_device(
    inputs,
    lengths,
    rel_embed,
    out_grad,
    norm_gain,
    norm_bias,
    ffn1_in,
    ffn1_out,
    query_w,
    key_w,
    value_w,
    pos_w,
    attn_out,
    pos_bias,
    conv_value,
    conv_gate,
    depthwise,
    bn_gain,
    bn_bias,
    conv_out,
    ffn2_in,
    ffn2_out,
):
    size_t = lax.axis_size("tensor")
    me_t = lax.axis_index("tensor")
    me_dp = lax.axis_index("dp")
    _, _, masks = dp_plan()
    rows, width = inputs.shape[1], inputs.shape[2]
    shard = width // lax.axis_size("dp")
    channels = size_t * query_w.shape[1]

    norm_cols = jnp.concatenate([norm_gain, norm_bias], 0).T
    norm_cols = jnp.pad(norm_cols, ((0, 0), (0, LANES - norm_cols.shape[1])))
    first = gather_tensor([ffn1_in, ffn1_out.T])
    first = gather_dp(jnp.concatenate(first + [norm_cols], 1))
    small = jnp.concatenate([depthwise, pos_bias, bn_gain[None], bn_bias[None]], 0)
    small = jnp.pad(small, ((0, -small.shape[0] % 16), (0, 0)))
    (small,) = gather_tensor([small])
    ker = depthwise.shape[0]
    attn_w = gather_dp(
        jnp.concatenate(gather_tensor([query_w, key_w, value_w, pos_w, attn_out.T]), 1)
    )
    conv_w = gather_dp(jnp.concatenate(gather_tensor([conv_value, conv_gate, conv_out.T]), 1))
    second = gather_dp(jnp.concatenate(gather_tensor([ffn2_in, ffn2_out.T]), 1))
    hidden_units = size_t * ffn1_in.shape[1]
    first_in, first_out = first[:, :hidden_units], first[:, hidden_units : 2 * hidden_units]
    second_in, second_out = second[:, :hidden_units], second[:, hidden_units:]
    conv_out_w = conv_w[:, 2 * channels :]
    norm_rows = first[:, 2 * hidden_units :].T.astype(F32)
    gains, betas = norm_rows[0:5], norm_rows[5:10]
    taps = jnp.pad(small[:ker].astype(F32), ((0, 32 - ker), (0, 0)))
    pair_bias = small[ker : ker + 2].astype(F32)
    batch_gain = small[ker + 2].astype(F32)
    batch_bias = small[ker + 3].astype(F32)

    feature = jnp.arange(width)
    mask_of = jnp.asarray(masks, jnp.int32)[feature // shard]
    source = (mask_of ^ me_dp) * shard + feature % shard
    order = (jnp.arange(width)[:, None] == source[None, :]).astype(BF)
    stream = dot(inputs[0], order)
    cotangent = dot(out_grad[0], order)
    span = rows * size_t
    wide = -(-(span + rows) // LANES) * LANES
    rel_rows = jnp.pad(rel_embed, ((0, span + wide - rel_embed.shape[0]), (0, 0)))
    rel_rows = lax.dynamic_slice_in_dim(rel_rows, rows * (size_t - 1 - me_t), wide, 0)
    rel_rows = dot(rel_rows, order).astype(BF)
    place = jnp.stack([me_t, lengths[0], me_t * rows]).astype(jnp.int32)
    pad_mask = (me_t * rows + jnp.arange(rows) < lengths[0]).astype(F32)[:, None]

    normed, norm_one = norm_forward(stream, gains[0], betas[0])
    branch, ffn_first = ffn_forward(normed.astype(BF), first_in, first_out)
    stream = stream + 0.5 * branch

    normed, norm_two = norm_forward(stream, gains[1], betas[1])
    normed = normed.astype(BF)
    rows_stack = jnp.stack([normed] + [swap(normed, "tensor", m) for m in range(1, size_t)])
    kept = attn_forward(place, rows_stack, attn_w, rel_rows, pair_bias)
    attn_out_w = attn_w[:, 4 * channels :]
    stream = stream + dot(kept[0], attn_out_w, ((1,), (1,)))

    normed, norm_three = norm_forward(stream, gains[2], betas[2])
    normed_three = normed.astype(BF)
    before, after = edge_rows(normed_three, False)
    rows_ext = jnp.concatenate([before, normed_three, after], 0)
    gated, value_half, logistic, depth, sums = conv_forward(place, rows_ext, conv_w, taps)
    sums = sum_all(sums)
    tokens_valid = sums[2]
    mean_depth = sums[0] / tokens_valid
    inv_std = lax.rsqrt(sums[1] / tokens_valid - mean_depth * mean_depth + EPS)
    scaled = (depth - mean_depth) * inv_std
    normal_out = scaled * batch_gain + batch_bias
    activated = jax.nn.silu(normal_out).astype(BF)
    stream = stream + dot(activated, conv_out_w, ((1,), (1,)))

    normed, norm_four = norm_forward(stream, gains[3], betas[3])
    branch, ffn_second = ffn_forward(normed.astype(BF), second_in, second_out)
    stream = stream + 0.5 * branch
    block_out, norm_five = norm_forward(stream, gains[4], betas[4])

    stream_grad, gain_five, beta_five = norm_backward(cotangent, norm_five, gains[4])
    normed_grad, second_in_grad, second_out_grad = ffn_backward(
        0.5 * stream_grad, ffn_second, second_in, second_out
    )
    second_sum = scatter_dp(jnp.concatenate([second_in_grad, second_out_grad], 1))
    second_in_grad, second_out_grad = scatter_tensor(second_sum, [ffn2_in.shape[1]] * 2)
    extra_grad, gain_four, beta_four = norm_backward(normed_grad, norm_four, gains[3])
    stream_grad = stream_grad + extra_grad

    gb = stream_grad.astype(BF)
    outs_grad = dot(gb, activated, ((0,), (0,)))
    normal_grad = dot(gb, conv_out_w) * swish_slope(normal_out)
    totals = jnp.stack([jnp.sum(normal_grad, 0), jnp.sum(normal_grad * scaled, 0)])
    totals = sum_all(jnp.pad(totals, ((0, 6), (0, 0))))
    sum_gain = batch_gain * totals[0]
    sum_cross = batch_gain * totals[1]
    square_grad = -0.5 * inv_std * inv_std * sum_cross / tokens_valid
    first_grad = (inv_std * inv_std * mean_depth * sum_cross - inv_std * sum_gain) / tokens_valid
    depth_grad = inv_std * batch_gain * normal_grad + pad_mask * (
        first_grad + 2.0 * depth * square_grad
    )
    before, after = edge_rows(depth_grad, True)
    grad_ext = jnp.concatenate([before, depth_grad, after], 0)
    value_grad, gate_grad, taps_grad = conv_backward(
        place, grad_ext, gated, value_half, logistic, taps
    )
    conv_grads = jnp.concatenate(
        [
            dot(normed_three, value_grad, ((0,), (0,))),
            dot(normed_three, gate_grad, ((0,), (0,))),
            outs_grad,
        ],
        1,
    ).astype(BF)
    normed_grad = dot(value_grad, conv_w[:, :channels], ((1,), (1,))) + dot(
        gate_grad, conv_w[:, channels : 2 * channels], ((1,), (1,))
    )
    extra_grad, gain_three, beta_three = norm_backward(normed_grad, norm_three, gains[2])
    stream_grad = stream_grad + extra_grad

    gb = stream_grad.astype(BF)
    dq, dk, dv, dp, do, bias_grad, own_grad, others = attn_backward(
        place, rows_stack, attn_w, rel_rows, gb, kept
    )
    normed_grad = own_grad
    for m in range(1, size_t):
        normed_grad = normed_grad + swap(others[m - 1], "tensor", m).astype(F32)
    part = query_w.shape[1]
    middle_sum = scatter_dp(jnp.concatenate([dq, dk, dv, dp, do, conv_grads], 1))
    query_grad, key_grad, value_grad, pos_grad, attn_grad, values_grad, gates_grad, outs_grad = (
        scatter_tensor(middle_sum, [part] * 8)
    )
    extra_grad, gain_two, beta_two = norm_backward(normed_grad, norm_two, gains[1])
    stream_grad = stream_grad + extra_grad

    normed_grad, first_in_grad, first_out_grad = ffn_backward(
        0.5 * stream_grad, ffn_first, first_in, first_out
    )
    extra_grad, gain_one, beta_one = norm_backward(normed_grad, norm_one, gains[0])
    stream_grad = stream_grad + extra_grad
    norm_grads = jnp.stack(
        [gain_one, gain_two, gain_three, gain_four, gain_five]
        + [beta_one, beta_two, beta_three, beta_four, beta_five]
    )
    norm_grads = jnp.pad(norm_grads, ((0, LANES - 10), (0, 0))).T.astype(BF)
    first_sum = scatter_dp(jnp.concatenate([first_in_grad, first_out_grad, norm_grads], 1))
    first_in_grad, first_out_grad, norm_cols = scatter_tensor(
        first_sum, [ffn1_in.shape[1]] * 2, LANES
    )
    norm_rows = norm_cols.T

    channel_rows = jnp.concatenate([taps_grad, bias_grad], 0)
    block = channels // size_t
    own_rows = channel_rows[:, :block]
    for m in range(1, size_t):
        own_rows = own_rows + swap(channel_rows[:, m * block : (m + 1) * block], "tensor", m)
    chips, doublings, _ = dp_plan()
    for step in doublings:
        own_rows = own_rows + swap(own_rows, "dp", step)
    own_rows = own_rows + sum(swap(own_rows, "dp", m) for m in chips[1:])

    block_out = dot(block_out.astype(BF), order, ((1,), (1,))).astype(BF)
    stream_grad = dot(stream_grad, order.astype(F32), ((1,), (1,)), precision=HIGHEST)
    return (
        block_out[None],
        stream_grad[None],
        norm_rows[0:5],
        norm_rows[5:10],
        first_in_grad,
        first_out_grad.T,
        query_grad,
        key_grad,
        value_grad,
        pos_grad,
        attn_grad.T,
        own_rows[32:34],
        values_grad,
        gates_grad,
        own_rows[:ker],
        totals[1, :block],
        totals[0, :block],
        outs_grad.T,
        second_in_grad,
        second_out_grad.T,
    )


def solution(mesh):
    return jax.shard_map(
        on_device,
        mesh=mesh,
        in_specs=(
            P("dp", "tensor", None),
            P("dp"),
            P(),
            P("dp", "tensor", None),
            P(None, "dp"),
            P(None, "dp"),
            P("dp", "tensor"),
            P("tensor", "dp"),
            P("dp", "tensor"),
            P("dp", "tensor"),
            P("dp", "tensor"),
            P("dp", "tensor"),
            P("tensor", "dp"),
            P(None, "tensor"),
            P("dp", "tensor"),
            P("dp", "tensor"),
            P(None, "tensor"),
            P("tensor"),
            P("tensor"),
            P("tensor", "dp"),
            P("dp", "tensor"),
            P("tensor", "dp"),
        ),
        out_specs=(
            P("dp", "tensor", None),
            P("dp", "tensor", None),
            P(None, "dp"),
            P(None, "dp"),
            P("dp", "tensor"),
            P("tensor", "dp"),
            P("dp", "tensor"),
            P("dp", "tensor"),
            P("dp", "tensor"),
            P("dp", "tensor"),
            P("tensor", "dp"),
            P(None, "tensor"),
            P("dp", "tensor"),
            P("dp", "tensor"),
            P(None, "tensor"),
            P("tensor"),
            P("tensor"),
            P("tensor", "dp"),
            P("dp", "tensor"),
            P("tensor", "dp"),
        ),
        check_vma=False,
    )
```

```python
import jax
import jax.numpy as jnp
from jax import lax
from jax.experimental import pallas as pl
from jax.experimental.pallas import tpu as pltpu
from jax.sharding import PartitionSpec as P

DH = 64
LANES = 128
HALO = 16
EPS = 1e-05
NEG = -1000000000.0
HIGHEST = lax.Precision.HIGHEST
BF = jnp.bfloat16
F32 = jnp.float32


def dot(left, right, dims=((1,), (0,)), **kw):
    return lax.dot_general(left, right, (dims, ((), ())), preferred_element_type=F32, **kw)


def dot_t(left, right):
    return dot(left, right, ((1,), (1,)))


def swap(values, axis, mask):
    return lax.ppermute(values, axis, [(i, i ^ mask) for i in range(lax.axis_size(axis))])


def dp_plan():
    size = lax.axis_size("dp")
    chips = [m for m in (0, 2, 4, 6) if m < size]
    doublings = [1] + [1 << b for b in range(3, 20) if 1 << b < size]
    return chips, doublings


def run(kernel, ins, outs, scratch=(), grid=(1,), aliases=None, after=(), micros=3, limit=24, name=None):
    count = len(ins)

    def body(*refs):
        kernel(*refs[:count], *refs[count + len(after) :])

    def whole(shape):
        return pl.BlockSpec(
            tuple(shape), lambda g: (0,) * len(shape), pipeline_mode=pl.Buffered(1)
        )

    return pl.pallas_call(
        body,
        grid=grid,
        in_specs=[spec or whole(a.shape) for a, spec in ins] + [ANY] * len(after),
        out_specs=[spec or whole(s) for s, _, spec in outs],
        out_shape=[jax.ShapeDtypeStruct(s, d) for s, d, _ in outs],
        scratch_shapes=list(scratch),
        input_output_aliases=aliases or {},
        compiler_params=pltpu.CompilerParams(vmem_limit_bytes=limit * 1024 * 1024),
        cost_estimate=pl.CostEstimate(
            flops=int(micros * 1e9), bytes_accessed=int(micros * 3.0e6), transcendentals=0
        ),
        name=name,
    )(*[a for a, _ in ins], *after)


SMEM = pl.BlockSpec(memory_space=pltpu.SMEM)
ANY = pl.BlockSpec(memory_space=pl.ANY)


def column(rows, offset=0):
    return pl.BlockSpec((rows, LANES), lambda g: (0, offset + g))


def heads(pairs, rows, span):
    return pl.BlockSpec((pairs, rows, span), lambda g: (g, 0, 0))


def regroup(blocks, widths, extras=(), after=(), name="regroup"):
    rows = blocks[0].shape[0]
    count, total = len(blocks), sum(widths)

    def kernel(*refs):
        out, at, start = refs[-1], 0, 0
        for width in widths:
            for b in range(count):
                out[:, at : at + width] = refs[b][:, start : start + width]
                at += width
            start += width
        for ref in refs[count:-1]:
            out[:, at : at + ref.shape[1]] = ref[...]
            at += ref.shape[1]

    columns = count * total + sum(e.shape[1] for e in extras)
    return run(
        kernel, [(b, None) for b in (*blocks, *extras)], [((rows, columns), BF, None)],
        after=after, micros=1, name=name,
    )[0]


def stack_rows(pieces, after=(), name="stack_rows"):
    rows, columns = pieces[0].shape
    if rows % 16:
        return jnp.concatenate(pieces, 0)

    def kernel(*refs):
        for i in range(len(pieces)):
            refs[-1][i * rows : (i + 1) * rows, :] = refs[i][...]

    return run(
        kernel, [(p, None) for p in pieces], [((len(pieces) * rows, columns), BF, None)],
        after=after, micros=1.5, name=name,
    )[0]


def tensor_swaps(block):
    return [swap(block, "tensor", m) for m in range(1, lax.axis_size("tensor"))]


def chip_swaps(block):
    chips, _ = dp_plan()
    return [swap(block, "dp", m) for m in chips[1:]]


def core_swap(pieces, after=(), name="stack_rows"):
    _, doublings = dp_plan()
    rows = stack_rows(pieces, after, name)
    for step in doublings[:-1]:
        rows = jnp.concatenate([rows, swap(rows, "dp", step)], 0)
    return rows, swap(rows, "dp", doublings[-1])


def core_other(send):
    _, doublings = dp_plan()
    return swap(send, "dp", doublings[-1])


def reduce_core(pairs, extra=0, name="reduce_core"):
    chips, doublings = dp_plan()
    if len(doublings) > 1:
        keep, other = [jnp.concatenate(x, 1) for x in zip(*pairs)]
        for step in doublings[-2::-1]:
            both = (keep.astype(F32) + other.astype(F32)).astype(BF)
            main, tail = both[: both.shape[0] - extra], both[both.shape[0] - extra :]
            half = main.shape[0] // 2
            keep = jnp.concatenate([main[:half], tail], 0)
            other = swap(jnp.concatenate([main[half:], tail], 0), "dp", step)
        pairs = [(keep, other)]
    main = pairs[0][0].shape[0] - extra
    columns = sum(keep.shape[1] for keep, _ in pairs)
    rows = main // len(chips)
    if rows % 16:
        both = keep.astype(F32) + other.astype(F32)
        parts = [
            jnp.concatenate([both[i * rows : (i + 1) * rows], both[main:]], 0)
            for i in range(len(chips))
        ]
        return [parts[0]] + [p.astype(BF) for p in parts[1:]]

    def kernel(*refs):
        outs, at = refs[2 * len(pairs) :], 0
        for keep_ref, other_ref in zip(refs[0 : 2 * len(pairs) : 2], refs[1 : 2 * len(pairs) : 2]):
            cols = slice(at, at + keep_ref.shape[1])
            at += keep_ref.shape[1]
            for i, out in enumerate(outs):
                one = slice(i * rows, (i + 1) * rows)
                total = keep_ref[one, :].astype(F32) + other_ref[one, :].astype(F32)
                out[:rows, cols] = total.astype(out.dtype)
                if extra:
                    total = keep_ref[main:, :].astype(F32) + other_ref[main:, :].astype(F32)
                    out[rows:, cols] = total.astype(out.dtype)

    return run(
        kernel, [(x, None) for pair in pairs for x in pair],
        [((rows + extra, columns), F32 if i == 0 else BF, None) for i in range(len(chips))],
        micros=2.5, name=name,
    )


def reduce_chips(pieces):
    chips, _ = dp_plan()
    return [pieces[0]] + [swap(p, "dp", m) for p, m in zip(pieces[1:], chips[1:])]


def reduce_split(parts, widths, after=(), name="reduce_split"):
    size = lax.axis_size("tensor")
    rows = parts[0].shape[0]

    def kernel(*refs):
        total = refs[0][...]
        for r in refs[1 : len(parts)]:
            total = total + r[...].astype(F32)
        for mask in range(size):
            out = refs[len(parts) + mask]
            at, start = 0, 0
            for width in widths:
                cut = total[:, start + mask * width : start + (mask + 1) * width]
                out[:, at : at + width] = cut.astype(out.dtype)
                at += width
                start += size * width

    return run(
        kernel, [(p, None) for p in parts],
        [((rows, sum(widths)), F32 if m == 0 else BF, None) for m in range(size)],
        after=after, micros=1.5, name=name,
    )


def cut_columns(total, widths):
    parts, at = [], 0
    for width in widths:
        parts.append(total[:, at : at + width])
        at += width
    return parts


def reduce_tensor(cuts):
    total = cuts[0]
    for mask in range(1, len(cuts)):
        total = total + swap(cuts[mask], "tensor", mask).astype(F32)
    return total


def block_swap(values, mask):
    width = values.shape[1] // 4
    return jnp.concatenate(
        [values[:, (b ^ mask) * width : ((b ^ mask) + 1) * width] for b in range(4)], 1
    )


def edges_of(me, last, first):
    even = (me & 1) == 0
    return jnp.where(even, last, first), jnp.where(even, first, last)


def edges_from(me, by_1, by_3):
    even = (me & 1) == 0
    return jnp.where(even, by_3, by_1), jnp.where(even, by_1, by_3)


def sum_tensor(place, own, packs, name):
    by_1, by_2, by_3 = [swap(p, "tensor", m) for m, p in enumerate(packs, 1)]
    columns = own.shape[1]

    def kernel(place_ref, own_ref, one_ref, two_ref, three_ref, sums_ref, before_ref, after_ref):
        one, three = block_swap(one_ref[...], 1), block_swap(three_ref[...], 3)
        sums_ref[...] = own_ref[...] + one[:8] + block_swap(two_ref[...], 2) + three[:8]
        before_ref[...], after_ref[...] = edges_from(place_ref[0], one[8:], three[8:])

    return run(
        kernel, [(place, SMEM), (own, None), (by_1, None), (by_2, None), (by_3, None)],
        [((8, columns), F32, None)] + [((HALO, columns), F32, None)] * 2,
        micros=1, name=name,
    )


def sum_dp(total):
    _, doublings = dp_plan()
    for step in doublings:
        total = total + swap(total, "dp", step)
    return [total] + chip_swaps(total)


def norm(stream, gain, beta_row):
    centered = stream - jnp.mean(stream, -1, keepdims=True)
    inv_std = lax.rsqrt(jnp.mean(centered * centered, -1, keepdims=True) + EPS)
    scaled = centered * inv_std
    return scaled * gain + beta_row, scaled, inv_std


def norm_back(upstream, stream, gain):
    centered = stream - jnp.mean(stream, -1, keepdims=True)
    inv_std = lax.rsqrt(jnp.mean(centered * centered, -1, keepdims=True) + EPS)
    scaled = centered * inv_std
    grad = upstream * gain
    out = inv_std * (
        grad - jnp.mean(grad, -1, keepdims=True) - scaled * jnp.mean(grad * scaled, -1, keepdims=True)
    )
    return out, jnp.sum(upstream * scaled, 0, keepdims=True), jnp.sum(upstream, 0, keepdims=True)


def swish_slope(inner_act):
    logistic = jax.nn.sigmoid(inner_act)
    return logistic * (1.0 + inner_act * (1.0 - logistic))


def lanes_of(h, rows):
    lane = lax.broadcasted_iota(jnp.int32, (rows, LANES), 1)
    return (lane >= h * DH) & (lane < (h + 1) * DH)


def both(a_ref, b_ref):
    return jnp.concatenate([a_ref[...], b_ref[...]], 0)


def ordered_rows(me, block, rows):
    return pl.ds(pl.multiple_of((me ^ block) * rows, 64), rows)


def channel_sums(rows, count=8):
    return jnp.concatenate(rows + [jnp.zeros((count - len(rows), rows[0].shape[1]), F32)], 0)


def first_norm(stream, columns):
    rows, width = stream.shape
    half = width // 2

    def kernel(stream_ref, a_ref, b_ref, norms_ref, normed_ref):
        for ref, at in ((a_ref, 0), (b_ref, half)):
            norms_ref[:, at : at + half] = ref[...].astype(F32).T[:16]
        normed = norm(stream_ref[...], norms_ref[0:1, :], norms_ref[5:6, :])[0]
        normed_ref[...] = normed.astype(BF)

    return run(
        kernel, [(stream, None), (columns[0], None), (columns[1], None)],
        [((16, width), F32, None), ((rows, width), BF, None)], micros=1, name="first_norm",
    )


def ffn1_forward(stream, normed, halves, norms, after):
    rows, width = stream.shape
    half = width // 2
    hidden_units = halves[0].shape[1] // 2

    def kernel(stream_ref, normed_ref, a_ref, b_ref, norms_ref, inner_ref, out_ref, next_ref):
        normed = normed_ref[...]
        low = jnp.zeros((rows, half), F32)
        high = jnp.zeros((rows, half), F32)
        for j in range(0, hidden_units, 512):
            at = slice(j, j + 512)
            after = slice(hidden_units + j, hidden_units + j + 512)
            inner = dot(normed[:, :half], a_ref[:, at]) + dot(normed[:, half:], b_ref[:, at])
            inner_ref[:, at] = inner
            hidden = jax.nn.silu(inner).astype(BF)
            low = low + dot_t(hidden, a_ref[:, after])
            high = high + dot_t(hidden, b_ref[:, after])
        out = stream_ref[...] + 0.5 * jnp.concatenate([low, high], 1)
        out_ref[...] = out
        next_ref[...] = norm(out, norms_ref[1:2, :], norms_ref[6:7, :])[0].astype(BF)

    return run(
        kernel, [(x, None) for x in (stream, normed, *halves, norms)],
        [((rows, hidden_units), F32, None), ((rows, width), F32, None), ((rows, width), BF, None)],
        after=after, micros=4, name="ffn1_forward",
    )


def ffn1_hidden(blocks, halves, units):
    rows, width = blocks[0].shape
    half, count = width // 2, len(blocks)
    span = count * rows

    def kernel(a_ref, b_ref, *refs):
        hidden_ref, slope_ref, normed_t_ref = refs[count:]
        for b in range(count):
            normed = refs[b][...]
            at = slice(b * rows, (b + 1) * rows)
            inner = dot(normed[:, :half], a_ref[...]) + dot(normed[:, half:], b_ref[...])
            logistic = jax.nn.sigmoid(inner)
            hidden_ref[at, :] = (inner * logistic).astype(BF)
            slope_ref[at, :] = logistic * (1.0 + inner * (1.0 - logistic))
            normed_t_ref[:, at] = normed.T

    own = pl.BlockSpec((half, units), lambda g: (0, 0), pipeline_mode=pl.Buffered(1))
    return run(
        kernel, [(x, own) for x in halves] + [(x, None) for x in blocks],
        [((span, units), BF, None), ((span, units), F32, None), ((width, span), BF, None)],
        micros=2, name="ffn1_hidden",
    )


def ffn1_branch_grad(own_a, own_b, others, stream_grad, stream, norms, after):
    rows, width = stream.shape

    def kernel(*refs):
        upstream = refs[0][...] + refs[1][...]
        for r in refs[2 : 2 + len(others)]:
            upstream = upstream + r[...].astype(F32)
        grad_ref, stream_ref, norms_ref, out_ref, gb_ref, sums_ref = refs[2 + len(others) :]
        extra, dgain, dbeta = norm_back(upstream, stream_ref[...], norms_ref[1:2, :])
        sums_ref[...] = channel_sums([dgain, dbeta])
        out = grad_ref[...] + extra
        out_ref[...] = out
        gb_ref[...] = (0.5 * out).astype(BF)

    ins = [own_a, own_b, *others, stream_grad, stream, norms]
    return run(
        kernel, [(x, None) for x in ins],
        [((rows, width), F32, None), ((rows, width), BF, None), ((8, width), F32, None)],
        after=after, micros=1.5, name="ffn1_branch_grad",
    )


def ffn1_back_tokens(stream_grad, gb, stream, norms, inner, halves, order, sums, after):
    rows, width = stream.shape
    hidden_units = inner.shape[1]
    half = width // 2

    def kernel(grad_ref, gb_ref, stream_ref, norms_ref, inner_ref, a_ref, b_ref, order_ref, s1_ref, s2_ref, s4_ref,
               out_ref, norm_rows_ref):
        gb = gb_ref[...]
        low = jnp.zeros((rows, half), F32)
        high = jnp.zeros((rows, half), F32)
        for j in range(0, hidden_units, 512):
            at = slice(j, j + 512)
            after = slice(hidden_units + j, hidden_units + j + 512)
            grad = dot(gb[:, :half], a_ref[:, after]) + dot(gb[:, half:], b_ref[:, after])
            grad = (grad * swish_slope(inner_ref[:, at])).astype(BF)
            low = low + dot_t(grad, a_ref[:, at])
            high = high + dot_t(grad, b_ref[:, at])
        extra, dgain, dbeta = norm_back(
            jnp.concatenate([low, high], 1), stream_ref[...], norms_ref[0:1, :]
        )
        gains = [dgain, s1_ref[0:1, :], s2_ref[0:1, :], s4_ref[0:1, :], s4_ref[2:3, :]]
        betas = [dbeta, s1_ref[1:2, :], s2_ref[1:2, :], s4_ref[1:2, :], s4_ref[3:4, :]]
        norm_rows_ref[...] = channel_sums(gains + betas, 16)
        out_ref[...] = dot(
            grad_ref[...] + extra, order_ref[...].astype(F32), ((1,), (1,)), precision=HIGHEST
        )

    ins = [stream_grad, gb, stream, norms, inner, *halves, order, *sums]
    return run(
        kernel, [(x, None) for x in ins],
        [((rows, width), F32, None), ((16, width), F32, None)],
        after=after, micros=5, name="ffn1_back_tokens",
    )


def ffn1_back_weights(gb_blocks, hidden, slope, normed_t, halves, norm_rows, after):
    width, span = normed_t.shape
    units, rows, half = hidden.shape[1], gb_blocks[0].shape[0], width // 2
    count = len(gb_blocks)

    def kernel(hidden_ref, slope_ref, normed_t_ref, a_ref, b_ref, *refs):
        block_refs, norm_refs = refs[:count], refs[count : 2 * count]
        keep_ref, send_ref, gb_t, grad = refs[2 * count :]
        for b in range(count):
            gb = block_refs[b][...]
            at = slice(b * rows, (b + 1) * rows)
            gb_t[:, at] = gb.T
            one = dot(gb[:, :half], a_ref[...]) + dot(gb[:, half:], b_ref[...])
            grad[at, :] = (one * slope_ref[at, :]).astype(BF)
        columns = sum(r[...] for r in norm_refs)
        columns = jnp.concatenate([columns, jnp.zeros((LANES - 16, width), F32)], 0).T
        grads = [dot(normed_t_ref[...], grad[...]), dot(gb_t[...], hidden_ref[...]), columns]
        at = 0
        for g in grads:
            keep_ref[:, at : at + g.shape[1]] = g[:half].astype(BF)
            send_ref[:, at : at + g.shape[1]] = g[half:].astype(BF)
            at += g.shape[1]

    first = halves[0].shape[1] // (2 * units)
    own = pl.BlockSpec((half, units), lambda g: (0, first), pipeline_mode=pl.Buffered(1))
    total = 2 * units + LANES
    return run(
        kernel,
        [(hidden, None), (slope, None), (normed_t, None), (halves[0], own), (halves[1], own)]
        + [(x, None) for x in (*gb_blocks, *norm_rows)],
        [((half, total), BF, None), ((half, total), BF, None)],
        scratch=[pltpu.VMEM((width, span), BF), pltpu.VMEM((span, units), BF)],
        after=after, micros=4, name="ffn1_back_weights",
    )


def attn_queries(normed, halves, rel_rows, small, span, bias_row, after):
    rows, width = normed.shape
    wide, columns = rel_rows.shape[0], small.shape[1]
    groups, pairs = columns // LANES, LANES // DH
    half = width // 2

    def kernel(rows_ref, aq_ref, bq_ref, ap_ref, bp_ref, rel_ref, small_ref, qu_ref, qv_ref, pos_ref, table_ref):
        queries = dot(rows_ref[...], both(aq_ref, bq_ref))
        bias = small_ref[...].astype(F32)
        qu_ref[...] = (queries + bias[bias_row : bias_row + 1]).astype(BF)
        query_v = (queries + bias[bias_row + 1 : bias_row + 2]).astype(BF)
        qv_ref[...] = query_v
        positions = dot(rel_ref[...], both(ap_ref, bp_ref)).astype(BF)
        pos_ref[...] = positions
        for h in range(pairs):
            mine = jnp.where(lanes_of(h, rows), query_v, jnp.zeros_like(query_v))
            table = dot_t(mine, positions)
            shifted = pltpu.roll(table, wide - (rows - 1), 1, stride=1, stride_axis=0)
            table_ref[h] = shifted[:, :span]

    def weight(i):
        return column(half, i * groups)

    a, b = halves
    return run(
        kernel,
        [(normed, None), (a, weight(0)), (b, weight(0)), (a, weight(3)), (b, weight(3)), (rel_rows, None), (small, column(small.shape[0]))],
        [((rows, columns), BF, column(rows)), ((rows, columns), BF, column(rows)), ((wide, columns), BF, column(wide)),
         ((groups * pairs, rows, span), F32, heads(pairs, rows, span))],
        grid=(groups,), after=after, micros=0.2, name="attn_queries",
    )


def attn_main(place, blocks, halves, query_u, table, stream, norms):
    rows, width = stream.shape
    span, columns = table.shape[2], query_u.shape[1]
    groups, pairs = columns // LANES, LANES // DH
    half = width // 2
    count = len(blocks)

    def kernel(place_ref, *refs):
        block_refs = refs[:count]
        (ak_ref, bk_ref, av_ref, bv_ref, ao_ref, bo_ref, qu_ref, table_ref, stream_ref, norms_ref,
         mixed_ref, probs_ref, keys_ref, vals_ref, out_ref, normed_ref, edge_1_ref, edge_3_ref) = refs[count:]
        me, length = place_ref[0], place_ref[1]
        wk, wv = both(ak_ref, bk_ref), both(av_ref, bv_ref)
        for b in range(count):
            at = ordered_rows(me, b, rows)
            keys_ref[at, :] = dot(block_refs[b][...], wk).astype(BF)
            vals_ref[at, :] = dot(block_refs[b][...], wv).astype(BF)
        keys, vals, query_u = keys_ref[...], vals_ref[...], qu_ref[...]
        visible = lax.broadcasted_iota(jnp.int32, (rows, span), 1) < length
        mixed = jnp.zeros((rows, LANES), F32)
        for h in range(pairs):
            mine = lanes_of(h, rows)
            content = dot_t(jnp.where(mine, query_u, jnp.zeros_like(query_u)), keys)
            scores = jnp.where(visible, (content + table_ref[h]) * DH ** (-0.5), NEG)
            exponent = jnp.exp(scores - jnp.max(scores, -1, keepdims=True))
            probs = exponent / jnp.sum(exponent, -1, keepdims=True)
            probs_ref[h] = probs
            mixed = jnp.where(mine, dot(probs.astype(BF), vals), mixed)
        mixed = mixed.astype(BF)
        mixed_ref[...] = mixed

        @pl.when(pl.program_id(0) == 0)
        def _():
            out_ref[...] = stream_ref[...]

        out_ref[...] += dot_t(mixed, both(ao_ref, bo_ref))

        @pl.when(pl.program_id(0) == groups - 1)
        def _():
            normed = norm(out_ref[...], norms_ref[2:3, :], norms_ref[7:8, :])[0].astype(BF)
            normed_ref[...] = normed
            edge_1_ref[...], edge_3_ref[...] = edges_of(me, normed[rows - HALO :], normed[:HALO])

    def weight(i):
        return column(half, i * groups)

    a, b = halves
    return run(
        kernel,
        [(place, SMEM)] + [(x, None) for x in blocks]
        + [(w, weight(i)) for i in (1, 2, 4) for w in (a, b)]
        + [(query_u, column(rows)), (table, heads(pairs, rows, span)), (stream, None), (norms, None)],
        [((rows, columns), BF, column(rows)), ((groups * pairs, rows, span), F32, heads(pairs, rows, span)),
         ((span, columns), BF, column(span)), ((span, columns), BF, column(span)),
         ((rows, width), F32, None), ((rows, width), BF, None), ((HALO, width), BF, None), ((HALO, width), BF, None)],
        grid=(groups,), micros=9, name="attn_main",
    )


def attn_back_keys(place, gb, halves, probs, keys, vals, query_u, count, after):
    rows, width = gb.shape
    span, columns = keys.shape
    groups, pairs = columns // LANES, LANES // DH
    half = width // 2

    def kernel(place_ref, gb_ref, ao_ref, bo_ref, ak_ref, bk_ref, av_ref, bv_ref, probs_ref, keys_ref, vals_ref, qu_ref,
               gp_ref, dk_ref, dv_ref, own_ref, *refs):
        other_refs, total = refs[:-1], refs[-1]
        me = place_ref[0]
        step = pl.program_id(0)
        gm = dot(gb_ref[...], both(ao_ref, bo_ref)).astype(BF)
        gm_t, qu_t = gm.T, qu_ref[...].T
        vals = vals_ref[...]
        dk_t, dv_t = [], []
        for h in range(pairs):
            head = slice(h * DH, (h + 1) * DH)
            probs = probs_ref[h]
            dprobs = dot_t(jnp.where(lanes_of(h, rows), gm, jnp.zeros_like(gm)), vals)
            delta = jnp.sum(dprobs * probs, -1, keepdims=True)
            gp = ((DH ** (-0.5) * probs) * (dprobs - delta)).astype(BF)
            gp_ref[h] = gp
            dv_t.append(dot(gm_t[head], probs.astype(BF)))
            dk_t.append(dot(qu_t[head], gp))
        dk = jnp.concatenate(dk_t, 0).T.astype(BF)
        dv = jnp.concatenate(dv_t, 0).T.astype(BF)
        dk_ref[...] = dk
        dv_ref[...] = dv
        grad = dot_t(dk, both(ak_ref, bk_ref)) + dot_t(dv, both(av_ref, bv_ref))

        @pl.when(step == 0)
        def _():
            total[...] = grad

        @pl.when(step > 0)
        def _():
            total[...] += grad

        @pl.when(step == groups - 1)
        def _():
            own_ref[...] = total[ordered_rows(me, 0, rows), :]
            for b in range(1, count):
                other_refs[b - 1][...] = total[ordered_rows(me, b, rows), :].astype(BF)

    def weight(i):
        return column(half, i * groups)

    a, b = halves
    return run(
        kernel,
        [(place, SMEM), (gb, None)] + [(w, weight(i)) for i in (4, 1, 2) for w in (a, b)]
        + [(probs, heads(pairs, rows, span)), (keys, column(span)), (vals, column(span)), (query_u, column(rows))],
        [((groups * pairs, rows, span), BF, heads(pairs, rows, span)), ((span, columns), BF, column(span)), ((span, columns), BF, column(span)),
         ((rows, width), F32, None)] + [((rows, width), BF, None)] * (count - 1),
        scratch=[pltpu.VMEM((span, width), F32)],
        grid=(groups,), after=after, micros=11, name="attn_back_keys",
    )


def attn_back_queries(place, gp, keys, positions, query_v, dk, dv, mixed, gb, blocks, rel_rows, halves, taps_grad, after):
    rows, width = gb.shape
    span, columns = keys.shape
    wide = rel_rows.shape[0]
    groups, pairs = columns // LANES, LANES // DH
    half = width // 2
    count = len(blocks)

    def kernel(place_ref, gp_ref, keys_ref, pos_ref, qv_ref, dk_ref, dv_ref, mixed_ref, aq_ref, bq_ref, gb_ref, rel_ref, dtaps_ref, *refs):
        block_refs = refs[:count]
        keep_ref, send_ref, own_ref, ordered_t, rel_t, gb_t = refs[count:]
        me = place_ref[0]
        step = pl.program_id(0)

        @pl.when(step == 0)
        def _():
            for b in range(count):
                rel_t[:, b * rows : (b + 1) * rows] = block_refs[b][...].T
            for k in range(count):
                picked = rel_t[:, 0:rows]
                for b in range(1, count):
                    picked = jnp.where((me ^ b) == k, rel_t[:, b * rows : (b + 1) * rows], picked)
                ordered_t[:, k * rows : (k + 1) * rows] = picked
            rel_t[...] = rel_ref[...].T
            gb_t[...] = gb_ref[...].T
            own_ref[...] = jnp.zeros_like(own_ref)

        i = lax.broadcasted_iota(jnp.int32, (rows, rows), 0)
        j = lax.broadcasted_iota(jnp.int32, (rows, rows), 1)
        flip = jnp.where(i + j == rows - 1, 1.0, 0.0)
        flip_low = flip.astype(BF)
        keys, positions = keys_ref[...], pos_ref[...]
        qv_t = dot(flip_low, qv_ref[...]).astype(BF).T
        du = jnp.zeros((rows, LANES), F32)
        dv_rows = jnp.zeros((rows, LANES), F32)
        dp_t = []
        for h in range(pairs):
            mine = lanes_of(h, rows)
            gp = gp_ref[h]
            du = jnp.where(mine, dot(gp, keys), du)
            flipped = dot(flip_low, gp)
            table = jnp.concatenate([flipped, jnp.zeros((rows, wide - span), F32)], 1)
            table = pltpu.roll(table, 0, 1, stride=1, stride_axis=0).astype(BF)
            dp_t.append(dot(qv_t[h * DH : (h + 1) * DH], table))
            dv_rows = jnp.where(mine, dot(table, positions), dv_rows)
        dv_rows = dot(flip, dv_rows, precision=HIGHEST)
        bias = channel_sums(
            [jnp.sum(du, 0, keepdims=True), jnp.sum(dv_rows, 0, keepdims=True)], 16
        )
        nothing = jnp.zeros((16, LANES), F32)
        extras = [dtaps_ref[:16, :], dtaps_ref[16:, :], bias, nothing, nothing]
        dq = (du + dv_rows).astype(BF)
        dp = jnp.concatenate(dp_t, 0).T.astype(BF)
        own_ref[...] += dot_t(dq, both(aq_ref, bq_ref))
        grads = [
            dot(block_refs[0][...].T, dq),
            dot(ordered_t[...], dk_ref[...]),
            dot(ordered_t[...], dv_ref[...]),
            dot(rel_t[...], dp),
            dot(gb_t[...], mixed_ref[...]),
        ]
        for n, grad in enumerate(grads):
            at = pl.ds(pl.multiple_of((n * groups + step) * LANES, LANES), LANES)
            keep_ref[:half, at] = grad[:half].astype(BF)
            send_ref[:half, at] = grad[half:].astype(BF)
            keep_ref[half:, at] = extras[n].astype(BF)
            send_ref[half:, at] = extras[n].astype(BF)

    a, b = halves
    return run(
        kernel,
        [(place, SMEM), (gp, heads(pairs, rows, span)), (keys, column(span)), (positions, column(wide)), (query_v, column(rows)),
         (dk, column(span)), (dv, column(span)), (mixed, column(rows)), (a, column(half)), (b, column(half)), (gb, None), (rel_rows, None), (taps_grad, column(32))]
        + [(x, None) for x in blocks],
        [((half + 16, 5 * columns), BF, None), ((half + 16, 5 * columns), BF, None), ((rows, width), F32, None)],
        scratch=[pltpu.VMEM((width, span), BF), pltpu.VMEM((width, wide), BF), pltpu.VMEM((width, rows), BF)],
        grid=(groups,), after=after, micros=13, name="attn_back_queries",
    )


def joined(a_ref, b_ref, at):
    return jnp.concatenate([a_ref[:, at], b_ref[:, at]], 0)


def conv_forward(place, normed, by_1, by_3, halves, at, small, ker):
    rows, width = normed.shape
    columns = small.shape[1]
    groups, half, ext = columns // LANES, width // 2, rows + 2 * HALO

    def kernel(place_ref, rows_ref, one_ref, three_ref, av_ref, bv_ref, ag_ref, bg_ref, small_ref,
               gated_ref, value_ref, gate_ref, depth_ref, sums_ref, pack_1_ref, pack_3_ref):
        me, length, start = place_ref[0], place_ref[1], place_ref[2]
        before, after = edges_from(me, one_ref[...], three_ref[...])
        tokens = jnp.concatenate([before, rows_ref[...], after], 0)
        value_half = dot(tokens, both(av_ref, bv_ref))
        logistic = jax.nn.sigmoid(dot(tokens, both(ag_ref, bg_ref)))
        token = start - HALO + lax.broadcasted_iota(jnp.int32, value_half.shape, 0)
        mask = jnp.where((token >= 0) & (token < length), 1.0, 0.0)
        gated_ref[...] = mask * value_half * logistic
        value_ref[...] = value_half[HALO : HALO + rows]
        gate_ref[...] = logistic[HALO : HALO + rows]
        taps = small_ref[...].astype(F32)
        depth = jnp.zeros((rows, LANES), F32)
        for k in range(ker):
            depth = depth + taps[k : k + 1, :] * gated_ref[k + 1 : k + 1 + rows, :]
        depth_ref[...] = depth
        mask = mask[HALO : HALO + rows]
        masked = depth * mask
        sums = channel_sums([jnp.sum(x, 0, keepdims=True) for x in (masked, masked * depth, mask)])
        sums_ref[...] = sums
        one, three = edges_of(me, depth[rows - HALO :], depth[:HALO])
        pack_1_ref[:8, :], pack_1_ref[8:, :] = sums, one
        pack_3_ref[:8, :], pack_3_ref[8:, :] = sums, three

    return run(
        kernel,
        [(place, SMEM), (normed, None), (by_1, None), (by_3, None)]
        + [(w, column(half, at + i * groups)) for i in (0, 1) for w in halves] + [(small, column(small.shape[0]))],
        [((ext, columns), F32, column(ext))] + [((rows, columns), F32, column(rows))] * 3
        + [((8, columns), F32, column(8))] + [((8 + HALO, columns), F32, column(8 + HALO))] * 2,
        grid=(groups,), micros=4, name="conv_forward",
    )


def batch_terms(sums_ref):
    count = sums_ref[2:3, :]
    mean = sums_ref[0:1, :] / count
    inv_std = lax.rsqrt(sums_ref[1:2, :] / count - mean * mean + EPS)
    return count, mean, inv_std


def turn(place, stream, depth, sums, norms, small, ker, halves, cotangent):
    rows, width = stream.shape
    columns = depth.shape[1]
    groups = columns // LANES
    half = width // 2
    total = halves[0].shape[1]
    hidden_units = (total - 3 * columns) // 2
    units = hidden_units // groups
    parts = len(sums)

    def kernel(place_ref, stream_ref, depth_ref, norms_ref, small_ref, ac_ref, bc_ref, ai_ref, bi_ref, ao_ref, bo_ref, cot_ref, *refs):
        (sums_ref, out_ref, keep_ref, send_ref, ckeep_ref, csend_ref, grad_ref, ngrad_ref, own_ref, pack_1_ref, pack_3_ref, nsums_ref,
         inner_ref, hidden_ref) = refs[parts:]
        sums_ref[...] = sum(r[...] for r in refs[:parts])
        _, mean, inv_std = batch_terms(sums_ref)
        batch_gain = small_ref[...].astype(F32)[ker + 2 : ker + 3]
        batch_bias = small_ref[...].astype(F32)[ker + 3 : ker + 4]
        scaled = (depth_ref[...] - mean) * inv_std
        normal = scaled * batch_gain + batch_bias
        active = jax.nn.silu(normal).astype(BF)
        wc = both(ac_ref, bc_ref)
        stream3 = stream_ref[...] + dot_t(active, wc)
        normed = norm(stream3, norms_ref[3:4, :], norms_ref[8:9, :])[0].astype(BF)
        branch = jnp.zeros((rows, width), F32)
        for p in range(groups):
            j = slice(p * units, (p + 1) * units)
            inner = dot(normed, joined(ai_ref, bi_ref, j))
            inner_ref[:, j] = inner
            hidden = jax.nn.silu(inner).astype(BF)
            hidden_ref[:, j] = hidden
            branch = branch + dot_t(hidden, joined(ao_ref, bo_ref, j))
        stream4 = stream3 + 0.5 * branch
        out_ref[...] = norm(stream4, norms_ref[4:5, :], norms_ref[9:10, :])[0].astype(BF)
        grad, gain5, beta5 = norm_back(cot_ref[...], stream4, norms_ref[4:5, :])
        gb = (0.5 * grad).astype(BF)
        gb_t, normed_t = gb.T, normed.T
        upstream = jnp.zeros((rows, width), F32)
        for p in range(groups):
            j = slice(p * units, (p + 1) * units)
            after = slice(hidden_units + p * units, hidden_units + (p + 1) * units)
            inner_grad = dot(gb, joined(ao_ref, bo_ref, j))
            inner_grad = (inner_grad * swish_slope(inner_ref[:, j])).astype(BF)
            in_grad = dot(normed_t, inner_grad)
            keep_ref[:, j] = in_grad[:half].astype(BF)
            send_ref[:, j] = in_grad[half:].astype(BF)
            out_grad = dot(gb_t, hidden_ref[:, j])
            keep_ref[:, after] = out_grad[:half].astype(BF)
            send_ref[:, after] = out_grad[half:].astype(BF)
            upstream = upstream + dot_t(inner_grad, joined(ai_ref, bi_ref, j))
        extra, gain4, beta4 = norm_back(upstream, stream3, norms_ref[3:4, :])
        nsums_ref[...] = channel_sums([gain4, beta4, gain5, beta5])
        grad = grad + extra
        grad_ref[...] = grad
        gb = grad.astype(BF)
        weight_grad = dot(gb.T, active)
        ckeep_ref[...] = weight_grad[:half].astype(BF)
        csend_ref[...] = weight_grad[half:].astype(BF)
        ngrad = dot(gb, wc) * swish_slope(normal)
        ngrad_ref[...] = ngrad
        own = channel_sums([jnp.sum(ngrad, 0, keepdims=True), jnp.sum(ngrad * scaled, 0, keepdims=True)])
        own_ref[...] = own
        one, three = edges_of(place_ref[0], ngrad[rows - HALO :], ngrad[:HALO])
        pack_1_ref[:8, :], pack_1_ref[8:, :] = own, one
        pack_3_ref[:8, :], pack_3_ref[8:, :] = own, three

    def block(columns, index):
        return pl.BlockSpec((half, columns), lambda g: (0, index), pipeline_mode=pl.Buffered(1))

    specs = [block(columns, (total - columns) // columns), block(hidden_units, 0), block(hidden_units, 1)]
    return run(
        kernel,
        [(place, SMEM), (stream, None), (depth, None), (norms, None), (small, None)]
        + [(w, spec) for spec in specs for w in halves] + [(cotangent, None)]
        + [(s, None) for s in sums],
        [((8, columns), F32, None), ((rows, width), BF, None), ((half, 2 * hidden_units), BF, None), ((half, 2 * hidden_units), BF, None),
         ((half, columns), BF, None), ((half, columns), BF, None), ((rows, width), F32, None), ((rows, columns), F32, None), ((8, columns), F32, None)]
        + [((8 + HALO, columns), F32, None)] * 2 + [((8, width), F32, None)],
        scratch=[pltpu.VMEM((rows, hidden_units), F32), pltpu.VMEM((rows, hidden_units), BF)],
        micros=12, limit=36, name="turn",
    )


def conv_backward(place, ngrad, ngrad_edges, depth, depth_edges, sums, totals, small, ker, gated, value_half, logistic, normed, halves, at,
                  keep, send, stream_grad, stream, norms, after):
    rows, columns = depth.shape
    width = normed.shape[1]
    groups, half, ext = columns // LANES, width // 2, rows + 2 * HALO
    span = rows * lax.axis_size("tensor")
    parts = len(totals)

    def kernel(place_ref, ngrad_ref, nb_ref, na_ref, depth_ref, db_ref, da_ref, sums_ref, small_ref, gated_ref, value_ref, gate_ref,
               normed_ref, av_ref, bv_ref, ag_ref, bg_ref, sgrad_ref, stream_ref, norms_ref, *refs):
        (ckeep_ref, csend_ref, keep_ref, send_ref, dtaps_ref, out_ref, gb_ref, nsums_ref, totals_ref, grad_ref, acc_ref, normed_t) = refs[parts:]
        length, start = place_ref[1], place_ref[2]
        step = pl.program_id(0)
        totals_ref[...] = sum(r[...] for r in refs[:parts])

        @pl.when(step == 0)
        def _():
            normed_t[...] = normed_ref[...].T
            acc_ref[...] = jnp.zeros_like(acc_ref)
            keep_ref[:, 2 * columns :] = ckeep_ref[...]
            send_ref[:, 2 * columns :] = csend_ref[...]

        taps = small_ref[...].astype(F32)
        count, mean, inv_std = batch_terms(sums_ref)
        batch_gain = taps[ker + 2 : ker + 3]
        sum_gain = batch_gain * totals_ref[0:1, :]
        sum_cross = batch_gain * totals_ref[1:2, :]
        square = inv_std * inv_std * sum_cross / count
        shift = mean * square - inv_std * sum_gain / count
        scale = inv_std * batch_gain
        for first, part, deep in ((0, nb_ref, db_ref), (HALO, ngrad_ref, depth_ref), (HALO + rows, na_ref, da_ref)):
            token = start + (first - HALO) + lax.broadcasted_iota(jnp.int32, part.shape, 0)
            grad = scale * part[...] + jnp.where(token < length, shift - deep[...] * square, 0.0)
            grad_ref[first : first + part.shape[0], :] = jnp.where(
                (token >= 0) & (token < span), grad, 0.0
            )
        own = grad_ref[HALO : HALO + rows, :]
        total = jnp.zeros((rows, LANES), F32)
        for k in range(ker):
            total = total + taps[k : k + 1, :] * grad_ref[ker - k : ker - k + rows, :]
            dtaps_ref[k : k + 1, :] = jnp.sum(
                own * gated_ref[k + 1 : k + 1 + rows, :], 0, keepdims=True
            )
        dtaps_ref[ker:, :] = jnp.zeros_like(dtaps_ref[ker:, :])
        token = start + lax.broadcasted_iota(jnp.int32, total.shape, 0)
        total = jnp.where(token < length, total, 0.0)
        logistic = gate_ref[...]
        dvalue = (total * logistic).astype(BF)
        dgate = (total * value_ref[...] * logistic * (1.0 - logistic)).astype(BF)
        acc_ref[...] += dot_t(dvalue, both(av_ref, bv_ref))
        acc_ref[...] += dot_t(dgate, both(ag_ref, bg_ref))
        for n, grad in enumerate((dvalue, dgate)):
            weight_grad = dot(normed_t[...], grad)
            cols = pl.ds(pl.multiple_of((2 * step + n) * LANES, LANES), LANES)
            keep_ref[:, cols] = weight_grad[:half].astype(BF)
            send_ref[:, cols] = weight_grad[half:].astype(BF)

        @pl.when(step == groups - 1)
        def _():
            extra, dgain, dbeta = norm_back(acc_ref[...], stream_ref[...], norms_ref[2:3, :])
            out = sgrad_ref[...] + extra
            out_ref[...] = out
            gb_ref[...] = out.astype(BF)
            nsums_ref[...] = channel_sums([dgain, dbeta])

    edge = column(HALO)
    ins = [(place, SMEM), (ngrad, column(rows)), (ngrad_edges[0], edge), (ngrad_edges[1], edge), (depth, column(rows)), (depth_edges[0], edge), (depth_edges[1], edge),
           (sums, column(8)), (small, column(small.shape[0])), (gated, column(ext)), (value_half, column(rows)), (logistic, column(rows)),
           (normed, None)] + [(w, column(half, at + i * groups)) for i in (0, 1) for w in halves] + [
           (stream_grad, None), (stream, None), (norms, None)] + [(t, column(8)) for t in totals] + [(keep, None), (send, None)]
    return run(
        kernel, ins,
        [((half, 3 * columns), BF, None), ((half, 3 * columns), BF, None), ((32, columns), F32, column(32)),
         ((rows, width), F32, None), ((rows, width), BF, None), ((8, width), F32, None), ((8, columns), F32, column(8))],
        scratch=[pltpu.VMEM((ext, LANES), F32), pltpu.VMEM((rows, width), F32), pltpu.VMEM((width, rows), BF)],
        grid=(groups,), after=after, micros=8, name="conv_backward",
    )


def on_device(
    inputs,
    lengths,
    rel_embed,
    out_grad,
    norm_gain,
    norm_bias,
    ffn1_in_w,
    ffn1_out_w,
    query_w,
    key_w,
    value_w,
    pos_w,
    attn_out,
    pos_bias,
    conv_value,
    conv_gate,
    depthwise,
    bn_gain,
    bn_bias,
    conv_out,
    ffn2_in_w,
    ffn2_out_w,
):
    size_t = lax.axis_size("tensor")
    me_t = lax.axis_index("tensor")
    me_dp = lax.axis_index("dp")
    size_dp = lax.axis_size("dp")
    rows, width = inputs.shape[1], inputs.shape[2]
    shard = width // size_dp
    part, units = query_w.shape[1], ffn1_in_w.shape[1]
    channels, hidden_units = size_t * part, size_t * units
    span = rows * size_t
    ker = depthwise.shape[0]
    place = jnp.stack([me_t, lengths[0], me_t * rows]).astype(jnp.int32)

    first_shard = regroup([ffn1_in_w, ffn1_out_w.T], [units], name="pack_ffn1")
    first_parts = [first_shard] + tensor_swaps(first_shard)
    norm_cols = jnp.concatenate([norm_gain, norm_bias], 0)
    norm_cols = jnp.pad(norm_cols, ((0, LANES - norm_cols.shape[0]), (0, 0))).T
    norm_cols = core_swap([norm_cols] + chip_swaps(norm_cols), name="rows_norms")
    small = jnp.concatenate([depthwise, pos_bias, bn_gain[None], bn_bias[None]], 0)
    step = max(shard, 16)
    small = jnp.pad(small, ((0, -small.shape[0] % step), (0, 0)))
    small = [small[i : i + shard] for i in range(0, small.shape[0], shard)]
    attn_shard = regroup(
        [query_w, key_w, value_w, pos_w, attn_out.T], [part], small, after=first_parts[1:],
        name="pack_attn",
    )
    attn_parts = [attn_shard] + tensor_swaps(attn_shard)
    second_shard = regroup(
        [ffn2_in_w, ffn2_out_w.T], [units], [conv_value, conv_gate, conv_out.T],
        after=attn_parts[1:], name="pack_second",
    )
    second_parts = [second_shard] + tensor_swaps(second_shard)
    conv_at = 2 * hidden_units // LANES

    feature = jnp.arange(width)
    block = feature // shard
    mask_of = (block & ~7) | ((block >> 2) & 1) | ((block & 3) << 1)
    source = (mask_of ^ me_dp) * shard + feature % shard
    order = (jnp.arange(width)[:, None] == source[None, :]).astype(BF)
    stream0 = dot(inputs[0], order)
    cotangent = dot(out_grad[0], order)
    wide = -(-(span + rows) // LANES) * LANES
    rel_rows = jnp.pad(rel_embed, ((0, span + wide - rel_embed.shape[0]), (0, 0)))
    rel_rows = lax.dynamic_slice_in_dim(rel_rows, rows * (size_t - 1 - me_t), wide, 0)
    rel_rows = dot(rel_rows, order).astype(BF)

    norms, normed_one = first_norm(stream0, norm_cols)
    first_block = regroup(first_parts, [units] * 2, after=[normed_one], name="cols_ffn1")
    first_blocks = [first_block] + chip_swaps(first_block)
    attn_block = regroup(attn_parts, [part] * 5, name="cols_attn")
    attn_blocks = [attn_block] + chip_swaps(attn_block)
    second_block = regroup(second_parts, [units] * 2 + [part] * 3, name="cols_second")
    second_blocks = [second_block] + chip_swaps(second_block)
    small = jnp.concatenate(
        [
            jnp.concatenate([p[:, 5 * part + i * LANES :][:, :LANES] for i in range(len(small))], 0)
            for p in attn_parts
        ],
        1,
    )
    first_w = core_swap(first_blocks, after=[attn_block, second_block], name="rows_ffn1")
    inner_one, stream1, normed_two = ffn1_forward(
        stream0, normed_one, first_w, norms, []
    )
    token_blocks = [normed_two] + tensor_swaps(normed_two)
    attn_w = core_swap(attn_blocks, after=[*token_blocks[1:], second_blocks[1]], name="rows_attn")
    query_u, query_v, positions, table = attn_queries(
        normed_two, attn_w, rel_rows, small, span, ker, []
    )
    normed_one = regroup([normed_one], [width], after=[table], name="carry_norm")
    first_tokens = [normed_one] + tensor_swaps(normed_one)
    mixed, probs, keys, vals, stream2, normed_three, edge_1, edge_3 = attn_main(
        place, token_blocks, attn_w, query_u, table, stream1, norms
    )
    hidden, slope, normed_t = ffn1_hidden(first_tokens, first_w, units)
    second_w = core_swap(second_blocks, after=[stream2, hidden], name="rows_second")
    gated, value_half, logistic, depth, sums, *packs = conv_forward(
        place, normed_three, swap(edge_1, "tensor", 1), swap(edge_3, "tensor", 3), second_w,
        conv_at, small, ker,
    )
    sums, *depth_edges = sum_tensor(place, sums, [packs[0], sums, packs[1]], "sums_forward")
    sums, block_out, keep, send, out_keep, out_send, stream_grad, ngrad, totals, *packs, norm_sums_4 = turn(
        place, stream2, depth, sum_dp(sums), norms, small, ker, second_w, cotangent
    )
    other = core_other(send)
    totals, *ngrad_edges = sum_tensor(place, totals, [packs[0], totals, packs[1]], "sums_back")
    conv_keep, conv_send, taps_grad, stream_grad, gb, norm_sums_2, totals = conv_backward(
        place, ngrad, ngrad_edges, depth, depth_edges, sums, sum_dp(totals), small, ker, gated,
        value_half, logistic, normed_three, second_w, conv_at, out_keep, out_send, stream_grad, stream2, norms, [other],
    )
    second_pieces = reduce_core([(keep, other), (conv_keep, core_other(conv_send))], name="core_second")
    second_cuts = reduce_chips(second_pieces)
    gp, dk, dv, own_a, *others = attn_back_keys(
        place, gb, attn_w, probs, keys, vals, query_u, size_t, [second_pieces[1]]
    )
    others = [swap(o, "tensor", m) for m, o in enumerate(others, 1)]
    keep, send, own_b = attn_back_queries(
        place, gp, keys, positions, query_v, dk, dv, mixed, gb, token_blocks, rel_rows, attn_w,
        taps_grad, [],
    )
    attn_pieces = reduce_core([(keep, core_other(send))], 16, name="core_attn")
    attn_cuts = reduce_chips(attn_pieces)
    stream_grad, gb, norm_sums_1 = ffn1_branch_grad(
        own_a, own_b, others, stream_grad, stream1, norms, second_cuts[1:2]
    )
    gb_blocks = [gb] + tensor_swaps(gb)
    input_grad, norm_rows = ffn1_back_tokens(
        stream_grad, gb, stream0, norms, inner_one, first_w, order,
        [norm_sums_1, norm_sums_2, norm_sums_4], attn_pieces[1:2],
    )
    norm_rows = [norm_rows] + tensor_swaps(norm_rows)
    keep, send = ffn1_back_weights(
        gb_blocks, hidden, slope, normed_t, first_w, norm_rows, attn_cuts[1:2]
    )
    first_cuts = reduce_chips(reduce_core([(keep, core_other(send))], name="core_ffn1"))
    widths = [units, units, 2 * part, part]
    second_cuts = reduce_split(second_cuts, widths, after=[*gb_blocks[1:], attn_pieces[1]], name="split_second")
    second_sum = reduce_tensor(second_cuts)
    second_in_grad, second_out_grad, pair_grad, outs_grad = cut_columns(second_sum, widths)
    attn_cuts = reduce_split(attn_cuts, [part] * 5, name="split_attn")
    attn_sum = reduce_tensor(attn_cuts)
    query_grad, key_grad, value_grad, pos_grad, attn_grad = cut_columns(attn_sum[:shard], [part] * 5)
    taps_grad = jnp.concatenate([attn_sum[shard:, :part], attn_sum[shard:, part : 2 * part]], 0)
    bias_grad = attn_sum[shard : shard + 2, 2 * part : 3 * part]
    first_sum = first_cuts[0] + sum(p.astype(F32) for p in first_cuts[1:])
    first_in_grad, first_out_grad, norm_cols = cut_columns(first_sum, [units, units, LANES])
    norm_rows = norm_cols[:, :10].T

    block_out = dot(block_out, order, ((1,), (1,))).astype(BF)
    return (
        block_out[None],
        input_grad[None],
        norm_rows[0:5],
        norm_rows[5:10],
        first_in_grad,
        first_out_grad.T,
        query_grad,
        key_grad,
        value_grad,
        pos_grad,
        attn_grad.T,
        bias_grad,
        pair_grad[:, :part],
        pair_grad[:, part:],
        taps_grad[:ker],
        totals[1, :part],
        totals[0, :part],
        outs_grad.T,
        second_in_grad,
        second_out_grad.T,
    )


def solution(mesh):
    return jax.shard_map(
        on_device,
        mesh=mesh,
        in_specs=(
            P("dp", "tensor", None),
            P("dp"),
            P(),
            P("dp", "tensor", None),
            P(None, "dp"),
            P(None, "dp"),
            P("dp", "tensor"),
            P("tensor", "dp"),
            P("dp", "tensor"),
            P("dp", "tensor"),
            P("dp", "tensor"),
            P("dp", "tensor"),
            P("tensor", "dp"),
            P(None, "tensor"),
            P("dp", "tensor"),
            P("dp", "tensor"),
            P(None, "tensor"),
            P("tensor"),
            P("tensor"),
            P("tensor", "dp"),
            P("dp", "tensor"),
            P("tensor", "dp"),
        ),
        out_specs=(
            P("dp", "tensor", None),
            P("dp", "tensor", None),
            P(None, "dp"),
            P(None, "dp"),
            P("dp", "tensor"),
            P("tensor", "dp"),
            P("dp", "tensor"),
            P("dp", "tensor"),
            P("dp", "tensor"),
            P("dp", "tensor"),
            P("tensor", "dp"),
            P(None, "tensor"),
            P("dp", "tensor"),
            P("dp", "tensor"),
            P(None, "tensor"),
            P("tensor"),
            P("tensor"),
            P("tensor", "dp"),
            P("dp", "tensor"),
            P("tensor", "dp"),
        ),
        check_vma=False,
    )
```

```python
import math

import jax
import jax.numpy as jnp
from jax import lax
from jax.experimental import pallas as pl
from jax.experimental.pallas import tpu as pltpu
from jax.sharding import PartitionSpec as P

DH = 64
LANES = 128
HALO = 16
EPS = 1e-05
NEG = -1000000000.0
HIGHEST = lax.Precision.HIGHEST
BF = jnp.bfloat16
F32 = jnp.float32


def dot(left, right, dims=((1,), (0,)), **kw):
    return lax.dot_general(left, right, (dims, ((), ())), preferred_element_type=F32, **kw)


def dot_t(left, right):
    return dot(left, right, ((1,), (1,)))


def swap(values, axis, mask):
    return lax.ppermute(values, axis, [(i, i ^ mask) for i in range(lax.axis_size(axis))])


def dp_plan():
    size = lax.axis_size("dp")
    chips = [m for m in (0, 2, 4, 6) if m < size]
    doublings = [1] + [1 << b for b in range(3, 20) if 1 << b < size]
    return chips, doublings


def run(kernel, ins, outs, scratch=(), grid=(1,), aliases=None, after=(), micros=3, limit=8, name=None):
    count = len(ins)

    def body(*refs):
        kernel(*refs[:count], *refs[count + len(after) :])

    def whole(shape):
        return pl.BlockSpec(
            tuple(shape), lambda g: (0,) * len(shape), pipeline_mode=pl.Buffered(1)
        )

    def held(shape, dtype, spec):
        if spec is None:
            return math.prod(shape) * jnp.dtype(dtype).itemsize
        if spec.block_shape is None:
            return 0
        buffers = 1 if spec.pipeline_mode is not None else 2
        return buffers * math.prod(spec.block_shape) * jnp.dtype(dtype).itemsize

    need = sum(held(a.shape, a.dtype, spec) for a, spec in ins)
    need += sum(held(*out) for out in outs)
    need += sum(math.prod(r.shape) * jnp.dtype(r.dtype).itemsize for r in scratch)
    limit = need // 2**20 + 1 + limit
    return pl.pallas_call(
        body,
        grid=grid,
        in_specs=[spec or whole(a.shape) for a, spec in ins] + [ANY] * len(after),
        out_specs=[spec or whole(s) for s, _, spec in outs],
        out_shape=[jax.ShapeDtypeStruct(s, d) for s, d, _ in outs],
        scratch_shapes=list(scratch),
        input_output_aliases=aliases or {},
        compiler_params=pltpu.CompilerParams(vmem_limit_bytes=limit * 1024 * 1024),
        cost_estimate=pl.CostEstimate(
            flops=int(micros * 1e9), bytes_accessed=int(micros * 3.0e6), transcendentals=0
        ),
        name=name,
    )(*[a for a, _ in ins], *after)


SMEM = pl.BlockSpec(memory_space=pltpu.SMEM)
ANY = pl.BlockSpec(memory_space=pl.ANY)


def column(rows, offset=0):
    return pl.BlockSpec((rows, LANES), lambda g: (0, offset + g))


def heads(pairs, rows, span):
    return pl.BlockSpec((pairs, rows, span), lambda g: (g, 0, 0))


def regroup(blocks, widths, extras=(), after=(), name="regroup"):
    rows = blocks[0].shape[0]
    count, total = len(blocks), sum(widths)

    def kernel(*refs):
        out, at, start = refs[-1], 0, 0
        for width in widths:
            for b in range(count):
                out[:, at : at + width] = refs[b][:, start : start + width]
                at += width
            start += width
        for ref in refs[count:-1]:
            out[:, at : at + ref.shape[1]] = ref[...]
            at += ref.shape[1]

    columns = count * total + sum(e.shape[1] for e in extras)
    return run(
        kernel, [(b, None) for b in (*blocks, *extras)], [((rows, columns), BF, None)],
        after=after, micros=1, name=name,
    )[0]


def stack_rows(pieces, after=(), name="stack_rows"):
    if any(p.shape[0] % 16 for p in pieces):
        return jnp.concatenate(pieces, 0)
    total = sum(p.shape[0] for p in pieces)

    def kernel(*refs):
        at = 0
        for ref in refs[:-1]:
            refs[-1][at : at + ref.shape[0], :] = ref[...]
            at += ref.shape[0]

    return run(
        kernel, [(p, None) for p in pieces], [((total, pieces[0].shape[1]), BF, None)],
        after=after, micros=1.5, name=name,
    )[0]


def tensor_swaps(block):
    return [swap(block, "tensor", m) for m in range(1, lax.axis_size("tensor"))]


def chip_swaps(block):
    chips, _ = dp_plan()
    return [swap(block, "dp", m) for m in chips[1:]]


def plane_swaps(block):
    half = block.shape[0] // 2
    by_x, by_y = swap(block, "dp", 2), swap(block, "dp", 4)
    return [by_x, by_y, swap(by_x[:half], "dp", 4), swap(by_y[half:], "dp", 2)]


def core_swap(pieces, after=(), name="stack_rows"):
    _, doublings = dp_plan()
    rows = stack_rows(pieces, after, name)
    for step in doublings[:-1]:
        rows = jnp.concatenate([rows, swap(rows, "dp", step)], 0)
    return rows, swap(rows, "dp", doublings[-1])


def core_other(send):
    _, doublings = dp_plan()
    return swap(send, "dp", doublings[-1])


def reduce_rest(keep, other, extra):
    _, doublings = dp_plan()
    for step in doublings[-2::-1]:
        both = (keep.astype(F32) + other.astype(F32)).astype(BF)
        main, tail = both[: both.shape[0] - extra], both[both.shape[0] - extra :]
        half = main.shape[0] // 2
        keep = jnp.concatenate([main[:half], tail], 0)
        other = swap(jnp.concatenate([main[half:], tail], 0), "dp", step)
    return keep, other


def reduce_core(arrays, sources, rows, columns, extra=0, name="reduce_core"):
    half = rows // 2

    def pieces(refs):
        for i, parts in enumerate(sources):
            for kept, received, row, at in parts:
                a, b = refs[kept], refs[received]
                value = a[row : row + rows, :].astype(F32) + b[row : row + rows, :].astype(F32)
                tail = None
                if extra:
                    kept, received, row, _ = sources[0][0]
                    a, b = refs[kept], refs[received]
                    first = a.shape[0] - extra
                    tail = a[first:, :].astype(F32) + b[first:, :].astype(F32)
                yield i, slice(at, at + value.shape[1]), value, tail

    shapes = [(rows + extra, F32), (rows, BF), (rows + extra, BF), (half + extra, BF), (half, BF)]
    if rows % 32:
        outs = [[] for _ in shapes]
        for i, _, value, tail in pieces(arrays):
            under = (lambda v: jnp.concatenate([v, tail], 0)) if extra else (lambda v: v)
            for out, part in {
                0: [(0, under(value))],
                1: [(1, value)],
                2: [(2, under(value))],
                3: [(3, under(value[:half])), (4, value[half:])],
            }[i]:
                outs[out].append(part)
        return [jnp.concatenate(o, 1).astype(d) for o, (_, d) in zip(outs, shapes)]

    def kernel(*refs):
        outs = refs[len(arrays) :]
        for i, cols, value, tail in pieces(refs):
            if i == 3:
                outs[3][:half, cols] = value[:half].astype(BF)
                outs[4][:, cols] = value[half:].astype(BF)
            else:
                outs[i][:rows, cols] = value.astype(outs[i].dtype)
            if extra and i in (0, 2):
                outs[i][rows:, cols] = tail.astype(outs[i].dtype)
            if extra and i == 3:
                outs[3][half:, cols] = tail.astype(BF)

    return run(
        kernel, [(x, None) for x in arrays], [((r, columns), d, None) for r, d in shapes],
        micros=2.5, name=name,
    )


def reduce_core_pairs(pairs, name):
    if len(dp_plan()[1]) > 1:
        pairs = [reduce_rest(*[jnp.concatenate(x, 1) for x in zip(*pairs)], 0)]
    rows = pairs[0][0].shape[0] // 4
    starts = [sum(p[0].shape[1] for p in pairs[:n]) for n in range(len(pairs))]
    sources = [
        [(2 * n, 2 * n + 1, i * rows, at) for n, at in enumerate(starts)] for i in range(4)
    ]
    columns = sum(p[0].shape[1] for p in pairs)
    return reduce_core([x for p in pairs for x in p], sources, rows, columns, name=name)


def reduce_core_pieces(keeps, sends, extra, name):
    if len(dp_plan()[1]) > 1:
        keep, send = [
            jnp.concatenate([p[: p.shape[0] - (0 if i else extra)] for i, p in enumerate(x)] + [x[0][-extra:]], 0)
            for x in (keeps, sends)
        ]
        keep, other = reduce_rest(keep, core_other(send), extra)
        rows = (keep.shape[0] - extra) // 4
        sources = [[(0, 1, i * rows, 0)] for i in range(4)]
        return reduce_core([keep, other], sources, rows, keep.shape[1], extra, name)
    rows, columns = keeps[1].shape
    sources = [[(i, 4 + i, 0, 0)] for i in range(4)]
    return reduce_core(
        [*keeps, *[core_other(x) for x in sends]], sources, rows, columns, extra, name
    )


def plane_first(parts):
    return swap(parts[3], "dp", 2), swap(parts[4], "dp", 4)


def plane_second(parts, came, after=(), name="plane_second"):
    own, x, y, _, _ = parts
    rows, extra, columns = x.shape[0], own.shape[0] - x.shape[0], x.shape[1]
    half = rows // 2

    def added(x, y, by_x, by_y):
        low = x[half:, :].astype(F32) + by_y[...].astype(F32)
        top = y[:half, :].astype(F32) + by_x[:half, :].astype(F32)
        tail = y[rows:, :].astype(F32) + by_x[half:, :].astype(F32) if extra else None
        return low.astype(BF), top.astype(BF), tail

    if rows % 32:
        low, top, tail = added(x, y, *came)
        x = jnp.concatenate([x[:half], low], 0)
        y = jnp.concatenate([top, y[half:rows]] + ([tail.astype(BF)] if extra else []), 0)
    else:

        def kernel(x_ref, y_ref, by_x_ref, by_y_ref, x_out, y_out):
            low, top, tail = added(x_ref, y_ref, by_x_ref, by_y_ref)
            x_out[:half, :] = x_ref[:half, :]
            x_out[half:, :] = low
            y_out[:half, :] = top
            y_out[half:rows, :] = y_ref[half:rows, :]
            if extra:
                y_out[rows:, :] = tail.astype(BF)

        x, y = run(
            kernel, [(v, None) for v in (x, y, *came)],
            [((rows, columns), BF, None), ((rows + extra, columns), BF, None)],
            after=after, micros=1.5, name=name,
        )
    return [own, swap(y, "dp", 4), swap(x, "dp", 2), came[0], x]


def reduce_split(parts, widths, shared=None, after=(), name="reduce_split"):
    size = lax.axis_size("tensor")
    rows, extra = parts[2].shape[0], parts[0].shape[0] - parts[2].shape[0]
    half = rows // 2

    def kernel(own_ref, y_ref, x_ref, came_ref, *refs):
        totals = [own_ref[:rows, :] + x_ref[...].astype(F32) + y_ref[:rows, :].astype(F32)]
        if extra:
            tail = own_ref[rows:, :] + y_ref[rows:, :].astype(F32)
            totals.append(tail + came_ref[half:, :].astype(F32))
        for mask in range(size):
            out = refs[mask - size]
            for total, first in zip(totals, (0, rows)):
                at, start, under = 0, 0, slice(first, first + total.shape[0])
                for width in widths:
                    cut = total[:, start + mask * width : start + (mask + 1) * width]
                    out[under, at : at + width] = cut.astype(out.dtype)
                    at += width
                    start += size * width
            if shared is not None:
                out[:rows, at:] = refs[0][...].astype(out.dtype)
                out[rows:, at:] = jnp.zeros((extra, LANES), out.dtype)

    more = [] if shared is None else [shared]
    return run(
        kernel, [(p, None) for p in (*parts, *more)],
        [((rows + extra, sum(widths) + LANES * len(more)), F32 if m == 0 else BF, None) for m in range(size)],
        after=after, micros=1.5, name=name,
    )


def cut_columns(total, widths):
    parts, at = [], 0
    for width in widths:
        parts.append(total[:, at : at + width])
        at += width
    return parts


def reduce_tensor(cuts):
    total = cuts[0]
    for mask in range(1, len(cuts)):
        total = total + swap(cuts[mask], "tensor", mask).astype(F32)
    return total


def block_swap(values, mask):
    width = values.shape[1] // 4
    return jnp.concatenate(
        [values[:, (b ^ mask) * width : ((b ^ mask) + 1) * width] for b in range(4)], 1
    )


def edges_of(me, last, first):
    even = (me & 1) == 0
    return jnp.where(even, last, first), jnp.where(even, first, last)


def edges_from(me, by_1, by_3):
    even = (me & 1) == 0
    return jnp.where(even, by_3, by_1), jnp.where(even, by_1, by_3)


def sum_tensor(place, own, packs, name):
    by_1, by_2, by_3 = [swap(p, "tensor", m) for m, p in enumerate(packs, 1)]
    columns = own.shape[1]

    def kernel(place_ref, own_ref, one_ref, two_ref, three_ref, sums_ref, before_ref, after_ref):
        one, three = block_swap(one_ref[...], 1), block_swap(three_ref[...], 3)
        sums_ref[...] = own_ref[...] + one[:8] + block_swap(two_ref[...], 2) + three[:8]
        before_ref[...], after_ref[...] = edges_from(place_ref[0], one[8:], three[8:])

    return run(
        kernel, [(place, SMEM), (own, None), (by_1, None), (by_2, None), (by_3, None)],
        [((8, columns), F32, None)] + [((HALO, columns), F32, None)] * 2,
        micros=1, name=name,
    )


def sum_dp(total):
    _, doublings = dp_plan()
    for step in doublings:
        total = total + swap(total, "dp", step)
    return [total] + chip_swaps(total)


def norm(stream, gain, beta_row):
    centered = stream - jnp.mean(stream, -1, keepdims=True)
    inv_std = lax.rsqrt(jnp.mean(centered * centered, -1, keepdims=True) + EPS)
    scaled = centered * inv_std
    return scaled * gain + beta_row, scaled, inv_std


def norm_back(upstream, stream, gain):
    centered = stream - jnp.mean(stream, -1, keepdims=True)
    inv_std = lax.rsqrt(jnp.mean(centered * centered, -1, keepdims=True) + EPS)
    scaled = centered * inv_std
    grad = upstream * gain
    out = inv_std * (
        grad - jnp.mean(grad, -1, keepdims=True) - scaled * jnp.mean(grad * scaled, -1, keepdims=True)
    )
    return out, jnp.sum(upstream * scaled, 0, keepdims=True), jnp.sum(upstream, 0, keepdims=True)


def swish_slope(inner_act):
    logistic = jax.nn.sigmoid(inner_act)
    return logistic * (1.0 + inner_act * (1.0 - logistic))


def lanes_of(h, rows):
    lane = lax.broadcasted_iota(jnp.int32, (rows, LANES), 1)
    return (lane >= h * DH) & (lane < (h + 1) * DH)


def both(a_ref, b_ref):
    return jnp.concatenate([a_ref[...], b_ref[...]], 0)


def ordered_rows(me, block, rows):
    return pl.ds(pl.multiple_of((me ^ block) * rows, 64), rows)


def channel_sums(rows, count=8):
    return jnp.concatenate(rows + [jnp.zeros((count - len(rows), rows[0].shape[1]), F32)], 0)


def first_norm(stream, columns):
    rows, width = stream.shape
    half = width // 2

    def kernel(stream_ref, a_ref, b_ref, norms_ref, normed_ref):
        for ref, at in ((a_ref, 0), (b_ref, half)):
            norms_ref[:, at : at + half] = ref[...].astype(F32).T[:16]
        normed = norm(stream_ref[...], norms_ref[0:1, :], norms_ref[5:6, :])[0]
        normed_ref[...] = normed.astype(BF)

    return run(
        kernel, [(stream, None), (columns[0], None), (columns[1], None)],
        [((16, width), F32, None), ((rows, width), BF, None)], micros=1, name="first_norm",
    )


def ffn1_forward(stream, normed, halves, norms, after):
    rows, width = stream.shape
    half = width // 2
    hidden_units = halves[0].shape[1] // 2

    def kernel(stream_ref, normed_ref, a_ref, b_ref, norms_ref, inner_ref, out_ref, next_ref):
        normed = normed_ref[...]
        low = jnp.zeros((rows, half), F32)
        high = jnp.zeros((rows, half), F32)
        for j in range(0, hidden_units, 512):
            at = slice(j, j + 512)
            after = slice(hidden_units + j, hidden_units + j + 512)
            inner = dot(normed[:, :half], a_ref[:, at]) + dot(normed[:, half:], b_ref[:, at])
            inner_ref[:, at] = inner
            hidden = jax.nn.silu(inner).astype(BF)
            low = low + dot_t(hidden, a_ref[:, after])
            high = high + dot_t(hidden, b_ref[:, after])
        out = stream_ref[...] + 0.5 * jnp.concatenate([low, high], 1)
        out_ref[...] = out
        next_ref[...] = norm(out, norms_ref[1:2, :], norms_ref[6:7, :])[0].astype(BF)

    return run(
        kernel, [(x, None) for x in (stream, normed, *halves, norms)],
        [((rows, hidden_units), F32, None), ((rows, width), F32, None), ((rows, width), BF, None)],
        after=after, micros=4, name="ffn1_forward",
    )


def ffn1_hidden(place, blocks, halves, units, after):
    rows, width = blocks[0].shape
    half, count = width // 2, len(blocks)
    span = count * rows

    def kernel(place_ref, a_ref, b_ref, *refs):
        hidden_ref, slope_ref, normed_t_ref, ordered = refs[count:]
        for b in range(count):
            normed = refs[b][...]
            at = ordered_rows(place_ref[0], b, rows)
            inner = dot(normed[:, :half], a_ref[...]) + dot(normed[:, half:], b_ref[...])
            logistic = jax.nn.sigmoid(inner)
            hidden_ref[at, :] = (inner * logistic).astype(BF)
            slope_ref[at, :] = logistic * (1.0 + inner * (1.0 - logistic))
            ordered[at, :] = normed
        normed_t_ref[...] = ordered[...].T

    own = pl.BlockSpec((half, units), lambda g: (0, 0), pipeline_mode=pl.Buffered(1))
    return run(
        kernel, [(place, SMEM)] + [(x, own) for x in halves] + [(x, None) for x in blocks],
        [((span, units), BF, None), ((span, units), F32, None), ((width, span), BF, None)],
        scratch=[pltpu.VMEM((span, width), BF)], after=after, micros=2, name="ffn1_hidden",
    )


def sum_parts(parts, name):
    def kernel(*refs):
        refs[-1][...] = sum(r[...].astype(F32) for r in refs[:-1])

    return run(kernel, [(p, None) for p in parts], [(parts[0].shape, F32, None)], micros=6, name=name)[0]


def ffn1_branch_grad(upstream, stream_grad, stream, norms, after):
    rows, width = stream.shape

    def kernel(upstream_ref, grad_ref, stream_ref, norms_ref, out_ref, gb_ref, sums_ref):
        extra, dgain, dbeta = norm_back(upstream_ref[...], stream_ref[...], norms_ref[1:2, :])
        sums_ref[...] = channel_sums([dgain, dbeta])
        out = grad_ref[...] + extra
        out_ref[...] = out
        gb_ref[...] = (0.5 * out).astype(BF)

    return run(
        kernel, [(x, None) for x in (upstream, stream_grad, stream, norms)],
        [((rows, width), F32, None), ((rows, width), BF, None), ((8, width), F32, None)],
        after=after, micros=1.5, name="ffn1_branch_grad",
    )


def ffn1_back_tokens(stream_grad, gb, stream, norms, inner, halves, order, sums, after):
    rows, width = stream.shape
    hidden_units = inner.shape[1]
    half = width // 2

    def kernel(grad_ref, gb_ref, stream_ref, norms_ref, inner_ref, a_ref, b_ref, order_ref, s1_ref, s2_ref, s4_ref,
               out_ref, norm_rows_ref, gb_out_ref):
        gb = gb_ref[...]
        gb_out_ref[...] = gb
        low = jnp.zeros((rows, half), F32)
        high = jnp.zeros((rows, half), F32)
        for j in range(0, hidden_units, 512):
            at = slice(j, j + 512)
            after = slice(hidden_units + j, hidden_units + j + 512)
            grad = dot(gb[:, :half], a_ref[:, after]) + dot(gb[:, half:], b_ref[:, after])
            grad = (grad * swish_slope(inner_ref[:, at])).astype(BF)
            low = low + dot_t(grad, a_ref[:, at])
            high = high + dot_t(grad, b_ref[:, at])
        extra, dgain, dbeta = norm_back(
            jnp.concatenate([low, high], 1), stream_ref[...], norms_ref[0:1, :]
        )
        gains = [dgain, s1_ref[0:1, :], s2_ref[0:1, :], s4_ref[0:1, :], s4_ref[2:3, :]]
        betas = [dbeta, s1_ref[1:2, :], s2_ref[1:2, :], s4_ref[1:2, :], s4_ref[3:4, :]]
        norm_rows_ref[...] = channel_sums(gains + betas, 16)
        out_ref[...] = dot(
            grad_ref[...] + extra, order_ref[...].astype(F32), ((1,), (1,)), precision=HIGHEST
        )

    ins = [stream_grad, gb, stream, norms, inner, *halves, order, *sums]
    return run(
        kernel, [(x, None) for x in ins],
        [((rows, width), F32, None), ((16, width), F32, None), ((rows, width), BF, None)],
        after=after, micros=5, name="ffn1_back_tokens",
    )


def ffn1_back_weights(gb, hidden, slope, normed_t, halves, norm_rows, after):
    width, span = normed_t.shape
    units, half = hidden.shape[1], width // 2

    def kernel(gb_ref, hidden_ref, slope_ref, normed_t_ref, a_ref, b_ref, norm_ref, keep_ref, send_ref):
        gb = gb_ref[...]
        grad = dot(gb[:, :half], a_ref[...]) + dot(gb[:, half:], b_ref[...])
        grad = (grad * slope_ref[...]).astype(BF)
        columns = jnp.concatenate([norm_ref[...], jnp.zeros((LANES - 16, width), F32)], 0).T
        grads = [dot(normed_t_ref[...], grad), dot(gb.T, hidden_ref[...]), columns]
        at = 0
        for g in grads:
            keep_ref[:, at : at + g.shape[1]] = g[:half].astype(BF)
            send_ref[:, at : at + g.shape[1]] = g[half:].astype(BF)
            at += g.shape[1]

    first = halves[0].shape[1] // (2 * units)
    own = pl.BlockSpec((half, units), lambda g: (0, first), pipeline_mode=pl.Buffered(1))
    total = 2 * units + LANES
    return run(
        kernel,
        [(gb, None), (hidden, None), (slope, None), (normed_t, None), (halves[0], own), (halves[1], own), (norm_rows, None)],
        [((half, total), BF, None), ((half, total), BF, None)],
        after=after, micros=4, name="ffn1_back_weights",
    )


def attn_queries(normed, halves, rel_rows, small, span, bias_row, after):
    rows, width = normed.shape
    wide, columns = rel_rows.shape[0], small.shape[1]
    groups, pairs = columns // LANES, LANES // DH
    half = width // 2

    def kernel(rows_ref, aq_ref, bq_ref, ap_ref, bp_ref, rel_ref, small_ref, qu_ref, qv_ref, pos_ref, table_ref):
        queries = dot(rows_ref[...], both(aq_ref, bq_ref))
        bias = small_ref[...].astype(F32)
        qu_ref[...] = (queries + bias[bias_row : bias_row + 1]).astype(BF)
        query_v = (queries + bias[bias_row + 1 : bias_row + 2]).astype(BF)
        qv_ref[...] = query_v
        positions = dot(rel_ref[...], both(ap_ref, bp_ref)).astype(BF)
        pos_ref[...] = positions
        for h in range(pairs):
            mine = jnp.where(lanes_of(h, rows), query_v, jnp.zeros_like(query_v))
            table = dot_t(mine, positions)
            shifted = pltpu.roll(table, wide - (rows - 1), 1, stride=1, stride_axis=0)
            table_ref[h] = shifted[:, :span]

    def weight(i):
        return column(half, i * groups)

    a, b = halves
    return run(
        kernel,
        [(normed, None), (a, weight(0)), (b, weight(0)), (a, weight(3)), (b, weight(3)), (rel_rows, None), (small, column(small.shape[0]))],
        [((rows, columns), BF, column(rows)), ((rows, columns), BF, column(rows)), ((wide, columns), BF, column(wide)),
         ((groups * pairs, rows, span), F32, heads(pairs, rows, span))],
        grid=(groups,), after=after, micros=0.5, name="attn_queries",
    )


def attn_main(place, tokens, halves, query_u, table, stream, norms, after):
    rows, width = stream.shape
    span, columns = table.shape[2], query_u.shape[1]
    groups, pairs = columns // LANES, LANES // DH
    half = width // 2

    def kernel(place_ref, rows_ref, *refs):
        (ak_ref, bk_ref, av_ref, bv_ref, ao_ref, bo_ref, qu_ref, table_ref, stream_ref, norms_ref,
         mixed_ref, probs_ref, keys_ref, vals_ref, out_ref, normed_ref, edge_1_ref, edge_3_ref) = refs
        me, length = place_ref[0], place_ref[1]
        keys = dot(rows_ref[...], both(ak_ref, bk_ref)).astype(BF)
        vals = dot(rows_ref[...], both(av_ref, bv_ref)).astype(BF)
        keys_ref[...], vals_ref[...], query_u = keys, vals, qu_ref[...]
        visible = lax.broadcasted_iota(jnp.int32, (rows, span), 1) < length
        mixed = jnp.zeros((rows, LANES), F32)
        for h in range(pairs):
            mine = lanes_of(h, rows)
            content = dot_t(jnp.where(mine, query_u, jnp.zeros_like(query_u)), keys)
            scores = jnp.where(visible, (content + table_ref[h]) * DH ** (-0.5), NEG)
            exponent = jnp.exp(scores - jnp.max(scores, -1, keepdims=True))
            probs = exponent / jnp.sum(exponent, -1, keepdims=True)
            probs_ref[h] = probs
            mixed = jnp.where(mine, dot(probs.astype(BF), vals), mixed)
        mixed = mixed.astype(BF)
        mixed_ref[...] = mixed

        @pl.when(pl.program_id(0) == 0)
        def _():
            out_ref[...] = stream_ref[...]

        out_ref[...] += dot_t(mixed, both(ao_ref, bo_ref))

        @pl.when(pl.program_id(0) == groups - 1)
        def _():
            normed = norm(out_ref[...], norms_ref[2:3, :], norms_ref[7:8, :])[0].astype(BF)
            normed_ref[...] = normed
            edge_1_ref[...], edge_3_ref[...] = edges_of(me, normed[rows - HALO :], normed[:HALO])

    def weight(i):
        return column(half, i * groups)

    a, b = halves
    return run(
        kernel,
        [(place, SMEM), (tokens, None)] + [(w, weight(i)) for i in (1, 2, 4) for w in (a, b)]
        + [(query_u, column(rows)), (table, heads(pairs, rows, span)), (stream, None), (norms, None)],
        [((rows, columns), BF, column(rows)), ((groups * pairs, rows, span), F32, heads(pairs, rows, span)),
         ((span, columns), BF, column(span)), ((span, columns), BF, column(span)),
         ((rows, width), F32, None), ((rows, width), BF, None), ((HALO, width), BF, None), ((HALO, width), BF, None)],
        grid=(groups,), after=after, micros=0.2, name="attn_main",
    )


def attn_back_keys(place, gb, halves, probs, keys, vals, query_u, count, after):
    rows, width = gb.shape
    span, columns = keys.shape
    groups, pairs = columns // LANES, LANES // DH
    half = width // 2

    def kernel(place_ref, gb_ref, ao_ref, bo_ref, ak_ref, bk_ref, av_ref, bv_ref, probs_ref, keys_ref, vals_ref, qu_ref,
               gp_ref, dk_ref, dv_ref, own_ref, *refs):
        other_refs, total = refs[:-1], refs[-1]
        me = place_ref[0]
        step = pl.program_id(0)
        gm = dot(gb_ref[...], both(ao_ref, bo_ref)).astype(BF)
        gm_t, qu_t = gm.T, qu_ref[...].T
        vals = vals_ref[...]
        dk_t, dv_t = [], []
        for h in range(pairs):
            head = slice(h * DH, (h + 1) * DH)
            probs = probs_ref[h]
            dprobs = dot_t(jnp.where(lanes_of(h, rows), gm, jnp.zeros_like(gm)), vals)
            delta = jnp.sum(dprobs * probs, -1, keepdims=True)
            gp = ((DH ** (-0.5) * probs) * (dprobs - delta)).astype(BF)
            gp_ref[h] = gp
            dv_t.append(dot(gm_t[head], probs.astype(BF)))
            dk_t.append(dot(qu_t[head], gp))
        dk = jnp.concatenate(dk_t, 0).T.astype(BF)
        dv = jnp.concatenate(dv_t, 0).T.astype(BF)
        dk_ref[...] = dk
        dv_ref[...] = dv
        grad = dot_t(dk, both(ak_ref, bk_ref)) + dot_t(dv, both(av_ref, bv_ref))

        @pl.when(step == 0)
        def _():
            total[...] = grad

        @pl.when(step > 0)
        def _():
            total[...] += grad

        @pl.when(step == groups - 1)
        def _():
            own_ref[...] = total[ordered_rows(me, 0, rows), :]
            for b in range(1, count):
                other_refs[b - 1][...] = total[ordered_rows(me, b, rows), :].astype(BF)

    def weight(i):
        return column(half, i * groups)

    a, b = halves
    return run(
        kernel,
        [(place, SMEM), (gb, None)] + [(w, weight(i)) for i in (4, 1, 2) for w in (a, b)]
        + [(probs, heads(pairs, rows, span)), (keys, column(span)), (vals, column(span)), (query_u, column(rows))],
        [((groups * pairs, rows, span), BF, heads(pairs, rows, span)), ((span, columns), BF, column(span)), ((span, columns), BF, column(span)),
         ((rows, width), F32, None)] + [((rows, width), BF, None)] * (count - 1),
        scratch=[pltpu.VMEM((span, width), F32)],
        grid=(groups,), after=after, micros=11, name="attn_back_keys",
    )


def attn_back_queries(gp, keys, positions, query_v, dk, dv, mixed, gb, normed, tokens, rel_rows, halves, taps_grad, after):
    rows, width = gb.shape
    span, columns = keys.shape
    wide = rel_rows.shape[0]
    groups, pairs = columns // LANES, LANES // DH
    half, pieces = width // 2, 4
    size = half // pieces

    def kernel(gp_ref, keys_ref, pos_ref, qv_ref, dk_ref, dv_ref, mixed_ref, aq_ref, bq_ref, gb_ref, rel_ref, dtaps_ref, normed_ref, tokens_ref, *refs):
        piece_refs, (own_ref, normed_t, tokens_t, rel_t, gb_t) = refs[: 2 * pieces], refs[2 * pieces :]
        step = pl.program_id(0)

        @pl.when(step == 0)
        def _():
            normed_t[...] = normed_ref[...].T
            tokens_t[...] = tokens_ref[...].T
            rel_t[...] = rel_ref[...].T
            gb_t[...] = gb_ref[...].T
            own_ref[...] = jnp.zeros_like(own_ref)

        i = lax.broadcasted_iota(jnp.int32, (rows, rows), 0)
        j = lax.broadcasted_iota(jnp.int32, (rows, rows), 1)
        flip = jnp.where(i + j == rows - 1, 1.0, 0.0)
        flip_low = flip.astype(BF)
        keys, positions = keys_ref[...], pos_ref[...]
        qv_t = dot(flip_low, qv_ref[...]).astype(BF).T
        du = jnp.zeros((rows, LANES), F32)
        dv_rows = jnp.zeros((rows, LANES), F32)
        dp_t = []
        for h in range(pairs):
            mine = lanes_of(h, rows)
            gp = gp_ref[h]
            du = jnp.where(mine, dot(gp, keys), du)
            flipped = dot(flip_low, gp)
            table = jnp.concatenate([flipped, jnp.zeros((rows, wide - span), F32)], 1)
            table = pltpu.roll(table, 0, 1, stride=1, stride_axis=0).astype(BF)
            dp_t.append(dot(qv_t[h * DH : (h + 1) * DH], table))
            dv_rows = jnp.where(mine, dot(table, positions), dv_rows)
        dv_rows = dot(flip, dv_rows, precision=HIGHEST)
        bias = channel_sums(
            [jnp.sum(du, 0, keepdims=True), jnp.sum(dv_rows, 0, keepdims=True)], 16
        )
        nothing = jnp.zeros((16, LANES), F32)
        extras = [dtaps_ref[:16, :], dtaps_ref[16:, :], bias, nothing, nothing]
        dq = (du + dv_rows).astype(BF)
        dp = jnp.concatenate(dp_t, 0).T.astype(BF)
        own_ref[...] += dot_t(dq, both(aq_ref, bq_ref))
        grads = [
            dot(normed_t[...], dq),
            dot(tokens_t[...], dk_ref[...]),
            dot(tokens_t[...], dv_ref[...]),
            dot(rel_t[...], dp),
            dot(gb_t[...], mixed_ref[...]),
        ]
        for n, grad in enumerate(grads):
            at = pl.ds(pl.multiple_of((n * groups + step) * LANES, LANES), LANES)
            low = grad.astype(BF)
            for i, ref in enumerate(piece_refs):
                ref[:size, at] = low[i * size : (i + 1) * size]
                if i % pieces == 0:
                    ref[size:, at] = extras[n].astype(BF)

    a, b = halves
    outs = run(
        kernel,
        [(gp, heads(pairs, rows, span)), (keys, column(span)), (positions, column(wide)), (query_v, column(rows)),
         (dk, column(span)), (dv, column(span)), (mixed, column(rows)), (a, column(half)), (b, column(half)), (gb, None), (rel_rows, None), (taps_grad, column(32)),
         (normed, None), (tokens, None)],
        [((size + (0 if i % pieces else 16), 5 * columns), BF, None) for i in range(2 * pieces)] + [((rows, width), F32, None)],
        scratch=[pltpu.VMEM((width, rows), BF), pltpu.VMEM((width, span), BF), pltpu.VMEM((width, wide), BF), pltpu.VMEM((width, rows), BF)],
        grid=(groups,), after=after, micros=13, name="attn_back_queries",
    )
    return outs[:pieces], outs[pieces : 2 * pieces], outs[-1]


def joined(a_ref, b_ref, at):
    return jnp.concatenate([a_ref[:, at], b_ref[:, at]], 0)


def conv_forward(place, normed, by_1, by_3, halves, at, small, ker):
    rows, width = normed.shape
    columns = small.shape[1]
    groups, half, ext = columns // LANES, width // 2, rows + 2 * HALO

    def kernel(place_ref, rows_ref, one_ref, three_ref, av_ref, bv_ref, ag_ref, bg_ref, small_ref,
               gated_ref, value_ref, gate_ref, depth_ref, sums_ref, pack_1_ref, pack_3_ref):
        me, length, start = place_ref[0], place_ref[1], place_ref[2]
        before, after = edges_from(me, one_ref[...], three_ref[...])
        tokens = jnp.concatenate([before, rows_ref[...], after], 0)
        value_half = dot(tokens, both(av_ref, bv_ref))
        logistic = jax.nn.sigmoid(dot(tokens, both(ag_ref, bg_ref)))
        token = start - HALO + lax.broadcasted_iota(jnp.int32, value_half.shape, 0)
        mask = jnp.where((token >= 0) & (token < length), 1.0, 0.0)
        gated_ref[...] = mask * value_half * logistic
        value_ref[...] = value_half[HALO : HALO + rows]
        gate_ref[...] = logistic[HALO : HALO + rows]
        taps = small_ref[...].astype(F32)
        depth = jnp.zeros((rows, LANES), F32)
        for k in range(ker):
            depth = depth + taps[k : k + 1, :] * gated_ref[k + 1 : k + 1 + rows, :]
        depth_ref[...] = depth
        mask = mask[HALO : HALO + rows]
        masked = depth * mask
        sums = channel_sums([jnp.sum(x, 0, keepdims=True) for x in (masked, masked * depth, mask)])
        sums_ref[...] = sums
        one, three = edges_of(me, depth[rows - HALO :], depth[:HALO])
        pack_1_ref[:8, :], pack_1_ref[8:, :] = sums, one
        pack_3_ref[:8, :], pack_3_ref[8:, :] = sums, three

    return run(
        kernel,
        [(place, SMEM), (normed, None), (by_1, None), (by_3, None)]
        + [(w, column(half, at + i * groups)) for i in (0, 1) for w in halves] + [(small, column(small.shape[0]))],
        [((ext, columns), F32, column(ext))] + [((rows, columns), F32, column(rows))] * 3
        + [((8, columns), F32, column(8))] + [((8 + HALO, columns), F32, column(8 + HALO))] * 2,
        grid=(groups,), micros=4, name="conv_forward",
    )


def batch_terms(sums_ref):
    count = sums_ref[2:3, :]
    mean = sums_ref[0:1, :] / count
    inv_std = lax.rsqrt(sums_ref[1:2, :] / count - mean * mean + EPS)
    return count, mean, inv_std


def turn(place, stream, depth, sums, norms, small, ker, halves, cotangent):
    rows, width = stream.shape
    columns = depth.shape[1]
    groups = columns // LANES
    half = width // 2
    total = halves[0].shape[1]
    hidden_units = (total - 3 * columns) // 2
    units = hidden_units // groups
    parts = len(sums)

    def kernel(place_ref, stream_ref, depth_ref, norms_ref, small_ref, ac_ref, bc_ref, ai_ref, bi_ref, ao_ref, bo_ref, cot_ref, *refs):
        (sums_ref, out_ref, keep_ref, send_ref, ckeep_ref, csend_ref, grad_ref, ngrad_ref, own_ref, pack_1_ref, pack_3_ref, nsums_ref,
         inner_ref, hidden_ref) = refs[parts:]
        sums_ref[...] = sum(r[...] for r in refs[:parts])
        _, mean, inv_std = batch_terms(sums_ref)
        batch_gain = small_ref[...].astype(F32)[ker + 2 : ker + 3]
        batch_bias = small_ref[...].astype(F32)[ker + 3 : ker + 4]
        scaled = (depth_ref[...] - mean) * inv_std
        normal = scaled * batch_gain + batch_bias
        active = jax.nn.silu(normal).astype(BF)
        wc = both(ac_ref, bc_ref)
        stream3 = stream_ref[...] + dot_t(active, wc)
        normed = norm(stream3, norms_ref[3:4, :], norms_ref[8:9, :])[0].astype(BF)
        branch = jnp.zeros((rows, width), F32)
        for p in range(groups):
            j = slice(p * units, (p + 1) * units)
            inner = dot(normed, joined(ai_ref, bi_ref, j))
            inner_ref[:, j] = inner
            hidden = jax.nn.silu(inner).astype(BF)
            hidden_ref[:, j] = hidden
            branch = branch + dot_t(hidden, joined(ao_ref, bo_ref, j))
        stream4 = stream3 + 0.5 * branch
        out_ref[...] = norm(stream4, norms_ref[4:5, :], norms_ref[9:10, :])[0].astype(BF)
        grad, gain5, beta5 = norm_back(cot_ref[...], stream4, norms_ref[4:5, :])
        gb = (0.5 * grad).astype(BF)
        gb_t, normed_t = gb.T, normed.T
        upstream = jnp.zeros((rows, width), F32)
        for p in range(groups):
            j = slice(p * units, (p + 1) * units)
            after = slice(hidden_units + p * units, hidden_units + (p + 1) * units)
            inner_grad = dot(gb, joined(ao_ref, bo_ref, j))
            inner_grad = (inner_grad * swish_slope(inner_ref[:, j])).astype(BF)
            in_grad = dot(normed_t, inner_grad)
            keep_ref[:, j] = in_grad[:half].astype(BF)
            send_ref[:, j] = in_grad[half:].astype(BF)
            out_grad = dot(gb_t, hidden_ref[:, j])
            keep_ref[:, after] = out_grad[:half].astype(BF)
            send_ref[:, after] = out_grad[half:].astype(BF)
            upstream = upstream + dot_t(inner_grad, joined(ai_ref, bi_ref, j))
        extra, gain4, beta4 = norm_back(upstream, stream3, norms_ref[3:4, :])
        nsums_ref[...] = channel_sums([gain4, beta4, gain5, beta5])
        grad = grad + extra
        grad_ref[...] = grad
        gb = grad.astype(BF)
        weight_grad = dot(gb.T, active)
        ckeep_ref[...] = weight_grad[:half].astype(BF)
        csend_ref[...] = weight_grad[half:].astype(BF)
        ngrad = dot(gb, wc) * swish_slope(normal)
        ngrad_ref[...] = ngrad
        own = channel_sums([jnp.sum(ngrad, 0, keepdims=True), jnp.sum(ngrad * scaled, 0, keepdims=True)])
        own_ref[...] = own
        one, three = edges_of(place_ref[0], ngrad[rows - HALO :], ngrad[:HALO])
        pack_1_ref[:8, :], pack_1_ref[8:, :] = own, one
        pack_3_ref[:8, :], pack_3_ref[8:, :] = own, three

    def block(columns, index):
        return pl.BlockSpec((half, columns), lambda g: (0, index), pipeline_mode=pl.Buffered(1))

    specs = [block(columns, (total - columns) // columns), block(hidden_units, 0), block(hidden_units, 1)]
    return run(
        kernel,
        [(place, SMEM), (stream, None), (depth, None), (norms, None), (small, None)]
        + [(w, spec) for spec in specs for w in halves] + [(cotangent, None)]
        + [(s, None) for s in sums],
        [((8, columns), F32, None), ((rows, width), BF, None), ((half, 2 * hidden_units), BF, None), ((half, 2 * hidden_units), BF, None),
         ((half, columns), BF, None), ((half, columns), BF, None), ((rows, width), F32, None), ((rows, columns), F32, None), ((8, columns), F32, None)]
        + [((8 + HALO, columns), F32, None)] * 2 + [((8, width), F32, None)],
        scratch=[pltpu.VMEM((rows, hidden_units), F32), pltpu.VMEM((rows, hidden_units), BF)],
        micros=12, limit=10, name="turn",
    )


def conv_backward(place, ngrad, ngrad_edges, depth, depth_edges, sums, totals, small, ker, gated, value_half, logistic, normed, halves, at,
                  keep, send, stream_grad, stream, norms, after):
    rows, columns = depth.shape
    width = normed.shape[1]
    groups, half, ext = columns // LANES, width // 2, rows + 2 * HALO
    span = rows * lax.axis_size("tensor")
    parts = len(totals)

    def kernel(place_ref, ngrad_ref, nb_ref, na_ref, depth_ref, db_ref, da_ref, sums_ref, small_ref, gated_ref, value_ref, gate_ref,
               normed_ref, av_ref, bv_ref, ag_ref, bg_ref, sgrad_ref, stream_ref, norms_ref, *refs):
        (ckeep_ref, csend_ref, keep_ref, send_ref, dtaps_ref, out_ref, gb_ref, nsums_ref, totals_ref, grad_ref, acc_ref, normed_t) = refs[parts:]
        length, start = place_ref[1], place_ref[2]
        step = pl.program_id(0)
        totals_ref[...] = sum(r[...] for r in refs[:parts])

        @pl.when(step == 0)
        def _():
            normed_t[...] = normed_ref[...].T
            acc_ref[...] = jnp.zeros_like(acc_ref)
            keep_ref[:, 2 * columns :] = ckeep_ref[...]
            send_ref[:, 2 * columns :] = csend_ref[...]

        taps = small_ref[...].astype(F32)
        count, mean, inv_std = batch_terms(sums_ref)
        batch_gain = taps[ker + 2 : ker + 3]
        sum_gain = batch_gain * totals_ref[0:1, :]
        sum_cross = batch_gain * totals_ref[1:2, :]
        square = inv_std * inv_std * sum_cross / count
        shift = mean * square - inv_std * sum_gain / count
        scale = inv_std * batch_gain
        for first, part, deep in ((0, nb_ref, db_ref), (HALO, ngrad_ref, depth_ref), (HALO + rows, na_ref, da_ref)):
            token = start + (first - HALO) + lax.broadcasted_iota(jnp.int32, part.shape, 0)
            grad = scale * part[...] + jnp.where(token < length, shift - deep[...] * square, 0.0)
            grad_ref[first : first + part.shape[0], :] = jnp.where(
                (token >= 0) & (token < span), grad, 0.0
            )
        own = grad_ref[HALO : HALO + rows, :]
        total = jnp.zeros((rows, LANES), F32)
        for k in range(ker):
            total = total + taps[k : k + 1, :] * grad_ref[ker - k : ker - k + rows, :]
            dtaps_ref[k : k + 1, :] = jnp.sum(
                own * gated_ref[k + 1 : k + 1 + rows, :], 0, keepdims=True
            )
        dtaps_ref[ker:, :] = jnp.zeros_like(dtaps_ref[ker:, :])
        token = start + lax.broadcasted_iota(jnp.int32, total.shape, 0)
        total = jnp.where(token < length, total, 0.0)
        logistic = gate_ref[...]
        dvalue = (total * logistic).astype(BF)
        dgate = (total * value_ref[...] * logistic * (1.0 - logistic)).astype(BF)
        acc_ref[...] += dot_t(dvalue, both(av_ref, bv_ref))
        acc_ref[...] += dot_t(dgate, both(ag_ref, bg_ref))
        for n, grad in enumerate((dvalue, dgate)):
            weight_grad = dot(normed_t[...], grad)
            cols = pl.ds(pl.multiple_of((2 * step + n) * LANES, LANES), LANES)
            keep_ref[:, cols] = weight_grad[:half].astype(BF)
            send_ref[:, cols] = weight_grad[half:].astype(BF)

        @pl.when(step == groups - 1)
        def _():
            extra, dgain, dbeta = norm_back(acc_ref[...], stream_ref[...], norms_ref[2:3, :])
            out = sgrad_ref[...] + extra
            out_ref[...] = out
            gb_ref[...] = out.astype(BF)
            nsums_ref[...] = channel_sums([dgain, dbeta])

    edge = column(HALO)
    ins = [(place, SMEM), (ngrad, column(rows)), (ngrad_edges[0], edge), (ngrad_edges[1], edge), (depth, column(rows)), (depth_edges[0], edge), (depth_edges[1], edge),
           (sums, column(8)), (small, column(small.shape[0])), (gated, column(ext)), (value_half, column(rows)), (logistic, column(rows)),
           (normed, None)] + [(w, column(half, at + i * groups)) for i in (0, 1) for w in halves] + [
           (stream_grad, None), (stream, None), (norms, None)] + [(t, column(8)) for t in totals] + [(keep, None), (send, None)]
    return run(
        kernel, ins,
        [((half, 3 * columns), BF, None), ((half, 3 * columns), BF, None), ((32, columns), F32, column(32)),
         ((rows, width), F32, None), ((rows, width), BF, None), ((8, width), F32, None), ((8, columns), F32, column(8))],
        scratch=[pltpu.VMEM((ext, LANES), F32), pltpu.VMEM((rows, width), F32), pltpu.VMEM((width, rows), BF)],
        grid=(groups,), after=after, micros=8, name="conv_backward",
    )


def on_device(
    inputs,
    lengths,
    rel_embed,
    out_grad,
    norm_gain,
    norm_bias,
    ffn1_in_w,
    ffn1_out_w,
    query_w,
    key_w,
    value_w,
    pos_w,
    attn_out,
    pos_bias,
    conv_value,
    conv_gate,
    depthwise,
    bn_gain,
    bn_bias,
    conv_out,
    ffn2_in_w,
    ffn2_out_w,
):
    size_t = lax.axis_size("tensor")
    me_t = lax.axis_index("tensor")
    me_dp = lax.axis_index("dp")
    size_dp = lax.axis_size("dp")
    rows, width = inputs.shape[1], inputs.shape[2]
    shard = width // size_dp
    part, units = query_w.shape[1], ffn1_in_w.shape[1]
    channels, hidden_units = size_t * part, size_t * units
    span = rows * size_t
    ker = depthwise.shape[0]
    place = jnp.stack([me_t, lengths[0], me_t * rows]).astype(jnp.int32)

    first_shard = regroup([ffn1_in_w, ffn1_out_w.T], [units], name="pack_ffn1")
    first_parts = [first_shard] + tensor_swaps(first_shard)
    norm_cols = jnp.concatenate([norm_gain, norm_bias], 0)
    norm_cols = jnp.pad(norm_cols, ((0, LANES - norm_cols.shape[0]), (0, 0))).T
    norm_cols = core_swap([norm_cols] + chip_swaps(norm_cols), name="rows_norms")
    small = jnp.concatenate([depthwise, pos_bias, bn_gain[None], bn_bias[None]], 0)
    step = max(shard, 16)
    small = jnp.pad(small, ((0, -small.shape[0] % step), (0, 0)))
    small = [small[i : i + shard] for i in range(0, small.shape[0], shard)]
    attn_shard = regroup(
        [query_w, key_w, value_w, pos_w, attn_out.T], [part], small, after=first_parts[1:],
        name="pack_attn",
    )
    attn_parts = [attn_shard] + tensor_swaps(attn_shard)
    second_shard = regroup(
        [ffn2_in_w, ffn2_out_w.T], [units], [conv_value, conv_gate, conv_out.T],
        after=attn_parts[1:], name="pack_second",
    )
    second_parts = [second_shard] + tensor_swaps(second_shard)
    conv_at = 2 * hidden_units // LANES

    feature = jnp.arange(width)
    block = feature // shard
    mask_of = (block & ~7) | ((block >> 2) & 1) | ((block & 3) << 1)
    source = (mask_of ^ me_dp) * shard + feature % shard
    order = (jnp.arange(width)[:, None] == source[None, :]).astype(BF)
    stream0 = dot(inputs[0], order)
    cotangent = dot(out_grad[0], order)
    wide = -(-(span + rows) // LANES) * LANES
    rel_rows = jnp.pad(rel_embed, ((0, span + wide - rel_embed.shape[0]), (0, 0)))
    rel_rows = lax.dynamic_slice_in_dim(rel_rows, rows * (size_t - 1 - me_t), wide, 0)
    rel_rows = dot(rel_rows, order).astype(BF)

    norms, normed_one = first_norm(stream0, norm_cols)
    first_block = regroup(first_parts, [units] * 2, after=[normed_one], name="cols_ffn1")
    first_blocks = [first_block] + plane_swaps(first_block)
    attn_block = regroup(attn_parts, [part] * 5, name="cols_attn")
    attn_blocks = [attn_block] + chip_swaps(attn_block)
    second_block = regroup(second_parts, [units] * 2 + [part] * 3, name="cols_second")
    second_blocks = [second_block] + plane_swaps(second_block)
    small = jnp.concatenate(
        [
            jnp.concatenate([p[:, 5 * part + i * LANES :][:, :LANES] for i in range(len(small))], 0)
            for p in attn_parts
        ],
        1,
    )
    first_w = core_swap(first_blocks, after=[attn_block, second_block], name="rows_ffn1")
    inner_one, stream1, normed_two = ffn1_forward(
        stream0, normed_one, first_w, norms, []
    )
    tokens = lax.all_gather(normed_two, "tensor", axis=0, tiled=True)
    attn_w = core_swap(attn_blocks, after=[tokens, *second_blocks[1:3]], name="rows_attn")
    query_u, query_v, positions, table = attn_queries(
        normed_two, attn_w, rel_rows, small, span, ker, []
    )
    normed_one = regroup([normed_one], [width], after=attn_w[:1], name="carry_norm")
    first_tokens = [normed_one] + tensor_swaps(normed_one)
    mixed, probs, keys, vals, stream2, normed_three, edge_1, edge_3 = attn_main(
        place, tokens, attn_w, query_u, table, stream1, norms, second_blocks[3:]
    )
    hidden, slope, normed_t = ffn1_hidden(place, first_tokens, first_w, units, [stream2])
    second_w = core_swap(second_blocks, after=[stream2, hidden], name="rows_second")
    gated, value_half, logistic, depth, sums, *packs = conv_forward(
        place, normed_three, swap(edge_1, "tensor", 1), swap(edge_3, "tensor", 3), second_w,
        conv_at, small, ker,
    )
    sums, *depth_edges = sum_tensor(place, sums, [packs[0], sums, packs[1]], "sums_forward")
    sums, block_out, keep, send, out_keep, out_send, stream_grad, ngrad, totals, *packs, norm_sums_4 = turn(
        place, stream2, depth, sum_dp(sums), norms, small, ker, second_w, cotangent
    )
    other = core_other(send)
    totals, *ngrad_edges = sum_tensor(place, totals, [packs[0], totals, packs[1]], "sums_back")
    conv_keep, conv_send, taps_grad, stream_grad, gb, norm_sums_2, totals = conv_backward(
        place, ngrad, ngrad_edges, depth, depth_edges, sums, sum_dp(totals), small, ker, gated,
        value_half, logistic, normed_three, second_w, conv_at, out_keep, out_send, stream_grad, stream2, norms, [other],
    )
    second_parts = reduce_core_pairs(
        [(keep, other), (conv_keep, core_other(conv_send))], "core_second"
    )
    came = plane_first(second_parts)
    gp, dk, dv, own_keys, *others = attn_back_keys(
        place, gb, attn_w, probs, keys, vals, query_u, size_t, second_parts[1:2]
    )
    others = [swap(o, "tensor", m) for m, o in enumerate(others, 1)]
    second_parts = plane_second(second_parts, came, [own_keys], "plane_second")
    plane_done = second_parts[4:]
    second_parts = second_parts[:4]
    keeps, sends, own = attn_back_queries(
        gp, keys, positions, query_v, dk, dv, mixed, gb, normed_two, tokens, rel_rows, attn_w,
        taps_grad, plane_done,
    )
    attn_parts = reduce_core_pieces(keeps, sends, 16, "core_attn")
    came = plane_first(attn_parts)
    stream_grad, gb, norm_sums_1 = ffn1_branch_grad(
        sum_parts([own_keys, own, *others], "sum_normed"), stream_grad, stream1, norms,
        [],
    )
    input_grad, norm_rows, gb = ffn1_back_tokens(
        stream_grad, gb, stream0, norms, inner_one, first_w, order,
        [norm_sums_1, norm_sums_2, norm_sums_4], attn_parts[1:2],
    )
    gb_all = lax.all_gather(gb, "tensor", axis=0, tiled=True)
    attn_parts = plane_second(attn_parts, came, [gb_all], "plane_attn")[:4]
    keep, send = ffn1_back_weights(gb_all, hidden, slope, normed_t, first_w, norm_rows, second_parts[1:3])
    first_parts = reduce_core_pairs([(keep, core_other(send))], "core_ffn1")
    first_parts = plane_second(first_parts, plane_first(first_parts), name="plane_ffn1")[:4]
    widths = [units, units, 2 * part, part]
    second_cuts = reduce_split(second_parts, widths, after=[gb_all], name="split_second")
    second_sum = reduce_tensor(second_cuts)
    second_in_grad, second_out_grad, pair_grad, outs_grad = cut_columns(second_sum, widths)
    first_sum = first_parts[0] + sum(p.astype(F32) for p in first_parts[1:3])
    first_in_grad, first_out_grad, norm_cols = cut_columns(first_sum, [units, units, LANES])
    attn_cuts = reduce_split(attn_parts, [part] * 5, norm_cols, name="split_attn")
    attn_sum = reduce_tensor(attn_cuts)
    query_grad, key_grad, value_grad, pos_grad, attn_grad, norm_cols = cut_columns(
        attn_sum[:shard], [part] * 5 + [LANES]
    )
    taps_grad = jnp.concatenate([attn_sum[shard:, :part], attn_sum[shard:, part : 2 * part]], 0)
    bias_grad = attn_sum[shard : shard + 2, 2 * part : 3 * part]
    norm_rows = norm_cols[:, :10].T

    block_out = dot(block_out, order, ((1,), (1,))).astype(BF)
    return (
        block_out[None],
        input_grad[None],
        norm_rows[0:5],
        norm_rows[5:10],
        first_in_grad,
        first_out_grad.T,
        query_grad,
        key_grad,
        value_grad,
        pos_grad,
        attn_grad.T,
        bias_grad,
        pair_grad[:, :part],
        pair_grad[:, part:],
        taps_grad[:ker],
        totals[1, :part],
        totals[0, :part],
        outs_grad.T,
        second_in_grad,
        second_out_grad.T,
    )


def solution(mesh):
    return jax.shard_map(
        on_device,
        mesh=mesh,
        in_specs=(
            P("dp", "tensor", None),
            P("dp"),
            P(),
            P("dp", "tensor", None),
            P(None, "dp"),
            P(None, "dp"),
            P("dp", "tensor"),
            P("tensor", "dp"),
            P("dp", "tensor"),
            P("dp", "tensor"),
            P("dp", "tensor"),
            P("dp", "tensor"),
            P("tensor", "dp"),
            P(None, "tensor"),
            P("dp", "tensor"),
            P("dp", "tensor"),
            P(None, "tensor"),
            P("tensor"),
            P("tensor"),
            P("tensor", "dp"),
            P("dp", "tensor"),
            P("tensor", "dp"),
        ),
        out_specs=(
            P("dp", "tensor", None),
            P("dp", "tensor", None),
            P(None, "dp"),
            P(None, "dp"),
            P("dp", "tensor"),
            P("tensor", "dp"),
            P("dp", "tensor"),
            P("dp", "tensor"),
            P("dp", "tensor"),
            P("dp", "tensor"),
            P("tensor", "dp"),
            P(None, "tensor"),
            P("dp", "tensor"),
            P("dp", "tensor"),
            P(None, "tensor"),
            P("tensor"),
            P("tensor"),
            P("tensor", "dp"),
            P("dp", "tensor"),
            P("tensor", "dp"),
        ),
        check_vma=False,
    )
```

```python
import math

import jax
import jax.numpy as jnp
from jax import lax
from jax.experimental import pallas as pl
from jax.experimental.pallas import tpu as pltpu
from jax.sharding import PartitionSpec as P

DH = 64
LANES = 128
HALO = 16
EPS = 1e-05
NEG = -1000000000.0
HIGHEST = lax.Precision.HIGHEST
BF = jnp.bfloat16
F32 = jnp.float32


def dot(left, right, dims=((1,), (0,)), **kw):
    return lax.dot_general(left, right, (dims, ((), ())), preferred_element_type=F32, **kw)


def dot_t(left, right):
    return dot(left, right, ((1,), (1,)))


def swap(values, axis, mask):
    return lax.ppermute(values, axis, [(i, i ^ mask) for i in range(lax.axis_size(axis))])


def dp_plan():
    size = lax.axis_size("dp")
    chips = [m for m in (0, 2, 4, 6) if m < size]
    doublings = [1] + [1 << b for b in range(3, 20) if 1 << b < size]
    return chips, doublings


def run(kernel, ins, outs, scratch=(), grid=(1,), aliases=None, after=(), micros=3, limit=8, name=None):
    count = len(ins)

    def body(*refs):
        kernel(*refs[:count], *refs[count + len(after) :])

    def whole(shape):
        return pl.BlockSpec(
            tuple(shape), lambda g: (0,) * len(shape), pipeline_mode=pl.Buffered(1)
        )

    def held(shape, dtype, spec):
        if spec is None:
            return math.prod(shape) * jnp.dtype(dtype).itemsize
        if spec.block_shape is None:
            return 0
        buffers = 1 if spec.pipeline_mode is not None else 2
        return buffers * math.prod(spec.block_shape) * jnp.dtype(dtype).itemsize

    need = sum(held(a.shape, a.dtype, spec) for a, spec in ins)
    need += sum(held(*out) for out in outs)
    need += sum(math.prod(r.shape) * jnp.dtype(r.dtype).itemsize for r in scratch)
    limit = need // 2**20 + 1 + limit
    return pl.pallas_call(
        body,
        grid=grid,
        in_specs=[spec or whole(a.shape) for a, spec in ins] + [ANY] * len(after),
        out_specs=[spec or whole(s) for s, _, spec in outs],
        out_shape=[jax.ShapeDtypeStruct(s, d) for s, d, _ in outs],
        scratch_shapes=list(scratch),
        input_output_aliases=aliases or {},
        compiler_params=pltpu.CompilerParams(vmem_limit_bytes=limit * 1024 * 1024),
        cost_estimate=pl.CostEstimate(
            flops=int(micros * 1e9), bytes_accessed=int(micros * 3.0e6), transcendentals=0
        ),
        name=name,
    )(*[a for a, _ in ins], *after)


SMEM = pl.BlockSpec(memory_space=pltpu.SMEM)
ANY = pl.BlockSpec(memory_space=pl.ANY)


def column(rows, offset=0):
    return pl.BlockSpec((rows, LANES), lambda g: (0, offset + g))


def heads(pairs, rows, span):
    return pl.BlockSpec((pairs, rows, span), lambda g: (g, 0, 0))


def regroup(blocks, widths, extras=(), skip=0, after=(), name="regroup"):
    rows = blocks[0].shape[0]
    count, total = len(blocks), sum(widths)

    def kernel(*refs):
        out, at, start = refs[-1], 0, skip
        for width in widths:
            for b in range(count):
                out[:, at : at + width] = refs[b][:, start : start + width]
                at += width
            start += width
        for ref in refs[count:-1]:
            out[:, at : at + ref.shape[1]] = ref[...]
            at += ref.shape[1]

    columns = count * total + sum(e.shape[1] for e in extras)
    return run(
        kernel, [(b, None) for b in (*blocks, *extras)], [((rows, columns), BF, None)],
        after=after, micros=1, name=name,
    )[0]


def stack_rows(pieces, after=(), name="stack_rows"):
    if any(p.shape[0] % 16 for p in pieces):
        return jnp.concatenate(pieces, 0)
    total = sum(p.shape[0] for p in pieces)

    def kernel(*refs):
        at = 0
        for ref in refs[:-1]:
            refs[-1][at : at + ref.shape[0], :] = ref[...]
            at += ref.shape[0]

    return run(
        kernel, [(p, None) for p in pieces], [((total, pieces[0].shape[1]), BF, None)],
        after=after, micros=1.5, name=name,
    )[0]


def tensor_swaps(block):
    return [swap(block, "tensor", m) for m in range(1, lax.axis_size("tensor"))]


def chip_swaps(block):
    chips, _ = dp_plan()
    return [swap(block, "dp", m) for m in chips[1:]]


def plane_swaps(block, after=(), name="plane_halves"):
    half, columns = block.shape[0] // 2, block.shape[1]
    by_x, by_y = swap(block, "dp", 2), swap(block, "dp", 4)
    if half % 16:
        top, low = by_x[:half], by_y[half:]
    else:

        def kernel(x_ref, y_ref, top_ref, low_ref):
            top_ref[...] = x_ref[:half, :]
            low_ref[...] = y_ref[half:, :]

        top, low = run(
            kernel, [(by_x, None), (by_y, None)], [((half, columns), BF, None)] * 2,
            after=after, micros=1, name=name,
        )
    return [by_x, by_y, swap(top, "dp", 4), swap(low, "dp", 2)], [top, low]


def core_swap(pieces, after=(), name="stack_rows"):
    _, doublings = dp_plan()
    rows = stack_rows(pieces, after, name)
    for step in doublings[:-1]:
        rows = jnp.concatenate([rows, swap(rows, "dp", step)], 0)
    return rows, swap(rows, "dp", doublings[-1])


def core_other(send):
    _, doublings = dp_plan()
    return swap(send, "dp", doublings[-1])


def reduce_rest(keep, other, extra):
    _, doublings = dp_plan()
    for step in doublings[-2::-1]:
        both = (keep.astype(F32) + other.astype(F32)).astype(BF)
        main, tail = both[: both.shape[0] - extra], both[both.shape[0] - extra :]
        half = main.shape[0] // 2
        keep = jnp.concatenate([main[:half], tail], 0)
        other = swap(jnp.concatenate([main[half:], tail], 0), "dp", step)
    return keep, other


def reduce_core(arrays, sources, rows, columns, extra=0, name="reduce_core"):
    half = rows // 2

    def pieces(refs):
        for i, parts in enumerate(sources):
            for kept, received, row, at in parts:
                a, b = refs[kept], refs[received]
                value = a[row : row + rows, :].astype(F32) + b[row : row + rows, :].astype(F32)
                tail = None
                if extra:
                    kept, received, row, _ = sources[0][0]
                    a, b = refs[kept], refs[received]
                    first = a.shape[0] - extra
                    tail = a[first:, :].astype(F32) + b[first:, :].astype(F32)
                yield i, slice(at, at + value.shape[1]), value, tail

    shapes = [(rows + extra, F32), (rows, BF), (rows + extra, BF), (half + extra, BF), (half, BF)]
    if rows % 32:
        outs = [[] for _ in shapes]
        for i, _, value, tail in pieces(arrays):
            under = (lambda v: jnp.concatenate([v, tail], 0)) if extra else (lambda v: v)
            for out, part in {
                0: [(0, under(value))],
                1: [(1, value)],
                2: [(2, under(value))],
                3: [(3, under(value[:half])), (4, value[half:])],
            }[i]:
                outs[out].append(part)
        return [jnp.concatenate(o, 1).astype(d) for o, (_, d) in zip(outs, shapes)]

    def kernel(*refs):
        outs = refs[len(arrays) :]
        for i, cols, value, tail in pieces(refs):
            if i == 3:
                outs[3][:half, cols] = value[:half].astype(BF)
                outs[4][:, cols] = value[half:].astype(BF)
            else:
                outs[i][:rows, cols] = value.astype(outs[i].dtype)
            if extra and i in (0, 2):
                outs[i][rows:, cols] = tail.astype(outs[i].dtype)
            if extra and i == 3:
                outs[3][half:, cols] = tail.astype(BF)

    return run(
        kernel, [(x, None) for x in arrays], [((r, columns), d, None) for r, d in shapes],
        micros=2.5, name=name,
    )


def reduce_core_pairs(pairs, name):
    if len(dp_plan()[1]) > 1:
        pairs = [reduce_rest(*[jnp.concatenate(x, 1) for x in zip(*pairs)], 0)]
    rows = pairs[0][0].shape[0] // 4
    starts = [sum(p[0].shape[1] for p in pairs[:n]) for n in range(len(pairs))]
    sources = [
        [(2 * n, 2 * n + 1, i * rows, at) for n, at in enumerate(starts)] for i in range(4)
    ]
    columns = sum(p[0].shape[1] for p in pairs)
    return reduce_core([x for p in pairs for x in p], sources, rows, columns, name=name)


def reduce_core_pieces(keeps, sends, extra, name):
    if len(dp_plan()[1]) > 1:
        keep, send = [
            jnp.concatenate([p[: p.shape[0] - (0 if i else extra)] for i, p in enumerate(x)] + [x[0][-extra:]], 0)
            for x in (keeps, sends)
        ]
        keep, other = reduce_rest(keep, core_other(send), extra)
        rows = (keep.shape[0] - extra) // 4
        sources = [[(0, 1, i * rows, 0)] for i in range(4)]
        return reduce_core([keep, other], sources, rows, keep.shape[1], extra, name)
    rows, columns = keeps[1].shape
    sources = [[(i, 4 + i, 0, 0)] for i in range(4)]
    return reduce_core(
        [*keeps, *[core_other(x) for x in sends]], sources, rows, columns, extra, name
    )


def plane_first(parts):
    return swap(parts[3], "dp", 2), swap(parts[4], "dp", 4)


def plane_second(parts, came, after=(), name="plane_second"):
    own, x, y, _, _ = parts
    rows, extra, columns = x.shape[0], own.shape[0] - x.shape[0], x.shape[1]
    half = rows // 2

    def added(x, y, by_x, by_y):
        low = x[half:, :].astype(F32) + by_y[...].astype(F32)
        top = y[:half, :].astype(F32) + by_x[:half, :].astype(F32)
        tail = y[rows:, :].astype(F32) + by_x[half:, :].astype(F32) if extra else None
        return low.astype(BF), top.astype(BF), tail

    if rows % 32:
        low, top, tail = added(x, y, *came)
        x = jnp.concatenate([x[:half], low], 0)
        y = jnp.concatenate([top, y[half:rows]] + ([tail.astype(BF)] if extra else []), 0)
    else:

        def kernel(x_ref, y_ref, by_x_ref, by_y_ref, x_out, y_out):
            low, top, tail = added(x_ref, y_ref, by_x_ref, by_y_ref)
            x_out[:half, :] = x_ref[:half, :]
            x_out[half:, :] = low
            y_out[:half, :] = top
            y_out[half:rows, :] = y_ref[half:rows, :]
            if extra:
                y_out[rows:, :] = tail.astype(BF)

        x, y = run(
            kernel, [(v, None) for v in (x, y, *came)],
            [((rows, columns), BF, None), ((rows + extra, columns), BF, None)],
            after=after, micros=1.5, name=name,
        )
    return [own, swap(y, "dp", 4), swap(x, "dp", 2), came[0], x]


def reduce_split(parts, widths, shared=None, after=(), name="reduce_split"):
    size = lax.axis_size("tensor")
    rows, extra = parts[2].shape[0], parts[0].shape[0] - parts[2].shape[0]
    half = rows // 2

    def kernel(own_ref, y_ref, x_ref, came_ref, *refs):
        totals = [own_ref[:rows, :] + x_ref[...].astype(F32) + y_ref[:rows, :].astype(F32)]
        if extra:
            tail = own_ref[rows:, :] + y_ref[rows:, :].astype(F32)
            totals.append(tail + came_ref[half:, :].astype(F32))
        for mask in range(size):
            out = refs[mask - size]
            for total, first in zip(totals, (0, rows)):
                at, start, under = 0, 0, slice(first, first + total.shape[0])
                for width in widths:
                    cut = total[:, start + mask * width : start + (mask + 1) * width]
                    out[under, at : at + width] = cut.astype(out.dtype)
                    at += width
                    start += size * width
            if shared is not None:
                out[:rows, at:] = refs[0][...].astype(out.dtype)
                out[rows:, at:] = jnp.zeros((extra, LANES), out.dtype)

    more = [] if shared is None else [shared]
    return run(
        kernel, [(p, None) for p in (*parts, *more)],
        [((rows + extra, sum(widths) + LANES * len(more)), F32 if m == 0 else BF, None) for m in range(size)],
        after=after, micros=1.5, name=name,
    )


def finish(cuts, shapes, pick, name):
    came = [swap(cut, "tensor", mask) for mask, cut in enumerate(cuts[1:], 1)]
    count = len(cuts)

    def kernel(*refs):
        total = refs[0][...]
        for r in refs[1:count]:
            total = total + r[...].astype(F32)
        for out, value in zip(refs[count:], pick(total)):
            out[...] = value

    return run(
        kernel, [(cuts[0], None)] + [(c, None) for c in came], [(s, F32, None) for s in shapes],
        micros=1, name=name,
    )


def cut_columns(total, widths):
    parts, at = [], 0
    for width in widths:
        parts.append(total[:, at : at + width])
        at += width
    return parts


def reduce_tensor(cuts):
    total = cuts[0]
    for mask in range(1, len(cuts)):
        total = total + swap(cuts[mask], "tensor", mask).astype(F32)
    return total


def block_swap(values, mask):
    width = values.shape[1] // 4
    return jnp.concatenate(
        [values[:, (b ^ mask) * width : ((b ^ mask) + 1) * width] for b in range(4)], 1
    )


def edges_of(me, last, first):
    even = (me & 1) == 0
    return jnp.where(even, last, first), jnp.where(even, first, last)


def edges_from(me, by_1, by_3):
    even = (me & 1) == 0
    return jnp.where(even, by_3, by_1), jnp.where(even, by_1, by_3)


def sum_tensor(place, own, packs, name):
    by_1, by_2, by_3 = [swap(p, "tensor", m) for m, p in enumerate(packs, 1)]
    columns = own.shape[1]

    def kernel(place_ref, own_ref, one_ref, two_ref, three_ref, sums_ref, before_ref, after_ref):
        one, three = block_swap(one_ref[...], 1), block_swap(three_ref[...], 3)
        sums_ref[...] = own_ref[...] + one[:8] + block_swap(two_ref[...], 2) + three[:8]
        before_ref[...], after_ref[...] = edges_from(place_ref[0], one[8:], three[8:])

    return run(
        kernel, [(place, SMEM), (own, None), (by_1, None), (by_2, None), (by_3, None)],
        [((8, columns), F32, None)] + [((HALO, columns), F32, None)] * 2,
        micros=1, name=name,
    )


def sum_dp(total):
    _, doublings = dp_plan()
    for step in doublings:
        total = total + swap(total, "dp", step)
    return [total] + chip_swaps(total)


def norm(stream, gain, beta_row):
    centered = stream - jnp.mean(stream, -1, keepdims=True)
    inv_std = lax.rsqrt(jnp.mean(centered * centered, -1, keepdims=True) + EPS)
    scaled = centered * inv_std
    return scaled * gain + beta_row, scaled, inv_std


def norm_back(upstream, stream, gain):
    centered = stream - jnp.mean(stream, -1, keepdims=True)
    inv_std = lax.rsqrt(jnp.mean(centered * centered, -1, keepdims=True) + EPS)
    scaled = centered * inv_std
    grad = upstream * gain
    out = inv_std * (
        grad - jnp.mean(grad, -1, keepdims=True) - scaled * jnp.mean(grad * scaled, -1, keepdims=True)
    )
    return out, jnp.sum(upstream * scaled, 0, keepdims=True), jnp.sum(upstream, 0, keepdims=True)


def swish_slope(inner_act):
    logistic = jax.nn.sigmoid(inner_act)
    return logistic * (1.0 + inner_act * (1.0 - logistic))


def lanes_of(h, rows):
    lane = lax.broadcasted_iota(jnp.int32, (rows, LANES), 1)
    return (lane >= h * DH) & (lane < (h + 1) * DH)


def both(a_ref, b_ref):
    return jnp.concatenate([a_ref[...], b_ref[...]], 0)


def ordered_rows(me, block, rows):
    return pl.ds(pl.multiple_of((me ^ block) * rows, 64), rows)


def channel_sums(rows, count=8):
    return jnp.concatenate(rows + [jnp.zeros((count - len(rows), rows[0].shape[1]), F32)], 0)


def first_norm(stream, columns):
    rows, width = stream.shape
    half = width // 2

    def kernel(stream_ref, a_ref, b_ref, norms_ref, normed_ref):
        for ref, at in ((a_ref, 0), (b_ref, half)):
            norms_ref[:, at : at + half] = ref[...].astype(F32).T[:16]
        normed = norm(stream_ref[...], norms_ref[0:1, :], norms_ref[5:6, :])[0]
        normed_ref[...] = normed.astype(BF)

    return run(
        kernel, [(stream, None), (columns[0], None), (columns[1], None)],
        [((16, width), F32, None), ((rows, width), BF, None)], micros=1, name="first_norm",
    )


def ffn1_forward(stream, normed, halves, norms, after):
    rows, width = stream.shape
    half = width // 2
    hidden_units = halves[0].shape[1] // 2

    def kernel(stream_ref, normed_ref, a_ref, b_ref, norms_ref, inner_ref, out_ref, next_ref):
        normed = normed_ref[...]
        low = jnp.zeros((rows, half), F32)
        high = jnp.zeros((rows, half), F32)
        for j in range(0, hidden_units, 512):
            at = slice(j, j + 512)
            after = slice(hidden_units + j, hidden_units + j + 512)
            inner = dot(normed[:, :half], a_ref[:, at]) + dot(normed[:, half:], b_ref[:, at])
            inner_ref[:, at] = inner
            hidden = jax.nn.silu(inner).astype(BF)
            low = low + dot_t(hidden, a_ref[:, after])
            high = high + dot_t(hidden, b_ref[:, after])
        out = stream_ref[...] + 0.5 * jnp.concatenate([low, high], 1)
        out_ref[...] = out
        next_ref[...] = norm(out, norms_ref[1:2, :], norms_ref[6:7, :])[0].astype(BF)

    return run(
        kernel, [(x, None) for x in (stream, normed, *halves, norms)],
        [((rows, hidden_units), F32, None), ((rows, width), F32, None), ((rows, width), BF, None)],
        after=after, micros=4, name="ffn1_forward",
    )


def ffn1_hidden(place, blocks, halves, units, after):
    rows, width = blocks[0].shape
    half, count = width // 2, len(blocks)
    span = count * rows

    def kernel(place_ref, a_ref, b_ref, *refs):
        hidden_ref, slope_ref, normed_t_ref, ordered = refs[count:]
        for b in range(count):
            normed = refs[b][...]
            at = ordered_rows(place_ref[0], b, rows)
            inner = dot(normed[:, :half], a_ref[...]) + dot(normed[:, half:], b_ref[...])
            logistic = jax.nn.sigmoid(inner)
            hidden_ref[at, :] = (inner * logistic).astype(BF)
            slope_ref[at, :] = logistic * (1.0 + inner * (1.0 - logistic))
            ordered[at, :] = normed
        normed_t_ref[...] = ordered[...].T

    own = pl.BlockSpec((half, units), lambda g: (0, 0), pipeline_mode=pl.Buffered(1))
    return run(
        kernel, [(place, SMEM)] + [(x, own) for x in halves] + [(x, None) for x in blocks],
        [((span, units), BF, None), ((span, units), F32, None), ((width, span), BF, None)],
        scratch=[pltpu.VMEM((span, width), BF)], after=after, micros=2, name="ffn1_hidden",
    )


def sum_parts(parts, name):
    def kernel(*refs):
        refs[-1][...] = sum(r[...].astype(F32) for r in refs[:-1])

    return run(kernel, [(p, None) for p in parts], [(parts[0].shape, F32, None)], micros=6, name=name)[0]


def ffn1_branch_grad(upstream, stream_grad, stream, norms, after):
    rows, width = stream.shape

    def kernel(upstream_ref, grad_ref, stream_ref, norms_ref, out_ref, gb_ref, sums_ref):
        extra, dgain, dbeta = norm_back(upstream_ref[...], stream_ref[...], norms_ref[1:2, :])
        sums_ref[...] = channel_sums([dgain, dbeta])
        out = grad_ref[...] + extra
        out_ref[...] = out
        gb_ref[...] = (0.5 * out).astype(BF)

    return run(
        kernel, [(x, None) for x in (upstream, stream_grad, stream, norms)],
        [((rows, width), F32, None), ((rows, width), BF, None), ((8, width), F32, None)],
        after=after, micros=1.5, name="ffn1_branch_grad",
    )


def ffn1_back_tokens(stream_grad, gb, stream, norms, inner, halves, sums, after):
    rows, width = stream.shape
    hidden_units = inner.shape[1]
    half = width // 2

    def kernel(grad_ref, gb_ref, stream_ref, norms_ref, inner_ref, a_ref, b_ref, s1_ref, s2_ref, s4_ref,
               out_ref, norm_rows_ref, gb_out_ref):
        gb = gb_ref[...]
        gb_out_ref[...] = gb
        low = jnp.zeros((rows, half), F32)
        high = jnp.zeros((rows, half), F32)
        for j in range(0, hidden_units, 512):
            at = slice(j, j + 512)
            after = slice(hidden_units + j, hidden_units + j + 512)
            grad = dot(gb[:, :half], a_ref[:, after]) + dot(gb[:, half:], b_ref[:, after])
            grad = (grad * swish_slope(inner_ref[:, at])).astype(BF)
            low = low + dot_t(grad, a_ref[:, at])
            high = high + dot_t(grad, b_ref[:, at])
        extra, dgain, dbeta = norm_back(
            jnp.concatenate([low, high], 1), stream_ref[...], norms_ref[0:1, :]
        )
        gains = [dgain, s1_ref[0:1, :], s2_ref[0:1, :], s4_ref[0:1, :], s4_ref[2:3, :]]
        betas = [dbeta, s1_ref[1:2, :], s2_ref[1:2, :], s4_ref[1:2, :], s4_ref[3:4, :]]
        norm_rows_ref[...] = channel_sums(gains + betas, 16)
        out_ref[...] = grad_ref[...] + extra

    ins = [stream_grad, gb, stream, norms, inner, *halves, *sums]
    return run(
        kernel, [(x, None) for x in ins],
        [((rows, width), F32, None), ((16, width), F32, None), ((rows, width), BF, None)],
        after=after, micros=5, name="ffn1_back_tokens",
    )


def ffn1_back_weights(gb, hidden, slope, normed_t, halves, norm_rows, after):
    width, span = normed_t.shape
    units, half = hidden.shape[1], width // 2

    def kernel(gb_ref, hidden_ref, slope_ref, normed_t_ref, a_ref, b_ref, norm_ref, keep_ref, send_ref):
        gb = gb_ref[...]
        grad = dot(gb[:, :half], a_ref[...]) + dot(gb[:, half:], b_ref[...])
        grad = (grad * slope_ref[...]).astype(BF)
        columns = jnp.concatenate([norm_ref[...], jnp.zeros((LANES - 16, width), F32)], 0).T
        grads = [dot(normed_t_ref[...], grad), dot(gb.T, hidden_ref[...]), columns]
        at = 0
        for g in grads:
            keep_ref[:, at : at + g.shape[1]] = g[:half].astype(BF)
            send_ref[:, at : at + g.shape[1]] = g[half:].astype(BF)
            at += g.shape[1]

    first = halves[0].shape[1] // (2 * units)
    own = pl.BlockSpec((half, units), lambda g: (0, first), pipeline_mode=pl.Buffered(1))
    total = 2 * units + LANES
    return run(
        kernel,
        [(gb, None), (hidden, None), (slope, None), (normed_t, None), (halves[0], own), (halves[1], own), (norm_rows, None)],
        [((half, total), BF, None), ((half, total), BF, None)],
        after=after, micros=4, name="ffn1_back_weights",
    )


def attn_queries(normed, halves, rel_rows, small, span, bias_row, after):
    rows, width = normed.shape
    wide, columns = rel_rows.shape[0], small.shape[1]
    groups, pairs = columns // LANES, LANES // DH
    half = width // 2

    def kernel(rows_ref, aq_ref, bq_ref, ap_ref, bp_ref, rel_ref, small_ref, qu_ref, qv_ref, pos_ref, table_ref):
        queries = dot(rows_ref[...], both(aq_ref, bq_ref))
        bias = small_ref[...].astype(F32)
        qu_ref[...] = (queries + bias[bias_row : bias_row + 1]).astype(BF)
        query_v = (queries + bias[bias_row + 1 : bias_row + 2]).astype(BF)
        qv_ref[...] = query_v
        positions = dot(rel_ref[...], both(ap_ref, bp_ref)).astype(BF)
        pos_ref[...] = positions
        for h in range(pairs):
            mine = jnp.where(lanes_of(h, rows), query_v, jnp.zeros_like(query_v))
            table = dot_t(mine, positions)
            shifted = pltpu.roll(table, wide - (rows - 1), 1, stride=1, stride_axis=0)
            table_ref[h] = shifted[:, :span]

    def weight(i):
        return column(half, i * groups)

    a, b = halves
    return run(
        kernel,
        [(normed, None), (a, weight(0)), (b, weight(0)), (a, weight(3)), (b, weight(3)), (rel_rows, None), (small, column(small.shape[0]))],
        [((rows, columns), BF, column(rows)), ((rows, columns), BF, column(rows)), ((wide, columns), BF, column(wide)),
         ((groups * pairs, rows, span), F32, heads(pairs, rows, span))],
        grid=(groups,), after=after, micros=0.5, name="attn_queries",
    )


def attn_main(place, tokens, halves, query_u, table, stream, norms, after):
    rows, width = stream.shape
    span, columns = table.shape[2], query_u.shape[1]
    groups, pairs = columns // LANES, LANES // DH
    half = width // 2

    def kernel(place_ref, rows_ref, *refs):
        (ak_ref, bk_ref, av_ref, bv_ref, ao_ref, bo_ref, qu_ref, table_ref, stream_ref, norms_ref,
         mixed_ref, probs_ref, keys_ref, vals_ref, out_ref, normed_ref, edge_1_ref, edge_3_ref) = refs
        me, length = place_ref[0], place_ref[1]
        keys = dot(rows_ref[...], both(ak_ref, bk_ref)).astype(BF)
        vals = dot(rows_ref[...], both(av_ref, bv_ref)).astype(BF)
        keys_ref[...], vals_ref[...], query_u = keys, vals, qu_ref[...]
        visible = lax.broadcasted_iota(jnp.int32, (rows, span), 1) < length
        mixed = jnp.zeros((rows, LANES), F32)
        for h in range(pairs):
            mine = lanes_of(h, rows)
            content = dot_t(jnp.where(mine, query_u, jnp.zeros_like(query_u)), keys)
            scores = jnp.where(visible, (content + table_ref[h]) * DH ** (-0.5), NEG)
            exponent = jnp.exp(scores - jnp.max(scores, -1, keepdims=True))
            probs = exponent / jnp.sum(exponent, -1, keepdims=True)
            probs_ref[h] = probs
            mixed = jnp.where(mine, dot(probs.astype(BF), vals), mixed)
        mixed = mixed.astype(BF)
        mixed_ref[...] = mixed

        @pl.when(pl.program_id(0) == 0)
        def _():
            out_ref[...] = stream_ref[...]

        out_ref[...] += dot_t(mixed, both(ao_ref, bo_ref))

        @pl.when(pl.program_id(0) == groups - 1)
        def _():
            normed = norm(out_ref[...], norms_ref[2:3, :], norms_ref[7:8, :])[0].astype(BF)
            normed_ref[...] = normed
            edge_1_ref[...], edge_3_ref[...] = edges_of(me, normed[rows - HALO :], normed[:HALO])

    def weight(i):
        return column(half, i * groups)

    a, b = halves
    return run(
        kernel,
        [(place, SMEM), (tokens, None)] + [(w, weight(i)) for i in (1, 2, 4) for w in (a, b)]
        + [(query_u, column(rows)), (table, heads(pairs, rows, span)), (stream, None), (norms, None)],
        [((rows, columns), BF, column(rows)), ((groups * pairs, rows, span), F32, heads(pairs, rows, span)),
         ((span, columns), BF, column(span)), ((span, columns), BF, column(span)),
         ((rows, width), F32, None), ((rows, width), BF, None), ((HALO, width), BF, None), ((HALO, width), BF, None)],
        grid=(groups,), after=after, micros=0.2, name="attn_main",
    )


def attn_back_keys(place, gb, halves, probs, keys, vals, query_u, count, after):
    rows, width = gb.shape
    span, columns = keys.shape
    groups, pairs = columns // LANES, LANES // DH
    half = width // 2

    def kernel(place_ref, gb_ref, ao_ref, bo_ref, ak_ref, bk_ref, av_ref, bv_ref, probs_ref, keys_ref, vals_ref, qu_ref,
               gp_ref, dk_ref, dv_ref, own_ref, *refs):
        other_refs, total = refs[:-1], refs[-1]
        me = place_ref[0]
        step = pl.program_id(0)
        gm = dot(gb_ref[...], both(ao_ref, bo_ref)).astype(BF)
        gm_t, qu_t = gm.T, qu_ref[...].T
        vals = vals_ref[...]
        dk_t, dv_t = [], []
        for h in range(pairs):
            head = slice(h * DH, (h + 1) * DH)
            probs = probs_ref[h]
            dprobs = dot_t(jnp.where(lanes_of(h, rows), gm, jnp.zeros_like(gm)), vals)
            delta = jnp.sum(dprobs * probs, -1, keepdims=True)
            gp = ((DH ** (-0.5) * probs) * (dprobs - delta)).astype(BF)
            gp_ref[h] = gp
            dv_t.append(dot(gm_t[head], probs.astype(BF)))
            dk_t.append(dot(qu_t[head], gp))
        dk = jnp.concatenate(dk_t, 0).T.astype(BF)
        dv = jnp.concatenate(dv_t, 0).T.astype(BF)
        dk_ref[...] = dk
        dv_ref[...] = dv
        grad = dot_t(dk, both(ak_ref, bk_ref)) + dot_t(dv, both(av_ref, bv_ref))

        @pl.when(step == 0)
        def _():
            total[...] = grad

        @pl.when(step > 0)
        def _():
            total[...] += grad

        @pl.when(step == groups - 1)
        def _():
            own_ref[...] = total[ordered_rows(me, 0, rows), :]
            for b in range(1, count):
                other_refs[b - 1][...] = total[ordered_rows(me, b, rows), :].astype(BF)

    def weight(i):
        return column(half, i * groups)

    a, b = halves
    return run(
        kernel,
        [(place, SMEM), (gb, None)] + [(w, weight(i)) for i in (4, 1, 2) for w in (a, b)]
        + [(probs, heads(pairs, rows, span)), (keys, column(span)), (vals, column(span)), (query_u, column(rows))],
        [((groups * pairs, rows, span), BF, heads(pairs, rows, span)), ((span, columns), BF, column(span)), ((span, columns), BF, column(span)),
         ((rows, width), F32, None)] + [((rows, width), BF, None)] * (count - 1),
        scratch=[pltpu.VMEM((span, width), F32)],
        grid=(groups,), after=after, micros=11, name="attn_back_keys",
    )


def attn_back_queries(gp, keys, positions, query_v, dk, dv, mixed, gb, normed, tokens, rel_rows, halves, taps_grad, after):
    rows, width = gb.shape
    span, columns = keys.shape
    wide = rel_rows.shape[0]
    groups, pairs = columns // LANES, LANES // DH
    half, pieces = width // 2, 4
    size = half // pieces

    def kernel(gp_ref, keys_ref, pos_ref, qv_ref, dk_ref, dv_ref, mixed_ref, aq_ref, bq_ref, gb_ref, rel_ref, dtaps_ref, normed_ref, tokens_ref, *refs):
        piece_refs, (own_ref, normed_t, tokens_t, rel_t, gb_t) = refs[: 2 * pieces], refs[2 * pieces :]
        step = pl.program_id(0)

        @pl.when(step == 0)
        def _():
            normed_t[...] = normed_ref[...].T
            tokens_t[...] = tokens_ref[...].T
            rel_t[...] = rel_ref[...].T
            gb_t[...] = gb_ref[...].T
            own_ref[...] = jnp.zeros_like(own_ref)

        i = lax.broadcasted_iota(jnp.int32, (rows, rows), 0)
        j = lax.broadcasted_iota(jnp.int32, (rows, rows), 1)
        flip = jnp.where(i + j == rows - 1, 1.0, 0.0)
        flip_low = flip.astype(BF)
        keys, positions = keys_ref[...], pos_ref[...]
        qv_t = dot(flip_low, qv_ref[...]).astype(BF).T
        du = jnp.zeros((rows, LANES), F32)
        dv_rows = jnp.zeros((rows, LANES), F32)
        dp_t = []
        for h in range(pairs):
            mine = lanes_of(h, rows)
            gp = gp_ref[h]
            du = jnp.where(mine, dot(gp, keys), du)
            flipped = dot(flip_low, gp)
            table = jnp.concatenate([flipped, jnp.zeros((rows, wide - span), F32)], 1)
            table = pltpu.roll(table, 0, 1, stride=1, stride_axis=0).astype(BF)
            dp_t.append(dot(qv_t[h * DH : (h + 1) * DH], table))
            dv_rows = jnp.where(mine, dot(table, positions), dv_rows)
        dv_rows = dot(flip, dv_rows, precision=HIGHEST)
        bias = channel_sums(
            [jnp.sum(du, 0, keepdims=True), jnp.sum(dv_rows, 0, keepdims=True)], 16
        )
        nothing = jnp.zeros((16, LANES), F32)
        extras = [dtaps_ref[:16, :], dtaps_ref[16:, :], bias, nothing, nothing]
        dq = (du + dv_rows).astype(BF)
        dp = jnp.concatenate(dp_t, 0).T.astype(BF)
        own_ref[...] += dot_t(dq, both(aq_ref, bq_ref))
        grads = [
            dot(normed_t[...], dq),
            dot(tokens_t[...], dk_ref[...]),
            dot(tokens_t[...], dv_ref[...]),
            dot(rel_t[...], dp),
            dot(gb_t[...], mixed_ref[...]),
        ]
        for n, grad in enumerate(grads):
            at = pl.ds(pl.multiple_of((n * groups + step) * LANES, LANES), LANES)
            low = grad.astype(BF)
            for i, ref in enumerate(piece_refs):
                ref[:size, at] = low[i * size : (i + 1) * size]
                if i % pieces == 0:
                    ref[size:, at] = extras[n].astype(BF)

    a, b = halves
    outs = run(
        kernel,
        [(gp, heads(pairs, rows, span)), (keys, column(span)), (positions, column(wide)), (query_v, column(rows)),
         (dk, column(span)), (dv, column(span)), (mixed, column(rows)), (a, column(half)), (b, column(half)), (gb, None), (rel_rows, None), (taps_grad, column(32)),
         (normed, None), (tokens, None)],
        [((size + (0 if i % pieces else 16), 5 * columns), BF, None) for i in range(2 * pieces)] + [((rows, width), F32, None)],
        scratch=[pltpu.VMEM((width, rows), BF), pltpu.VMEM((width, span), BF), pltpu.VMEM((width, wide), BF), pltpu.VMEM((width, rows), BF)],
        grid=(groups,), after=after, micros=13, name="attn_back_queries",
    )
    return outs[:pieces], outs[pieces : 2 * pieces], outs[-1]


def joined(a_ref, b_ref, at):
    return jnp.concatenate([a_ref[:, at], b_ref[:, at]], 0)


def conv_forward(place, normed, by_1, by_3, halves, at, small, ker, after):
    rows, width = normed.shape
    columns = small.shape[1]
    groups, half, ext = columns // LANES, width // 2, rows + 2 * HALO

    def kernel(place_ref, rows_ref, one_ref, three_ref, av_ref, bv_ref, ag_ref, bg_ref, small_ref,
               gated_ref, value_ref, gate_ref, depth_ref, sums_ref, pack_1_ref, pack_3_ref):
        me, length, start = place_ref[0], place_ref[1], place_ref[2]
        before, after = edges_from(me, one_ref[...], three_ref[...])
        tokens = jnp.concatenate([before, rows_ref[...], after], 0)
        value_half = dot(tokens, both(av_ref, bv_ref))
        logistic = jax.nn.sigmoid(dot(tokens, both(ag_ref, bg_ref)))
        token = start - HALO + lax.broadcasted_iota(jnp.int32, value_half.shape, 0)
        mask = jnp.where((token >= 0) & (token < length), 1.0, 0.0)
        gated_ref[...] = mask * value_half * logistic
        value_ref[...] = value_half[HALO : HALO + rows]
        gate_ref[...] = logistic[HALO : HALO + rows]
        taps = small_ref[...].astype(F32)
        depth = jnp.zeros((rows, LANES), F32)
        for k in range(ker):
            depth = depth + taps[k : k + 1, :] * gated_ref[k + 1 : k + 1 + rows, :]
        depth_ref[...] = depth
        mask = mask[HALO : HALO + rows]
        masked = depth * mask
        sums = channel_sums([jnp.sum(x, 0, keepdims=True) for x in (masked, masked * depth, mask)])
        sums_ref[...] = sums
        one, three = edges_of(me, depth[rows - HALO :], depth[:HALO])
        pack_1_ref[:8, :], pack_1_ref[8:, :] = sums, one
        pack_3_ref[:8, :], pack_3_ref[8:, :] = sums, three

    return run(
        kernel,
        [(place, SMEM), (normed, None), (by_1, None), (by_3, None)]
        + [(w, column(half, at + i * groups)) for i in (0, 1) for w in halves] + [(small, column(small.shape[0]))],
        [((ext, columns), F32, column(ext))] + [((rows, columns), F32, column(rows))] * 3
        + [((8, columns), F32, column(8))] + [((8 + HALO, columns), F32, column(8 + HALO))] * 2,
        grid=(groups,), after=after, micros=4, name="conv_forward",
    )


def batch_terms(sums_ref):
    count = sums_ref[2:3, :]
    mean = sums_ref[0:1, :] / count
    inv_std = lax.rsqrt(sums_ref[1:2, :] / count - mean * mean + EPS)
    return count, mean, inv_std


def turn(place, stream, depth, sums, norms, small, ker, conv_halves, halves, cotangent):
    rows, width = stream.shape
    columns = depth.shape[1]
    groups = columns // LANES
    half = width // 2
    hidden_units = halves[0].shape[1] // 2
    units = hidden_units // groups
    parts = len(sums)

    def kernel(place_ref, stream_ref, depth_ref, norms_ref, small_ref, ac_ref, bc_ref, ai_ref, bi_ref, ao_ref, bo_ref, cot_ref, *refs):
        (sums_ref, out_ref, keep_ref, send_ref, ckeep_ref, csend_ref, grad_ref, ngrad_ref, own_ref, pack_1_ref, pack_3_ref, nsums_ref,
         inner_ref, hidden_ref) = refs[parts:]
        sums_ref[...] = sum(r[...] for r in refs[:parts])
        _, mean, inv_std = batch_terms(sums_ref)
        batch_gain = small_ref[...].astype(F32)[ker + 2 : ker + 3]
        batch_bias = small_ref[...].astype(F32)[ker + 3 : ker + 4]
        scaled = (depth_ref[...] - mean) * inv_std
        normal = scaled * batch_gain + batch_bias
        active = jax.nn.silu(normal).astype(BF)
        wc = both(ac_ref, bc_ref)
        stream3 = stream_ref[...] + dot_t(active, wc)
        normed = norm(stream3, norms_ref[3:4, :], norms_ref[8:9, :])[0].astype(BF)
        branch = jnp.zeros((rows, width), F32)
        for p in range(groups):
            j = slice(p * units, (p + 1) * units)
            inner = dot(normed, joined(ai_ref, bi_ref, j))
            inner_ref[:, j] = inner
            hidden = jax.nn.silu(inner).astype(BF)
            hidden_ref[:, j] = hidden
            branch = branch + dot_t(hidden, joined(ao_ref, bo_ref, j))
        stream4 = stream3 + 0.5 * branch
        out_ref[...] = norm(stream4, norms_ref[4:5, :], norms_ref[9:10, :])[0].astype(BF)
        grad, gain5, beta5 = norm_back(cot_ref[...], stream4, norms_ref[4:5, :])
        gb = (0.5 * grad).astype(BF)
        gb_t, normed_t = gb.T, normed.T
        upstream = jnp.zeros((rows, width), F32)
        for p in range(groups):
            j = slice(p * units, (p + 1) * units)
            after = slice(hidden_units + p * units, hidden_units + (p + 1) * units)
            inner_grad = dot(gb, joined(ao_ref, bo_ref, j))
            inner_grad = (inner_grad * swish_slope(inner_ref[:, j])).astype(BF)
            in_grad = dot(normed_t, inner_grad)
            keep_ref[:, j] = in_grad[:half].astype(BF)
            send_ref[:, j] = in_grad[half:].astype(BF)
            out_grad = dot(gb_t, hidden_ref[:, j])
            keep_ref[:, after] = out_grad[:half].astype(BF)
            send_ref[:, after] = out_grad[half:].astype(BF)
            upstream = upstream + dot_t(inner_grad, joined(ai_ref, bi_ref, j))
        extra, gain4, beta4 = norm_back(upstream, stream3, norms_ref[3:4, :])
        nsums_ref[...] = channel_sums([gain4, beta4, gain5, beta5])
        grad = grad + extra
        grad_ref[...] = grad
        gb = grad.astype(BF)
        weight_grad = dot(gb.T, active)
        ckeep_ref[...] = weight_grad[:half].astype(BF)
        csend_ref[...] = weight_grad[half:].astype(BF)
        ngrad = dot(gb, wc) * swish_slope(normal)
        ngrad_ref[...] = ngrad
        own = channel_sums([jnp.sum(ngrad, 0, keepdims=True), jnp.sum(ngrad * scaled, 0, keepdims=True)])
        own_ref[...] = own
        one, three = edges_of(place_ref[0], ngrad[rows - HALO :], ngrad[:HALO])
        pack_1_ref[:8, :], pack_1_ref[8:, :] = own, one
        pack_3_ref[:8, :], pack_3_ref[8:, :] = own, three

    def block(columns, index):
        return pl.BlockSpec((half, columns), lambda g: (0, index), pipeline_mode=pl.Buffered(1))

    specs = [block(hidden_units, 0), block(hidden_units, 1)]
    return run(
        kernel,
        [(place, SMEM), (stream, None), (depth, None), (norms, None), (small, None)]
        + [(w, block(columns, 7)) for w in conv_halves] + [(w, spec) for spec in specs for w in halves] + [(cotangent, None)]
        + [(s, None) for s in sums],
        [((8, columns), F32, None), ((rows, width), BF, None), ((half, 2 * hidden_units), BF, None), ((half, 2 * hidden_units), BF, None),
         ((half, columns), BF, None), ((half, columns), BF, None), ((rows, width), F32, None), ((rows, columns), F32, None), ((8, columns), F32, None)]
        + [((8 + HALO, columns), F32, None)] * 2 + [((8, width), F32, None)],
        scratch=[pltpu.VMEM((rows, hidden_units), F32), pltpu.VMEM((rows, hidden_units), BF)],
        micros=12, limit=10, name="turn",
    )


def conv_backward(place, ngrad, ngrad_edges, depth, depth_edges, sums, totals, small, ker, gated, value_half, logistic, normed, halves, at,
                  keep, send, stream_grad, stream, norms, after):
    rows, columns = depth.shape
    width = normed.shape[1]
    groups, half, ext = columns // LANES, width // 2, rows + 2 * HALO
    span = rows * lax.axis_size("tensor")
    parts = len(totals)

    def kernel(place_ref, ngrad_ref, nb_ref, na_ref, depth_ref, db_ref, da_ref, sums_ref, small_ref, gated_ref, value_ref, gate_ref,
               normed_ref, av_ref, bv_ref, ag_ref, bg_ref, sgrad_ref, stream_ref, norms_ref, *refs):
        (ckeep_ref, csend_ref, keep_ref, send_ref, dtaps_ref, out_ref, gb_ref, nsums_ref, totals_ref, grad_ref, acc_ref, normed_t) = refs[parts:]
        length, start = place_ref[1], place_ref[2]
        step = pl.program_id(0)
        totals_ref[...] = sum(r[...] for r in refs[:parts])

        @pl.when(step == 0)
        def _():
            normed_t[...] = normed_ref[...].T
            acc_ref[...] = jnp.zeros_like(acc_ref)
            keep_ref[:, 2 * columns :] = ckeep_ref[...]
            send_ref[:, 2 * columns :] = csend_ref[...]

        taps = small_ref[...].astype(F32)
        count, mean, inv_std = batch_terms(sums_ref)
        batch_gain = taps[ker + 2 : ker + 3]
        sum_gain = batch_gain * totals_ref[0:1, :]
        sum_cross = batch_gain * totals_ref[1:2, :]
        square = inv_std * inv_std * sum_cross / count
        shift = mean * square - inv_std * sum_gain / count
        scale = inv_std * batch_gain
        for first, part, deep in ((0, nb_ref, db_ref), (HALO, ngrad_ref, depth_ref), (HALO + rows, na_ref, da_ref)):
            token = start + (first - HALO) + lax.broadcasted_iota(jnp.int32, part.shape, 0)
            grad = scale * part[...] + jnp.where(token < length, shift - deep[...] * square, 0.0)
            grad_ref[first : first + part.shape[0], :] = jnp.where(
                (token >= 0) & (token < span), grad, 0.0
            )
        own = grad_ref[HALO : HALO + rows, :]
        total = jnp.zeros((rows, LANES), F32)
        for k in range(ker):
            total = total + taps[k : k + 1, :] * grad_ref[ker - k : ker - k + rows, :]
            dtaps_ref[k : k + 1, :] = jnp.sum(
                own * gated_ref[k + 1 : k + 1 + rows, :], 0, keepdims=True
            )
        dtaps_ref[ker:, :] = jnp.zeros_like(dtaps_ref[ker:, :])
        token = start + lax.broadcasted_iota(jnp.int32, total.shape, 0)
        total = jnp.where(token < length, total, 0.0)
        logistic = gate_ref[...]
        dvalue = (total * logistic).astype(BF)
        dgate = (total * value_ref[...] * logistic * (1.0 - logistic)).astype(BF)
        acc_ref[...] += dot_t(dvalue, both(av_ref, bv_ref))
        acc_ref[...] += dot_t(dgate, both(ag_ref, bg_ref))
        for n, grad in enumerate((dvalue, dgate)):
            weight_grad = dot(normed_t[...], grad)
            cols = pl.ds(pl.multiple_of((2 * step + n) * LANES, LANES), LANES)
            keep_ref[:, cols] = weight_grad[:half].astype(BF)
            send_ref[:, cols] = weight_grad[half:].astype(BF)

        @pl.when(step == groups - 1)
        def _():
            extra, dgain, dbeta = norm_back(acc_ref[...], stream_ref[...], norms_ref[2:3, :])
            out = sgrad_ref[...] + extra
            out_ref[...] = out
            gb_ref[...] = out.astype(BF)
            nsums_ref[...] = channel_sums([dgain, dbeta])

    edge = column(HALO)
    ins = [(place, SMEM), (ngrad, column(rows)), (ngrad_edges[0], edge), (ngrad_edges[1], edge), (depth, column(rows)), (depth_edges[0], edge), (depth_edges[1], edge),
           (sums, column(8)), (small, column(small.shape[0])), (gated, column(ext)), (value_half, column(rows)), (logistic, column(rows)),
           (normed, None)] + [(w, column(half, at + i * groups)) for i in (0, 1) for w in halves] + [
           (stream_grad, None), (stream, None), (norms, None)] + [(t, column(8)) for t in totals] + [(keep, None), (send, None)]
    return run(
        kernel, ins,
        [((half, 3 * columns), BF, None), ((half, 3 * columns), BF, None), ((32, columns), F32, column(32)),
         ((rows, width), F32, None), ((rows, width), BF, None), ((8, width), F32, None), ((8, columns), F32, column(8))],
        scratch=[pltpu.VMEM((ext, LANES), F32), pltpu.VMEM((rows, width), F32), pltpu.VMEM((width, rows), BF)],
        grid=(groups,), after=after, micros=8, name="conv_backward",
    )


def on_device(
    inputs,
    lengths,
    rel_embed,
    out_grad,
    norm_gain,
    norm_bias,
    ffn1_in_w,
    ffn1_out_w,
    query_w,
    key_w,
    value_w,
    pos_w,
    attn_out,
    pos_bias,
    conv_value,
    conv_gate,
    depthwise,
    bn_gain,
    bn_bias,
    conv_out,
    ffn2_in_w,
    ffn2_out_w,
):
    size_t = lax.axis_size("tensor")
    me_t = lax.axis_index("tensor")
    me_dp = lax.axis_index("dp")
    size_dp = lax.axis_size("dp")
    rows, width = inputs.shape[1], inputs.shape[2]
    shard = width // size_dp
    part, units = query_w.shape[1], ffn1_in_w.shape[1]
    channels, hidden_units = size_t * part, size_t * units
    span = rows * size_t
    ker = depthwise.shape[0]
    place = jnp.stack([me_t, lengths[0], me_t * rows]).astype(jnp.int32)

    first_shard = regroup([ffn1_in_w, ffn1_out_w.T], [units], name="pack_ffn1")
    first_parts = [first_shard] + tensor_swaps(first_shard)
    norm_cols = jnp.concatenate([norm_gain, norm_bias], 0)
    norm_cols = jnp.pad(norm_cols, ((0, LANES - norm_cols.shape[0]), (0, 0))).T
    norm_cols = regroup([norm_cols], [LANES], after=[first_shard], name="pack_norms")
    norm_cols = core_swap([norm_cols] + chip_swaps(norm_cols), name="rows_norms")
    small = jnp.concatenate([depthwise, pos_bias, bn_gain[None], bn_bias[None]], 0)
    step = max(shard, 16)
    small = jnp.pad(small, ((0, -small.shape[0] % step), (0, 0)))
    small = [small[i : i + shard] for i in range(0, small.shape[0], shard)]
    attn_shard = regroup(
        [query_w, key_w, value_w, pos_w, attn_out.T, conv_value, conv_gate, conv_out.T],
        [part], small, after=first_parts[1:], name="pack_attn",
    )
    attn_parts = [attn_shard] + tensor_swaps(attn_shard)
    second_shard = regroup(
        [ffn2_in_w, ffn2_out_w.T], [units], after=attn_parts[1:], name="pack_second"
    )
    second_parts = [second_shard] + tensor_swaps(second_shard)

    feature = jnp.arange(width)
    block = feature // shard
    mask_of = (block & ~7) | ((block >> 2) & 1) | ((block & 3) << 1)
    source = (mask_of ^ me_dp) * shard + feature % shard
    order = (jnp.arange(width)[:, None] == source[None, :]).astype(BF)
    stream0 = dot(inputs[0], order)
    cotangent = dot(out_grad[0], order)
    wide = -(-(span + rows) // LANES) * LANES
    rel_rows = jnp.pad(rel_embed, ((0, span + wide - rel_embed.shape[0]), (0, 0)))
    rel_rows = lax.dynamic_slice_in_dim(rel_rows, rows * (size_t - 1 - me_t), wide, 0)
    rel_rows = dot(rel_rows, order).astype(BF)

    norms, normed_one = first_norm(stream0, norm_cols)
    first_block = regroup(first_parts, [units] * 2, after=[normed_one], name="cols_ffn1")
    first_blocks = [first_block] + plane_swaps(first_block, name="halves_ffn1")[0]
    attn_block = regroup(attn_parts, [part] * 8, name="cols_attn")
    attn_blocks = [attn_block] + chip_swaps(attn_block)
    if len(small) == 1:
        small = regroup(attn_parts, [part], skip=8 * part, name="cols_small")
    else:
        pieces = [cut_columns(p[:, 8 * part :], [LANES] * len(small)) for p in attn_parts]
        small = jnp.concatenate([jnp.concatenate(p, 0) for p in pieces], 1)
    first_w = core_swap(first_blocks, after=[attn_block, rel_rows, small, *second_parts[1:]], name="rows_ffn1")
    inner_one, stream1, normed_two = ffn1_forward(
        stream0, normed_one, first_w, norms, []
    )
    tokens = lax.all_gather(normed_two, "tensor", axis=0, tiled=True)
    second_block = regroup(second_parts, [units] * 2, after=[tokens], name="cols_second")
    attn_w = core_swap(attn_blocks, after=[tokens], name="rows_attn")
    query_u, query_v, positions, table = attn_queries(
        normed_two, attn_w, rel_rows, small, span, ker, []
    )
    normed_one = regroup([normed_one], [width], after=attn_w[:1], name="carry_norm")
    first_tokens = [normed_one] + tensor_swaps(normed_one)
    mixed, probs, keys, vals, stream2, normed_three, edge_1, edge_3 = attn_main(
        place, tokens, attn_w, query_u, table, stream1, norms, []
    )
    hidden, slope, normed_t = ffn1_hidden(place, first_tokens, first_w, units, [stream2])
    swaps, halves = plane_swaps(second_block, [stream2], "halves_second")
    second_blocks = [second_block] + swaps
    gated, value_half, logistic, depth, sums, *packs = conv_forward(
        place, normed_three, swap(edge_1, "tensor", 1), swap(edge_3, "tensor", 3), attn_w,
        5 * channels // LANES, small, ker, [hidden, halves[0]],
    )
    second_w = core_swap(second_blocks, after=[sums], name="rows_second")
    sums, *depth_edges = sum_tensor(place, sums, [packs[0], sums, packs[1]], "sums_forward")
    sums, block_out, keep, send, out_keep, out_send, stream_grad, ngrad, totals, *packs, norm_sums_4 = turn(
        place, stream2, depth, sum_dp(sums), norms, small, ker, attn_w, second_w, cotangent
    )
    other = core_other(send)
    block_out = dot(block_out, order, ((1,), (1,))).astype(BF)
    totals, *ngrad_edges = sum_tensor(place, totals, [packs[0], totals, packs[1]], "sums_back")
    conv_keep, conv_send, taps_grad, stream_grad, gb, norm_sums_2, totals = conv_backward(
        place, ngrad, ngrad_edges, depth, depth_edges, sums, sum_dp(totals), small, ker, gated,
        value_half, logistic, normed_three, attn_w, 5 * channels // LANES, out_keep, out_send, stream_grad, stream2, norms, [other],
    )
    second_parts = reduce_core_pairs(
        [(keep, other), (conv_keep, core_other(conv_send))], "core_second"
    )
    came = plane_first(second_parts)
    gp, dk, dv, own_keys, *others = attn_back_keys(
        place, gb, attn_w, probs, keys, vals, query_u, size_t, [second_parts[1], block_out]
    )
    others = [swap(o, "tensor", m) for m, o in enumerate(others, 1)]
    second_parts = plane_second(second_parts, came, [own_keys], "plane_second")
    plane_done = second_parts[4:]
    second_parts = second_parts[:4]
    keeps, sends, own = attn_back_queries(
        gp, keys, positions, query_v, dk, dv, mixed, gb, normed_two, tokens, rel_rows, attn_w,
        taps_grad, plane_done,
    )
    attn_parts = reduce_core_pieces(keeps, sends, 16, "core_attn")
    came = plane_first(attn_parts)
    stream_grad, gb, norm_sums_1 = ffn1_branch_grad(
        sum_parts([own_keys, own, *others], "sum_normed"), stream_grad, stream1, norms,
        [],
    )
    input_grad, norm_rows, gb = ffn1_back_tokens(
        stream_grad, gb, stream0, norms, inner_one, first_w,
        [norm_sums_1, norm_sums_2, norm_sums_4], attn_parts[1:2],
    )
    gb_all = lax.all_gather(gb, "tensor", axis=0, tiled=True)
    attn_parts = plane_second(attn_parts, came, [gb_all], "plane_attn")
    plane_done, attn_parts = attn_parts[4:], attn_parts[:4]
    keep, send = ffn1_back_weights(gb_all, hidden, slope, normed_t, first_w, norm_rows, [*second_parts[1:3], *plane_done])
    first_parts = reduce_core_pairs([(keep, core_other(send))], "core_ffn1")
    core_done = first_parts[1:2]
    first_parts = plane_second(first_parts, plane_first(first_parts), name="plane_ffn1")[:4]
    widths = [units, units, 2 * part, part]
    second_cuts = reduce_split(second_parts, widths, after=core_done, name="split_second")
    flat, square = (shard, part), (shard, units)

    def pick(total):
        wide, out, pair, conv = cut_columns(total, widths)
        return [wide, out, pair[:, :part], pair[:, part:], conv]

    second_in_grad, second_out_grad, values_grad, gates_grad, outs_grad = finish(
        second_cuts, [square, square, flat, flat, flat], pick, "finish_second"
    )
    first_sum = first_parts[0] + sum(p.astype(F32) for p in first_parts[1:3])
    first_in_grad, first_out_grad, norm_cols = cut_columns(first_sum, [units, units, LANES])
    attn_cuts = reduce_split(attn_parts, [part] * 5, norm_cols, name="split_attn")

    def pick(total):
        columns = cut_columns(total, [part] * 5 + [LANES])
        norms = columns[5][:shard].T
        taps = jnp.concatenate([columns[0][shard:], columns[1][shard:]], 0)
        grads = [c[:shard] for c in columns[:5]]
        return grads + [norms[0:5], norms[5:10], taps[:ker], columns[2][shard : shard + 2]]

    query_grad, key_grad, value_grad, pos_grad, attn_grad, gain_grad, beta_grad, taps_grad, bias_grad = finish(
        attn_cuts, [flat] * 5 + [(5, shard), (5, shard), (ker, part), (2, part)], pick, "finish_attn"
    )

    input_grad = dot(input_grad, order.astype(F32), ((1,), (1,)), precision=HIGHEST)
    return (
        block_out[None],
        input_grad[None],
        gain_grad,
        beta_grad,
        first_in_grad,
        first_out_grad.T,
        query_grad,
        key_grad,
        value_grad,
        pos_grad,
        attn_grad.T,
        bias_grad,
        values_grad,
        gates_grad,
        taps_grad,
        totals[1, :part],
        totals[0, :part],
        outs_grad.T,
        second_in_grad,
        second_out_grad.T,
    )


def solution(mesh):
    return jax.shard_map(
        on_device,
        mesh=mesh,
        in_specs=(
            P("dp", "tensor", None),
            P("dp"),
            P(),
            P("dp", "tensor", None),
            P(None, "dp"),
            P(None, "dp"),
            P("dp", "tensor"),
            P("tensor", "dp"),
            P("dp", "tensor"),
            P("dp", "tensor"),
            P("dp", "tensor"),
            P("dp", "tensor"),
            P("tensor", "dp"),
            P(None, "tensor"),
            P("dp", "tensor"),
            P("dp", "tensor"),
            P(None, "tensor"),
            P("tensor"),
            P("tensor"),
            P("tensor", "dp"),
            P("dp", "tensor"),
            P("tensor", "dp"),
        ),
        out_specs=(
            P("dp", "tensor", None),
            P("dp", "tensor", None),
            P(None, "dp"),
            P(None, "dp"),
            P("dp", "tensor"),
            P("tensor", "dp"),
            P("dp", "tensor"),
            P("dp", "tensor"),
            P("dp", "tensor"),
            P("dp", "tensor"),
            P("tensor", "dp"),
            P(None, "tensor"),
            P("dp", "tensor"),
            P("dp", "tensor"),
            P(None, "tensor"),
            P("tensor"),
            P("tensor"),
            P("tensor", "dp"),
            P("dp", "tensor"),
            P("tensor", "dp"),
        ),
        check_vma=False,
    )
```

```python
import math

import jax
import jax.numpy as jnp
from jax import lax
from jax.experimental import pallas as pl
from jax.experimental.pallas import tpu as pltpu
from jax.sharding import PartitionSpec as P

DH = 64
LANES = 128
HALO = 16
EPS = 1e-05
NEG = -1000000000.0
HIGHEST = lax.Precision.HIGHEST
BF = jnp.bfloat16
F32 = jnp.float32


def dot(left, right, dims=((1,), (0,)), **kw):
    return lax.dot_general(left, right, (dims, ((), ())), preferred_element_type=F32, **kw)


def dot_t(left, right):
    return dot(left, right, ((1,), (1,)))


def swap(values, axis, mask):
    return lax.ppermute(values, axis, [(i, i ^ mask) for i in range(lax.axis_size(axis))])


def dp_plan():
    size = lax.axis_size("dp")
    chips = [m for m in (0, 2, 4, 6) if m < size]
    doublings = [1] + [1 << b for b in range(3, 20) if 1 << b < size]
    return chips, doublings


def run(kernel, ins, outs, scratch=(), grid=(1,), aliases=None, after=(), micros=3, limit=8, name=None):
    count = len(ins)

    def body(*refs):
        kernel(*refs[:count], *refs[count + len(after) :])

    def whole(shape):
        return pl.BlockSpec(
            tuple(shape), lambda g: (0,) * len(shape), pipeline_mode=pl.Buffered(1)
        )

    def held(shape, dtype, spec):
        if spec is None:
            return math.prod(shape) * jnp.dtype(dtype).itemsize
        if spec.block_shape is None:
            return 0
        buffers = 1 if spec.pipeline_mode is not None else 2
        return buffers * math.prod(spec.block_shape) * jnp.dtype(dtype).itemsize

    need = sum(held(a.shape, a.dtype, spec) for a, spec in ins)
    need += sum(held(*out) for out in outs)
    need += sum(math.prod(r.shape) * jnp.dtype(r.dtype).itemsize for r in scratch)
    limit = need // 2**20 + 1 + limit
    return pl.pallas_call(
        body,
        grid=grid,
        in_specs=[spec or whole(a.shape) for a, spec in ins] + [ANY] * len(after),
        out_specs=[spec or whole(s) for s, _, spec in outs],
        out_shape=[jax.ShapeDtypeStruct(s, d) for s, d, _ in outs],
        scratch_shapes=list(scratch),
        input_output_aliases=aliases or {},
        compiler_params=pltpu.CompilerParams(vmem_limit_bytes=limit * 1024 * 1024),
        cost_estimate=pl.CostEstimate(
            flops=int(micros * 1e9), bytes_accessed=int(micros * 3.0e6), transcendentals=0
        ),
        name=name,
    )(*[a for a, _ in ins], *after)


SMEM = pl.BlockSpec(memory_space=pltpu.SMEM)
ANY = pl.BlockSpec(memory_space=pl.ANY)


def column(rows, offset=0):
    return pl.BlockSpec((rows, LANES), lambda g: (0, offset + g))


def heads(pairs, rows, span):
    return pl.BlockSpec((pairs, rows, span), lambda g: (g, 0, 0))


def regroup(blocks, widths, extras=(), skip=0, after=(), name="regroup"):
    rows = blocks[0].shape[0]
    count, total = len(blocks), sum(widths)

    def kernel(*refs):
        out, at, start = refs[-1], 0, skip
        for width in widths:
            for b in range(count):
                out[:, at : at + width] = refs[b][:, start : start + width]
                at += width
            start += width
        for ref in refs[count:-1]:
            out[:, at : at + ref.shape[1]] = ref[...]
            at += ref.shape[1]

    columns = count * total + sum(e.shape[1] for e in extras)
    return run(
        kernel, [(b, None) for b in (*blocks, *extras)], [((rows, columns), BF, None)],
        after=after, micros=1, name=name,
    )[0]


def stack_rows(pieces, after=(), name="stack_rows"):
    if any(p.shape[0] % 16 for p in pieces):
        return jnp.concatenate(pieces, 0)
    total = sum(p.shape[0] for p in pieces)

    def kernel(*refs):
        at = 0
        for ref in refs[:-1]:
            refs[-1][at : at + ref.shape[0], :] = ref[...]
            at += ref.shape[0]

    return run(
        kernel, [(p, None) for p in pieces], [((total, pieces[0].shape[1]), BF, None)],
        after=after, micros=1.5, name=name,
    )[0]


def tensor_swaps(block):
    return [swap(block, "tensor", m) for m in range(1, lax.axis_size("tensor"))]


def chip_swaps(block):
    chips, _ = dp_plan()
    return [swap(block, "dp", m) for m in chips[1:]]


def plane_swaps(block, after=(), name="plane_halves"):
    half, columns = block.shape[0] // 2, block.shape[1]
    by_x, by_y = swap(block, "dp", 2), swap(block, "dp", 4)
    if half % 16:
        top, low = by_x[:half], by_y[half:]
    else:

        def kernel(x_ref, y_ref, top_ref, low_ref):
            top_ref[...] = x_ref[:half, :]
            low_ref[...] = y_ref[half:, :]

        top, low = run(
            kernel, [(by_x, None), (by_y, None)], [((half, columns), BF, None)] * 2,
            after=after, micros=1, name=name,
        )
    return [by_x, by_y, swap(top, "dp", 4), swap(low, "dp", 2)], [top, low]


def core_swap(pieces, after=(), name="stack_rows"):
    _, doublings = dp_plan()
    rows = stack_rows(pieces, after, name)
    for step in doublings[:-1]:
        rows = jnp.concatenate([rows, swap(rows, "dp", step)], 0)
    return rows, swap(rows, "dp", doublings[-1])


def core_other(send):
    _, doublings = dp_plan()
    return swap(send, "dp", doublings[-1])


def reduce_rest(keep, other, extra):
    _, doublings = dp_plan()
    for step in doublings[-2::-1]:
        both = (keep.astype(F32) + other.astype(F32)).astype(BF)
        main, tail = both[: both.shape[0] - extra], both[both.shape[0] - extra :]
        half = main.shape[0] // 2
        keep = jnp.concatenate([main[:half], tail], 0)
        other = swap(jnp.concatenate([main[half:], tail], 0), "dp", step)
    return keep, other


def reduce_core(arrays, sources, rows, columns, extra=0, name="reduce_core"):
    half = rows // 2

    def pieces(refs):
        for i, parts in enumerate(sources):
            for kept, received, row, at in parts:
                a, b = refs[kept], refs[received]
                value = a[row : row + rows, :].astype(F32) + b[row : row + rows, :].astype(F32)
                tail = None
                if extra:
                    kept, received, row, _ = sources[0][0]
                    a, b = refs[kept], refs[received]
                    first = a.shape[0] - extra
                    tail = a[first:, :].astype(F32) + b[first:, :].astype(F32)
                yield i, slice(at, at + value.shape[1]), value, tail

    shapes = [(rows + extra, F32), (rows, BF), (rows + extra, BF), (half + extra, BF), (half, BF)]
    if rows % 32:
        outs = [[] for _ in shapes]
        for i, _, value, tail in pieces(arrays):
            under = (lambda v: jnp.concatenate([v, tail], 0)) if extra else (lambda v: v)
            for out, part in {
                0: [(0, under(value))],
                1: [(1, value)],
                2: [(2, under(value))],
                3: [(3, under(value[:half])), (4, value[half:])],
            }[i]:
                outs[out].append(part)
        return [jnp.concatenate(o, 1).astype(d) for o, (_, d) in zip(outs, shapes)]

    def kernel(*refs):
        outs = refs[len(arrays) :]
        for i, cols, value, tail in pieces(refs):
            if i == 3:
                outs[3][:half, cols] = value[:half].astype(BF)
                outs[4][:, cols] = value[half:].astype(BF)
            else:
                outs[i][:rows, cols] = value.astype(outs[i].dtype)
            if extra and i in (0, 2):
                outs[i][rows:, cols] = tail.astype(outs[i].dtype)
            if extra and i == 3:
                outs[3][half:, cols] = tail.astype(BF)

    return run(
        kernel, [(x, None) for x in arrays], [((r, columns), d, None) for r, d in shapes],
        micros=2.5, name=name,
    )


def reduce_core_pairs(pairs, name):
    if len(dp_plan()[1]) > 1:
        pairs = [reduce_rest(*[jnp.concatenate(x, 1) for x in zip(*pairs)], 0)]
    rows = pairs[0][0].shape[0] // 4
    starts = [sum(p[0].shape[1] for p in pairs[:n]) for n in range(len(pairs))]
    sources = [
        [(2 * n, 2 * n + 1, i * rows, at) for n, at in enumerate(starts)] for i in range(4)
    ]
    columns = sum(p[0].shape[1] for p in pairs)
    return reduce_core([x for p in pairs for x in p], sources, rows, columns, name=name)


def reduce_core_pieces(keeps, sends, extra, name):
    if len(dp_plan()[1]) > 1:
        keep, send = [
            jnp.concatenate([p[: p.shape[0] - (0 if i else extra)] for i, p in enumerate(x)] + [x[0][-extra:]], 0)
            for x in (keeps, sends)
        ]
        keep, other = reduce_rest(keep, core_other(send), extra)
        rows = (keep.shape[0] - extra) // 4
        sources = [[(0, 1, i * rows, 0)] for i in range(4)]
        return reduce_core([keep, other], sources, rows, keep.shape[1], extra, name)
    rows, columns = keeps[1].shape
    sources = [[(i, 4 + i, 0, 0)] for i in range(4)]
    return reduce_core(
        [*keeps, *[core_other(x) for x in sends]], sources, rows, columns, extra, name
    )


def plane_first(parts):
    return swap(parts[3], "dp", 2), swap(parts[4], "dp", 4)


def plane_second(parts, came, after=(), name="plane_second"):
    own, x, y, _, _ = parts
    rows, extra, columns = x.shape[0], own.shape[0] - x.shape[0], x.shape[1]
    half = rows // 2

    def added(x, y, by_x, by_y):
        low = x[half:, :].astype(F32) + by_y[...].astype(F32)
        top = y[:half, :].astype(F32) + by_x[:half, :].astype(F32)
        tail = y[rows:, :].astype(F32) + by_x[half:, :].astype(F32) if extra else None
        return low.astype(BF), top.astype(BF), tail

    if rows % 32:
        low, top, tail = added(x, y, *came)
        x = jnp.concatenate([x[:half], low], 0)
        y = jnp.concatenate([top, y[half:rows]] + ([tail.astype(BF)] if extra else []), 0)
    else:

        def kernel(x_ref, y_ref, by_x_ref, by_y_ref, x_out, y_out):
            low, top, tail = added(x_ref, y_ref, by_x_ref, by_y_ref)
            x_out[:half, :] = x_ref[:half, :]
            x_out[half:, :] = low
            y_out[:half, :] = top
            y_out[half:rows, :] = y_ref[half:rows, :]
            if extra:
                y_out[rows:, :] = tail.astype(BF)

        x, y = run(
            kernel, [(v, None) for v in (x, y, *came)],
            [((rows, columns), BF, None), ((rows + extra, columns), BF, None)],
            after=after, micros=1.5, name=name,
        )
    return [own, swap(y, "dp", 4), swap(x, "dp", 2), came[0], x]


def reduce_split(parts, widths, shared=None, after=(), name="reduce_split"):
    size = lax.axis_size("tensor")
    rows, extra = parts[2].shape[0], parts[0].shape[0] - parts[2].shape[0]
    half = rows // 2

    def kernel(own_ref, y_ref, x_ref, came_ref, *refs):
        totals = [own_ref[:rows, :] + x_ref[...].astype(F32) + y_ref[:rows, :].astype(F32)]
        if extra:
            tail = own_ref[rows:, :] + y_ref[rows:, :].astype(F32)
            totals.append(tail + came_ref[half:, :].astype(F32))
        for mask in range(size):
            out = refs[mask - size]
            for total, first in zip(totals, (0, rows)):
                at, start, under = 0, 0, slice(first, first + total.shape[0])
                for width in widths:
                    cut = total[:, start + mask * width : start + (mask + 1) * width]
                    out[under, at : at + width] = cut.astype(out.dtype)
                    at += width
                    start += size * width
            if shared is not None:
                out[:rows, at:] = refs[0][...].astype(out.dtype)
                out[rows:, at:] = jnp.zeros((extra, LANES), out.dtype)

    more = [] if shared is None else [shared]
    return run(
        kernel, [(p, None) for p in (*parts, *more)],
        [((rows + extra, sum(widths) + LANES * len(more)), F32 if m == 0 else BF, None) for m in range(size)],
        after=after, micros=1.5, name=name,
    )


def finish(cuts, shapes, pick, name):
    came = [swap(cut, "tensor", mask) for mask, cut in enumerate(cuts[1:], 1)]
    count = len(cuts)

    def kernel(*refs):
        total = refs[0][...]
        for r in refs[1:count]:
            total = total + r[...].astype(F32)
        for out, value in zip(refs[count:], pick(total)):
            out[...] = value

    return run(
        kernel, [(cuts[0], None)] + [(c, None) for c in came], [(s, F32, None) for s in shapes],
        micros=1, name=name,
    )


def cut_columns(total, widths):
    parts, at = [], 0
    for width in widths:
        parts.append(total[:, at : at + width])
        at += width
    return parts


def reduce_tensor(cuts):
    total = cuts[0]
    for mask in range(1, len(cuts)):
        total = total + swap(cuts[mask], "tensor", mask).astype(F32)
    return total


def block_swap(values, mask):
    width = values.shape[1] // 4
    return jnp.concatenate(
        [values[:, (b ^ mask) * width : ((b ^ mask) + 1) * width] for b in range(4)], 1
    )


def edges_of(me, last, first):
    even = (me & 1) == 0
    return jnp.where(even, last, first), jnp.where(even, first, last)


def edges_from(me, by_1, by_3):
    even = (me & 1) == 0
    return jnp.where(even, by_3, by_1), jnp.where(even, by_1, by_3)


def sum_tensor(place, own, packs, name):
    by_1, by_2, by_3 = [swap(p, "tensor", m) for m, p in enumerate(packs, 1)]
    columns = own.shape[1]

    def kernel(place_ref, own_ref, one_ref, two_ref, three_ref, sums_ref, before_ref, after_ref):
        one, three = block_swap(one_ref[...], 1), block_swap(three_ref[...], 3)
        sums_ref[...] = own_ref[...] + one[:8] + block_swap(two_ref[...], 2) + three[:8]
        before_ref[...], after_ref[...] = edges_from(place_ref[0], one[8:], three[8:])

    return run(
        kernel, [(place, SMEM), (own, None), (by_1, None), (by_2, None), (by_3, None)],
        [((8, columns), F32, None)] + [((HALO, columns), F32, None)] * 2,
        micros=1, name=name,
    )


def sum_dp(total):
    _, doublings = dp_plan()
    for step in doublings:
        total = total + swap(total, "dp", step)
    return [total] + chip_swaps(total)


def norm(stream, gain, beta_row):
    centered = stream - jnp.mean(stream, -1, keepdims=True)
    inv_std = lax.rsqrt(jnp.mean(centered * centered, -1, keepdims=True) + EPS)
    scaled = centered * inv_std
    return scaled * gain + beta_row, scaled, inv_std


def norm_back(upstream, stream, gain):
    centered = stream - jnp.mean(stream, -1, keepdims=True)
    inv_std = lax.rsqrt(jnp.mean(centered * centered, -1, keepdims=True) + EPS)
    scaled = centered * inv_std
    grad = upstream * gain
    out = inv_std * (
        grad - jnp.mean(grad, -1, keepdims=True) - scaled * jnp.mean(grad * scaled, -1, keepdims=True)
    )
    return out, jnp.sum(upstream * scaled, 0, keepdims=True), jnp.sum(upstream, 0, keepdims=True)


def swish_slope(inner_act):
    logistic = jax.nn.sigmoid(inner_act)
    return logistic * (1.0 + inner_act * (1.0 - logistic))


def lanes_of(h, rows):
    lane = lax.broadcasted_iota(jnp.int32, (rows, LANES), 1)
    return (lane >= h * DH) & (lane < (h + 1) * DH)


def both(a_ref, b_ref):
    return jnp.concatenate([a_ref[...], b_ref[...]], 0)


def beside(left, right):
    return jnp.concatenate([left, right], 1)


def ordered_rows(me, block, rows):
    return pl.ds(pl.multiple_of((me ^ block) * rows, 64), rows)


def channel_sums(rows, count=8):
    return jnp.concatenate(rows + [jnp.zeros((count - len(rows), rows[0].shape[1]), F32)], 0)


def first_norm(stream, columns):
    rows, width = stream.shape
    half = width // 2

    def kernel(stream_ref, a_ref, b_ref, norms_ref, normed_ref):
        for ref, at in ((a_ref, 0), (b_ref, half)):
            norms_ref[:, at : at + half] = ref[...].astype(F32).T[:16]
        normed = norm(stream_ref[...], norms_ref[0:1, :], norms_ref[5:6, :])[0]
        normed_ref[...] = normed.astype(BF)

    return run(
        kernel, [(stream, None), (columns[0], None), (columns[1], None)],
        [((16, width), F32, None), ((rows, width), BF, None)], micros=1, name="first_norm",
    )


def ffn1_forward(stream, normed, halves, norms, after):
    rows, width = stream.shape
    half = width // 2
    hidden_units = halves[0].shape[1] // 2

    def kernel(stream_ref, normed_ref, a_ref, b_ref, norms_ref, slope_ref, out_ref, next_ref):
        normed = normed_ref[...]
        low = jnp.zeros((rows, half), F32)
        high = jnp.zeros((rows, half), F32)
        for j in range(0, hidden_units, 512):
            at = slice(j, j + 512)
            after = slice(hidden_units + j, hidden_units + j + 512)
            inner = dot(normed[:, :half], a_ref[:, at]) + dot(normed[:, half:], b_ref[:, at])
            logistic = jax.nn.sigmoid(inner)
            slope_ref[:, at] = logistic * (1.0 + inner * (1.0 - logistic))
            hidden = (inner * logistic).astype(BF)
            low = low + dot_t(hidden, a_ref[:, after])
            high = high + dot_t(hidden, b_ref[:, after])
        out = stream_ref[...] + 0.5 * jnp.concatenate([low, high], 1)
        out_ref[...] = out
        next_ref[...] = norm(out, norms_ref[1:2, :], norms_ref[6:7, :])[0].astype(BF)

    return run(
        kernel, [(x, None) for x in (stream, normed, *halves, norms)],
        [((rows, hidden_units), F32, None), ((rows, width), F32, None), ((rows, width), BF, None)],
        after=after, micros=4, name="ffn1_forward",
    )


def ffn1_hidden(place, blocks, halves, units, after):
    rows, width = blocks[0].shape
    half, count = width // 2, len(blocks)
    span = count * rows

    def kernel(place_ref, a_ref, b_ref, *refs):
        hidden_ref, slope_ref, normed_t_ref, ordered = refs[count:]
        for b in range(count):
            normed = refs[b][...]
            at = ordered_rows(place_ref[0], b, rows)
            inner = dot(normed[:, :half], a_ref[...]) + dot(normed[:, half:], b_ref[...])
            logistic = jax.nn.sigmoid(inner)
            hidden_ref[at, :] = (inner * logistic).astype(BF)
            slope_ref[at, :] = logistic * (1.0 + inner * (1.0 - logistic))
            ordered[at, :] = normed
        normed_t_ref[...] = ordered[...].T

    own = pl.BlockSpec((half, units), lambda g: (0, 0), pipeline_mode=pl.Buffered(1))
    return run(
        kernel, [(place, SMEM)] + [(x, own) for x in halves] + [(x, None) for x in blocks],
        [((span, units), BF, None), ((span, units), F32, None), ((width, span), BF, None)],
        scratch=[pltpu.VMEM((span, width), BF)], after=after, micros=2, name="ffn1_hidden",
    )


def sum_parts(parts, name):
    def kernel(*refs):
        refs[-1][...] = sum(r[...].astype(F32) for r in refs[:-1])

    return run(kernel, [(p, None) for p in parts], [(parts[0].shape, F32, None)], micros=6, name=name)[0]


def ffn1_branch_grad(upstream, stream_grad, stream, norms, after):
    rows, width = stream.shape

    def kernel(upstream_ref, grad_ref, stream_ref, norms_ref, out_ref, gb_ref, sums_ref):
        extra, dgain, dbeta = norm_back(upstream_ref[...], stream_ref[...], norms_ref[1:2, :])
        sums_ref[...] = channel_sums([dgain, dbeta])
        out = grad_ref[...] + extra
        out_ref[...] = out
        gb_ref[...] = (0.5 * out).astype(BF)

    return run(
        kernel, [(x, None) for x in (upstream, stream_grad, stream, norms)],
        [((rows, width), F32, None), ((rows, width), BF, None), ((8, width), F32, None)],
        after=after, micros=1.5, name="ffn1_branch_grad",
    )


def ffn1_back_tokens(stream_grad, gb, stream, norms, inner, halves, sums, after):
    rows, width = stream.shape
    hidden_units = inner.shape[1]
    half = width // 2

    def kernel(grad_ref, gb_ref, stream_ref, norms_ref, slope_ref, a_ref, b_ref, s1_ref, s2_ref, s4_ref,
               out_ref, norm_rows_ref, gb_out_ref):
        gb = gb_ref[...]
        gb_out_ref[...] = gb
        low = jnp.zeros((rows, half), F32)
        high = jnp.zeros((rows, half), F32)
        for j in range(0, hidden_units, 512):
            at = slice(j, j + 512)
            after = slice(hidden_units + j, hidden_units + j + 512)
            grad = dot(gb[:, :half], a_ref[:, after]) + dot(gb[:, half:], b_ref[:, after])
            grad = (grad * slope_ref[:, at]).astype(BF)
            low = low + dot_t(grad, a_ref[:, at])
            high = high + dot_t(grad, b_ref[:, at])
        extra, dgain, dbeta = norm_back(
            jnp.concatenate([low, high], 1), stream_ref[...], norms_ref[0:1, :]
        )
        gains = [dgain, s1_ref[0:1, :], s2_ref[0:1, :], s4_ref[0:1, :], s4_ref[2:3, :]]
        betas = [dbeta, s1_ref[1:2, :], s2_ref[1:2, :], s4_ref[1:2, :], s4_ref[3:4, :]]
        norm_rows_ref[...] = channel_sums(gains + betas, 16)
        out_ref[...] = grad_ref[...] + extra

    ins = [stream_grad, gb, stream, norms, inner, *halves, *sums]
    return run(
        kernel, [(x, None) for x in ins],
        [((rows, width), F32, None), ((16, width), F32, None), ((rows, width), BF, None)],
        after=after, micros=5, name="ffn1_back_tokens",
    )


def ffn1_back_weights(gb, hidden, slope, normed_t, halves, norm_rows, after):
    width, span = normed_t.shape
    units, half = hidden.shape[1], width // 2

    def kernel(gb_ref, hidden_ref, slope_ref, normed_t_ref, a_ref, b_ref, norm_ref, keep_ref, send_ref):
        gb = gb_ref[...]
        grad = dot(gb[:, :half], a_ref[...]) + dot(gb[:, half:], b_ref[...])
        grad = (grad * slope_ref[...]).astype(BF)
        columns = jnp.concatenate([norm_ref[...], jnp.zeros((LANES - 16, width), F32)], 0).T
        grads = [dot(normed_t_ref[...], grad), dot(gb.T, hidden_ref[...]), columns]
        at = 0
        for g in grads:
            keep_ref[:, at : at + g.shape[1]] = g[:half].astype(BF)
            send_ref[:, at : at + g.shape[1]] = g[half:].astype(BF)
            at += g.shape[1]

    first = halves[0].shape[1] // (2 * units)
    own = pl.BlockSpec((half, units), lambda g: (0, first), pipeline_mode=pl.Buffered(1))
    total = 2 * units + LANES
    return run(
        kernel,
        [(gb, None), (hidden, None), (slope, None), (normed_t, None), (halves[0], own), (halves[1], own), (norm_rows, None)],
        [((half, total), BF, None), ((half, total), BF, None)],
        after=after, micros=4, name="ffn1_back_weights",
    )


def attn_queries(normed, halves, rel_rows, small, span, bias_row, after):
    rows, width = normed.shape
    wide, columns = rel_rows.shape[0], small.shape[1]
    groups, pairs = columns // LANES, LANES // DH
    half = width // 2

    def kernel(rows_ref, aq_ref, bq_ref, ap_ref, bp_ref, rel_ref, small_ref, qu_ref, qv_ref, pos_ref, table_ref):
        queries = dot(rows_ref[...], both(aq_ref, bq_ref))
        bias = small_ref[...].astype(F32)
        qu_ref[...] = (queries + bias[bias_row : bias_row + 1]).astype(BF)
        query_v = (queries + bias[bias_row + 1 : bias_row + 2]).astype(BF)
        qv_ref[...] = query_v
        positions = dot(rel_ref[...], both(ap_ref, bp_ref)).astype(BF)
        pos_ref[...] = positions
        for h in range(pairs):
            mine = jnp.where(lanes_of(h, rows), query_v * DH ** (-0.5), jnp.zeros_like(query_v))
            table = dot_t(mine, positions)
            shifted = pltpu.roll(table, wide - (rows - 1), 1, stride=1, stride_axis=0)
            table_ref[h] = shifted[:, :span]

    def weight(i):
        return column(half, i * groups)

    a, b = halves
    return run(
        kernel,
        [(normed, None), (a, weight(0)), (b, weight(0)), (a, weight(3)), (b, weight(3)), (rel_rows, None), (small, column(small.shape[0]))],
        [((rows, columns), BF, column(rows)), ((rows, columns), BF, column(rows)), ((wide, columns), BF, column(wide)),
         ((groups * pairs, rows, span), F32, heads(pairs, rows, span))],
        grid=(groups,), after=after, micros=0.5, name="attn_queries",
    )


def attn_main(place, tokens, halves, query_u, table, stream, norms, after):
    rows, width = stream.shape
    span, columns = table.shape[2], query_u.shape[1]
    groups, pairs = columns // LANES, LANES // DH
    half = width // 2

    def kernel(place_ref, rows_ref, *refs):
        (ak_ref, bk_ref, av_ref, bv_ref, ao_ref, bo_ref, qu_ref, table_ref, stream_ref, norms_ref,
         mixed_ref, probs_ref, keys_ref, vals_ref, out_ref, normed_ref, edge_1_ref, edge_3_ref) = refs
        me, length = place_ref[0], place_ref[1]
        pair = dot(rows_ref[...], beside(both(ak_ref, bk_ref), both(av_ref, bv_ref))).astype(BF)
        keys, vals = pair[:, :LANES], pair[:, LANES:]
        keys_ref[...], vals_ref[...], query_u = keys, vals, qu_ref[...]
        scaled_u = query_u * DH ** (-0.5)
        visible = lax.broadcasted_iota(jnp.int32, (rows, span), 1) < length
        mixed = jnp.zeros((rows, LANES), F32)
        for h in range(pairs):
            mine = lanes_of(h, rows)
            content = dot_t(jnp.where(mine, scaled_u, jnp.zeros_like(scaled_u)), keys)
            scores = jnp.where(visible, content + table_ref[h], NEG)
            exponent = jnp.exp(scores - jnp.max(scores, -1, keepdims=True))
            probs = exponent * (1.0 / jnp.sum(exponent, -1, keepdims=True))
            probs_ref[h] = probs
            mixed = jnp.where(mine, dot(probs.astype(BF), vals), mixed)
        mixed = mixed.astype(BF)
        mixed_ref[...] = mixed

        @pl.when(pl.program_id(0) == 0)
        def _():
            out_ref[...] = stream_ref[...]

        out_ref[...] += dot_t(mixed, both(ao_ref, bo_ref))

        @pl.when(pl.program_id(0) == groups - 1)
        def _():
            normed = norm(out_ref[...], norms_ref[2:3, :], norms_ref[7:8, :])[0].astype(BF)
            normed_ref[...] = normed
            edge_1_ref[...], edge_3_ref[...] = edges_of(me, normed[rows - HALO :], normed[:HALO])

    def weight(i):
        return column(half, i * groups)

    a, b = halves
    return run(
        kernel,
        [(place, SMEM), (tokens, None)] + [(w, weight(i)) for i in (1, 2, 4) for w in (a, b)]
        + [(query_u, column(rows)), (table, heads(pairs, rows, span)), (stream, None), (norms, None)],
        [((rows, columns), BF, column(rows)), ((groups * pairs, rows, span), F32, heads(pairs, rows, span)),
         ((span, columns), BF, column(span)), ((span, columns), BF, column(span)),
         ((rows, width), F32, None), ((rows, width), BF, None), ((HALO, width), BF, None), ((HALO, width), BF, None)],
        grid=(groups,), after=after, micros=0.2, name="attn_main",
    )


def attn_back_keys(place, gb, halves, probs, keys, vals, query_u, count, after):
    rows, width = gb.shape
    span, columns = keys.shape
    groups, pairs = columns // LANES, LANES // DH
    half = width // 2

    def kernel(place_ref, gb_ref, ao_ref, bo_ref, ak_ref, bk_ref, av_ref, bv_ref, probs_ref, keys_ref, vals_ref, qu_ref,
               gp_ref, dk_ref, dv_ref, own_ref, *refs):
        other_refs, total = refs[:-1], refs[-1]
        me = place_ref[0]
        step = pl.program_id(0)
        gm = dot(gb_ref[...], both(ao_ref, bo_ref)).astype(BF)
        gm_t, qu_t = gm.T, qu_ref[...].T
        vals = vals_ref[...]
        dk_t, dv_t = [], []
        for h in range(pairs):
            head = slice(h * DH, (h + 1) * DH)
            probs = probs_ref[h]
            mine = jnp.where(lanes_of(h, rows), gm * DH ** (-0.5), jnp.zeros_like(gm))
            dprobs = dot_t(mine, vals)
            delta = jnp.sum(dprobs * probs, -1, keepdims=True)
            gp = (probs * (dprobs - delta)).astype(BF)
            gp_ref[h] = gp
            dv_t.append(dot(gm_t[head], probs.astype(BF)))
            dk_t.append(dot(qu_t[head], gp))
        dk = jnp.concatenate(dk_t, 0).T.astype(BF)
        dv = jnp.concatenate(dv_t, 0).T.astype(BF)
        dk_ref[...] = dk
        dv_ref[...] = dv
        grad = dot_t(beside(dk, dv), beside(both(ak_ref, bk_ref), both(av_ref, bv_ref)))

        @pl.when(step == 0)
        def _():
            total[...] = grad

        @pl.when(step > 0)
        def _():
            total[...] += grad

        @pl.when(step == groups - 1)
        def _():
            own_ref[...] = total[ordered_rows(me, 0, rows), :]
            for b in range(1, count):
                other_refs[b - 1][...] = total[ordered_rows(me, b, rows), :].astype(BF)

    def weight(i):
        return column(half, i * groups)

    a, b = halves
    return run(
        kernel,
        [(place, SMEM), (gb, None)] + [(w, weight(i)) for i in (4, 1, 2) for w in (a, b)]
        + [(probs, heads(pairs, rows, span)), (keys, column(span)), (vals, column(span)), (query_u, column(rows))],
        [((groups * pairs, rows, span), BF, heads(pairs, rows, span)), ((span, columns), BF, column(span)), ((span, columns), BF, column(span)),
         ((rows, width), F32, None)] + [((rows, width), BF, None)] * (count - 1),
        scratch=[pltpu.VMEM((span, width), F32)],
        grid=(groups,), after=after, micros=11, name="attn_back_keys",
    )


def attn_back_queries(gp, keys, positions, query_v, dk, dv, mixed, gb, normed, tokens, rel_rows, halves, taps_grad, after):
    rows, width = gb.shape
    span, columns = keys.shape
    wide = rel_rows.shape[0]
    groups, pairs = columns // LANES, LANES // DH
    half, pieces = width // 2, 4
    size = half // pieces

    def kernel(gp_ref, keys_ref, pos_ref, qv_ref, dk_ref, dv_ref, mixed_ref, aq_ref, bq_ref, gb_ref, rel_ref, dtaps_ref, normed_ref, tokens_ref, *refs):
        piece_refs, (own_ref, normed_t, tokens_t, rel_t, gb_t) = refs[: 2 * pieces], refs[2 * pieces :]
        step = pl.program_id(0)

        @pl.when(step == 0)
        def _():
            normed_t[...] = normed_ref[...].T
            tokens_t[...] = tokens_ref[...].T
            rel_t[...] = rel_ref[...].T
            gb_t[...] = gb_ref[...].T
            own_ref[...] = jnp.zeros_like(own_ref)

        i = lax.broadcasted_iota(jnp.int32, (rows, rows), 0)
        j = lax.broadcasted_iota(jnp.int32, (rows, rows), 1)
        flip = jnp.where(i + j == rows - 1, 1.0, 0.0)
        flip_low = flip.astype(BF)
        keys, positions = keys_ref[...], pos_ref[...]
        qv_t = dot(flip_low, qv_ref[...]).astype(BF).T
        du = jnp.zeros((rows, LANES), F32)
        dv_rows = jnp.zeros((rows, LANES), F32)
        dp_t = []
        for h in range(pairs):
            mine = lanes_of(h, rows)
            gp = gp_ref[h]
            du = jnp.where(mine, dot(gp, keys), du)
            flipped = dot(flip_low, gp)
            table = jnp.concatenate([flipped, jnp.zeros((rows, wide - span), F32)], 1)
            table = pltpu.roll(table, 0, 1, stride=1, stride_axis=0).astype(BF)
            dp_t.append(dot(qv_t[h * DH : (h + 1) * DH], table))
            dv_rows = jnp.where(mine, dot(table, positions), dv_rows)
        dv_rows = dot(flip, dv_rows, precision=HIGHEST)
        bias = channel_sums(
            [jnp.sum(du, 0, keepdims=True), jnp.sum(dv_rows, 0, keepdims=True)], 16
        )
        nothing = jnp.zeros((16, LANES), F32)
        extras = [dtaps_ref[:16, :], dtaps_ref[16:, :], bias, nothing, nothing]
        dq = (du + dv_rows).astype(BF)
        dp = jnp.concatenate(dp_t, 0).T.astype(BF)
        own_ref[...] += dot_t(dq, both(aq_ref, bq_ref))
        pair = dot(tokens_t[...], beside(dk_ref[...], dv_ref[...]))
        grads = [
            dot(normed_t[...], dq),
            pair[:, :LANES],
            pair[:, LANES:],
            dot(rel_t[...], dp),
            dot(gb_t[...], mixed_ref[...]),
        ]
        for n, grad in enumerate(grads):
            at = pl.ds(pl.multiple_of((n * groups + step) * LANES, LANES), LANES)
            low = grad.astype(BF)
            for i, ref in enumerate(piece_refs):
                ref[:size, at] = low[i * size : (i + 1) * size]
                if i % pieces == 0:
                    ref[size:, at] = extras[n].astype(BF)

    a, b = halves
    outs = run(
        kernel,
        [(gp, heads(pairs, rows, span)), (keys, column(span)), (positions, column(wide)), (query_v, column(rows)),
         (dk, column(span)), (dv, column(span)), (mixed, column(rows)), (a, column(half)), (b, column(half)), (gb, None), (rel_rows, None), (taps_grad, column(32)),
         (normed, None), (tokens, None)],
        [((size + (0 if i % pieces else 16), 5 * columns), BF, None) for i in range(2 * pieces)] + [((rows, width), F32, None)],
        scratch=[pltpu.VMEM((width, rows), BF), pltpu.VMEM((width, span), BF), pltpu.VMEM((width, wide), BF), pltpu.VMEM((width, rows), BF)],
        grid=(groups,), after=after, micros=13, name="attn_back_queries",
    )
    return outs[:pieces], outs[pieces : 2 * pieces], outs[-1]


def joined(a_ref, b_ref, at):
    return jnp.concatenate([a_ref[:, at], b_ref[:, at]], 0)


def conv_forward(place, normed, by_1, by_3, halves, at, small, ker, after):
    rows, width = normed.shape
    columns = small.shape[1]
    groups, half, ext = columns // LANES, width // 2, rows + 2 * HALO

    def kernel(place_ref, rows_ref, one_ref, three_ref, av_ref, bv_ref, ag_ref, bg_ref, small_ref,
               gated_ref, value_ref, gate_ref, depth_ref, sums_ref, pack_1_ref, pack_3_ref):
        me, length, start = place_ref[0], place_ref[1], place_ref[2]
        before, after = edges_from(me, one_ref[...], three_ref[...])
        tokens = jnp.concatenate([before, rows_ref[...], after], 0)
        pair = dot(tokens, beside(both(av_ref, bv_ref), both(ag_ref, bg_ref)))
        value_half, logistic = pair[:, :LANES], jax.nn.sigmoid(pair[:, LANES:])
        token = start - HALO + lax.broadcasted_iota(jnp.int32, value_half.shape, 0)
        mask = jnp.where((token >= 0) & (token < length), 1.0, 0.0)
        gated_ref[...] = mask * value_half * logistic
        value_ref[...] = value_half[HALO : HALO + rows]
        gate_ref[...] = logistic[HALO : HALO + rows]
        taps = small_ref[...].astype(F32)
        depth = jnp.zeros((rows, LANES), F32)
        for k in range(ker):
            depth = depth + taps[k : k + 1, :] * gated_ref[k + 1 : k + 1 + rows, :]
        depth_ref[...] = depth
        mask = mask[HALO : HALO + rows]
        masked = depth * mask
        sums = channel_sums([jnp.sum(x, 0, keepdims=True) for x in (masked, masked * depth, mask)])
        sums_ref[...] = sums
        one, three = edges_of(me, depth[rows - HALO :], depth[:HALO])
        pack_1_ref[:8, :], pack_1_ref[8:, :] = sums, one
        pack_3_ref[:8, :], pack_3_ref[8:, :] = sums, three

    return run(
        kernel,
        [(place, SMEM), (normed, None), (by_1, None), (by_3, None)]
        + [(w, column(half, at + i * groups)) for i in (0, 1) for w in halves] + [(small, column(small.shape[0]))],
        [((ext, columns), F32, column(ext))] + [((rows, columns), F32, column(rows))] * 3
        + [((8, columns), F32, column(8))] + [((8 + HALO, columns), F32, column(8 + HALO))] * 2,
        grid=(groups,), after=after, micros=4, name="conv_forward",
    )


def batch_terms(sums_ref):
    count = sums_ref[2:3, :]
    mean = sums_ref[0:1, :] / count
    inv_std = lax.rsqrt(sums_ref[1:2, :] / count - mean * mean + EPS)
    return count, mean, inv_std


def turn(place, stream, depth, sums, norms, small, ker, conv_halves, halves, cotangent):
    rows, width = stream.shape
    columns = depth.shape[1]
    groups = columns // LANES
    half = width // 2
    hidden_units = halves[0].shape[1] // 2
    units = hidden_units // groups
    parts = len(sums)

    def kernel(place_ref, stream_ref, depth_ref, norms_ref, small_ref, ac_ref, bc_ref, ai_ref, bi_ref, ao_ref, bo_ref, cot_ref, *refs):
        (sums_ref, out_ref, keep_ref, send_ref, ckeep_ref, csend_ref, grad_ref, ngrad_ref, own_ref, pack_1_ref, pack_3_ref, nsums_ref,
         slope_ref, hidden_ref) = refs[parts:]
        sums_ref[...] = sum(r[...] for r in refs[:parts])
        _, mean, inv_std = batch_terms(sums_ref)
        batch_gain = small_ref[...].astype(F32)[ker + 2 : ker + 3]
        batch_bias = small_ref[...].astype(F32)[ker + 3 : ker + 4]
        scaled = (depth_ref[...] - mean) * inv_std
        normal = scaled * batch_gain + batch_bias
        active = jax.nn.silu(normal).astype(BF)
        wc = both(ac_ref, bc_ref)
        stream3 = stream_ref[...] + dot_t(active, wc)
        normed = norm(stream3, norms_ref[3:4, :], norms_ref[8:9, :])[0].astype(BF)
        branch = jnp.zeros((rows, width), F32)
        for p in range(groups):
            j = slice(p * units, (p + 1) * units)
            inner = dot(normed, joined(ai_ref, bi_ref, j))
            logistic = jax.nn.sigmoid(inner)
            slope_ref[:, j] = logistic * (1.0 + inner * (1.0 - logistic))
            hidden = (inner * logistic).astype(BF)
            hidden_ref[:, j] = hidden
            branch = branch + dot_t(hidden, joined(ao_ref, bo_ref, j))
        stream4 = stream3 + 0.5 * branch
        out_ref[...] = norm(stream4, norms_ref[4:5, :], norms_ref[9:10, :])[0].astype(BF)
        grad, gain5, beta5 = norm_back(cot_ref[...], stream4, norms_ref[4:5, :])
        gb = (0.5 * grad).astype(BF)
        gb_t, normed_t = gb.T, normed.T
        upstream = jnp.zeros((rows, width), F32)
        for p in range(groups):
            j = slice(p * units, (p + 1) * units)
            after = slice(hidden_units + p * units, hidden_units + (p + 1) * units)
            inner_grad = dot(gb, joined(ao_ref, bo_ref, j))
            inner_grad = (inner_grad * slope_ref[:, j]).astype(BF)
            in_grad = dot(normed_t, inner_grad)
            keep_ref[:, j] = in_grad[:half].astype(BF)
            send_ref[:, j] = in_grad[half:].astype(BF)
            out_grad = dot(gb_t, hidden_ref[:, j])
            keep_ref[:, after] = out_grad[:half].astype(BF)
            send_ref[:, after] = out_grad[half:].astype(BF)
            upstream = upstream + dot_t(inner_grad, joined(ai_ref, bi_ref, j))
        extra, gain4, beta4 = norm_back(upstream, stream3, norms_ref[3:4, :])
        nsums_ref[...] = channel_sums([gain4, beta4, gain5, beta5])
        grad = grad + extra
        grad_ref[...] = grad
        gb = grad.astype(BF)
        weight_grad = dot(gb.T, active)
        ckeep_ref[...] = weight_grad[:half].astype(BF)
        csend_ref[...] = weight_grad[half:].astype(BF)
        ngrad = dot(gb, wc) * swish_slope(normal)
        ngrad_ref[...] = ngrad
        own = channel_sums([jnp.sum(ngrad, 0, keepdims=True), jnp.sum(ngrad * scaled, 0, keepdims=True)])
        own_ref[...] = own
        one, three = edges_of(place_ref[0], ngrad[rows - HALO :], ngrad[:HALO])
        pack_1_ref[:8, :], pack_1_ref[8:, :] = own, one
        pack_3_ref[:8, :], pack_3_ref[8:, :] = own, three

    def block(columns, index):
        return pl.BlockSpec((half, columns), lambda g: (0, index), pipeline_mode=pl.Buffered(1))

    specs = [block(hidden_units, 0), block(hidden_units, 1)]
    return run(
        kernel,
        [(place, SMEM), (stream, None), (depth, None), (norms, None), (small, None)]
        + [(w, block(columns, 7)) for w in conv_halves] + [(w, spec) for spec in specs for w in halves] + [(cotangent, None)]
        + [(s, None) for s in sums],
        [((8, columns), F32, None), ((rows, width), BF, None), ((half, 2 * hidden_units), BF, None), ((half, 2 * hidden_units), BF, None),
         ((half, columns), BF, None), ((half, columns), BF, None), ((rows, width), F32, None), ((rows, columns), F32, None), ((8, columns), F32, None)]
        + [((8 + HALO, columns), F32, None)] * 2 + [((8, width), F32, None)],
        scratch=[pltpu.VMEM((rows, hidden_units), F32), pltpu.VMEM((rows, hidden_units), BF)],
        micros=12, limit=10, name="turn",
    )


def conv_backward(place, ngrad, ngrad_edges, depth, depth_edges, sums, totals, small, ker, gated, value_half, logistic, normed, halves, at,
                  keep, send, stream_grad, stream, norms, after):
    rows, columns = depth.shape
    width = normed.shape[1]
    groups, half, ext = columns // LANES, width // 2, rows + 2 * HALO
    span = rows * lax.axis_size("tensor")
    parts = len(totals)

    def kernel(place_ref, ngrad_ref, nb_ref, na_ref, depth_ref, db_ref, da_ref, sums_ref, small_ref, gated_ref, value_ref, gate_ref,
               normed_ref, av_ref, bv_ref, ag_ref, bg_ref, sgrad_ref, stream_ref, norms_ref, *refs):
        (ckeep_ref, csend_ref, keep_ref, send_ref, dtaps_ref, out_ref, gb_ref, nsums_ref, totals_ref, grad_ref, acc_ref, normed_t) = refs[parts:]
        length, start = place_ref[1], place_ref[2]
        step = pl.program_id(0)
        totals_ref[...] = sum(r[...] for r in refs[:parts])

        @pl.when(step == 0)
        def _():
            normed_t[...] = normed_ref[...].T
            acc_ref[...] = jnp.zeros_like(acc_ref)
            keep_ref[:, 2 * columns :] = ckeep_ref[...]
            send_ref[:, 2 * columns :] = csend_ref[...]

        taps = small_ref[...].astype(F32)
        count, mean, inv_std = batch_terms(sums_ref)
        batch_gain = taps[ker + 2 : ker + 3]
        sum_gain = batch_gain * totals_ref[0:1, :]
        sum_cross = batch_gain * totals_ref[1:2, :]
        square = inv_std * inv_std * sum_cross / count
        shift = mean * square - inv_std * sum_gain / count
        scale = inv_std * batch_gain
        for first, part, deep in ((0, nb_ref, db_ref), (HALO, ngrad_ref, depth_ref), (HALO + rows, na_ref, da_ref)):
            token = start + (first - HALO) + lax.broadcasted_iota(jnp.int32, part.shape, 0)
            grad = scale * part[...] + jnp.where(token < length, shift - deep[...] * square, 0.0)
            grad_ref[first : first + part.shape[0], :] = jnp.where(
                (token >= 0) & (token < span), grad, 0.0
            )
        own = grad_ref[HALO : HALO + rows, :]
        total = jnp.zeros((rows, LANES), F32)
        for k in range(ker):
            total = total + taps[k : k + 1, :] * grad_ref[ker - k : ker - k + rows, :]
            dtaps_ref[k : k + 1, :] = jnp.sum(
                own * gated_ref[k + 1 : k + 1 + rows, :], 0, keepdims=True
            )
        dtaps_ref[ker:, :] = jnp.zeros_like(dtaps_ref[ker:, :])
        token = start + lax.broadcasted_iota(jnp.int32, total.shape, 0)
        total = jnp.where(token < length, total, 0.0)
        logistic = gate_ref[...]
        dvalue = (total * logistic).astype(BF)
        dgate = (total * value_ref[...] * logistic * (1.0 - logistic)).astype(BF)
        pair = beside(dvalue, dgate)
        acc_ref[...] += dot_t(pair, beside(both(av_ref, bv_ref), both(ag_ref, bg_ref)))
        weight_grad = dot(normed_t[...], pair)
        cols = pl.ds(pl.multiple_of(2 * step * LANES, LANES), 2 * LANES)
        keep_ref[:, cols] = weight_grad[:half].astype(BF)
        send_ref[:, cols] = weight_grad[half:].astype(BF)

        @pl.when(step == groups - 1)
        def _():
            extra, dgain, dbeta = norm_back(acc_ref[...], stream_ref[...], norms_ref[2:3, :])
            out = sgrad_ref[...] + extra
            out_ref[...] = out
            gb_ref[...] = out.astype(BF)
            nsums_ref[...] = channel_sums([dgain, dbeta])

    edge = column(HALO)
    ins = [(place, SMEM), (ngrad, column(rows)), (ngrad_edges[0], edge), (ngrad_edges[1], edge), (depth, column(rows)), (depth_edges[0], edge), (depth_edges[1], edge),
           (sums, column(8)), (small, column(small.shape[0])), (gated, column(ext)), (value_half, column(rows)), (logistic, column(rows)),
           (normed, None)] + [(w, column(half, at + i * groups)) for i in (0, 1) for w in halves] + [
           (stream_grad, None), (stream, None), (norms, None)] + [(t, column(8)) for t in totals] + [(keep, None), (send, None)]
    return run(
        kernel, ins,
        [((half, 3 * columns), BF, None), ((half, 3 * columns), BF, None), ((32, columns), F32, column(32)),
         ((rows, width), F32, None), ((rows, width), BF, None), ((8, width), F32, None), ((8, columns), F32, column(8))],
        scratch=[pltpu.VMEM((ext, LANES), F32), pltpu.VMEM((rows, width), F32), pltpu.VMEM((width, rows), BF)],
        grid=(groups,), after=after, micros=8, name="conv_backward",
    )


def on_device(
    inputs,
    lengths,
    rel_embed,
    out_grad,
    norm_gain,
    norm_bias,
    ffn1_in_w,
    ffn1_out_w,
    query_w,
    key_w,
    value_w,
    pos_w,
    attn_out,
    pos_bias,
    conv_value,
    conv_gate,
    depthwise,
    bn_gain,
    bn_bias,
    conv_out,
    ffn2_in_w,
    ffn2_out_w,
):
    size_t = lax.axis_size("tensor")
    me_t = lax.axis_index("tensor")
    me_dp = lax.axis_index("dp")
    size_dp = lax.axis_size("dp")
    rows, width = inputs.shape[1], inputs.shape[2]
    shard = width // size_dp
    part, units = query_w.shape[1], ffn1_in_w.shape[1]
    channels, hidden_units = size_t * part, size_t * units
    span = rows * size_t
    ker = depthwise.shape[0]
    place = jnp.stack([me_t, lengths[0], me_t * rows]).astype(jnp.int32)

    first_shard = regroup([ffn1_in_w, ffn1_out_w.T], [units], name="pack_ffn1")
    first_parts = [first_shard] + tensor_swaps(first_shard)
    norm_cols = jnp.concatenate([norm_gain, norm_bias], 0)
    norm_cols = jnp.pad(norm_cols, ((0, LANES - norm_cols.shape[0]), (0, 0))).T
    norm_cols = regroup([norm_cols], [LANES], after=[first_shard], name="pack_norms")
    norm_cols = core_swap([norm_cols] + chip_swaps(norm_cols), name="rows_norms")
    small = jnp.concatenate([depthwise, pos_bias, bn_gain[None], bn_bias[None]], 0)
    step = max(shard, 16)
    small = jnp.pad(small, ((0, -small.shape[0] % step), (0, 0)))
    small = [small[i : i + shard] for i in range(0, small.shape[0], shard)]
    attn_shard = regroup(
        [query_w, key_w, value_w, pos_w, attn_out.T, conv_value, conv_gate, conv_out.T],
        [part], small, after=first_parts[1:], name="pack_attn",
    )
    attn_parts = [attn_shard] + tensor_swaps(attn_shard)
    second_shard = regroup(
        [ffn2_in_w, ffn2_out_w.T], [units], after=attn_parts[1:], name="pack_second"
    )
    second_parts = [second_shard] + tensor_swaps(second_shard)

    feature = jnp.arange(width)
    block = feature // shard
    mask_of = (block & ~7) | ((block >> 2) & 1) | ((block & 3) << 1)
    source = (mask_of ^ me_dp) * shard + feature % shard
    order = (jnp.arange(width)[:, None] == source[None, :]).astype(BF)
    stream0 = dot(inputs[0], order)
    cotangent = dot(out_grad[0], order)
    wide = -(-(span + rows) // LANES) * LANES
    rel_rows = jnp.pad(rel_embed, ((0, span + wide - rel_embed.shape[0]), (0, 0)))
    rel_rows = lax.dynamic_slice_in_dim(rel_rows, rows * (size_t - 1 - me_t), wide, 0)
    rel_rows = dot(rel_rows, order).astype(BF)

    norms, normed_one = first_norm(stream0, norm_cols)
    first_block = regroup(first_parts, [units] * 2, after=[normed_one], name="cols_ffn1")
    first_blocks = [first_block] + plane_swaps(first_block, name="halves_ffn1")[0]
    attn_block = regroup(attn_parts, [part] * 8, name="cols_attn")
    attn_blocks = [attn_block] + chip_swaps(attn_block)
    if len(small) == 1:
        small = regroup(attn_parts, [part], skip=8 * part, name="cols_small")
    else:
        pieces = [cut_columns(p[:, 8 * part :], [LANES] * len(small)) for p in attn_parts]
        small = jnp.concatenate([jnp.concatenate(p, 0) for p in pieces], 1)
    first_w = core_swap(first_blocks, after=[attn_block, rel_rows, small, *second_parts[1:]], name="rows_ffn1")
    slope_one, stream1, normed_two = ffn1_forward(
        stream0, normed_one, first_w, norms, []
    )
    tokens = lax.all_gather(normed_two, "tensor", axis=0, tiled=True)
    second_block = regroup(second_parts, [units] * 2, after=[tokens], name="cols_second")
    attn_w = core_swap(attn_blocks, after=[tokens], name="rows_attn")
    query_u, query_v, positions, table = attn_queries(
        normed_two, attn_w, rel_rows, small, span, ker, []
    )
    normed_one = regroup([normed_one], [width], after=attn_w[:1], name="carry_norm")
    first_tokens = [normed_one] + tensor_swaps(normed_one)
    mixed, probs, keys, vals, stream2, normed_three, edge_1, edge_3 = attn_main(
        place, tokens, attn_w, query_u, table, stream1, norms, []
    )
    hidden, slope, normed_t = ffn1_hidden(place, first_tokens, first_w, units, [stream2])
    swaps, halves = plane_swaps(second_block, [stream2], "halves_second")
    second_blocks = [second_block] + swaps
    gated, value_half, logistic, depth, sums, *packs = conv_forward(
        place, normed_three, swap(edge_1, "tensor", 1), swap(edge_3, "tensor", 3), attn_w,
        5 * channels // LANES, small, ker, [hidden, halves[0]],
    )
    second_w = core_swap(second_blocks, after=[sums], name="rows_second")
    sums, *depth_edges = sum_tensor(place, sums, [packs[0], sums, packs[1]], "sums_forward")
    sums, block_out, keep, send, out_keep, out_send, stream_grad, ngrad, totals, *packs, norm_sums_4 = turn(
        place, stream2, depth, sum_dp(sums), norms, small, ker, attn_w, second_w, cotangent
    )
    other = core_other(send)
    block_out = dot(block_out, order, ((1,), (1,))).astype(BF)
    totals, *ngrad_edges = sum_tensor(place, totals, [packs[0], totals, packs[1]], "sums_back")
    conv_keep, conv_send, taps_grad, stream_grad, gb, norm_sums_2, totals = conv_backward(
        place, ngrad, ngrad_edges, depth, depth_edges, sums, sum_dp(totals), small, ker, gated,
        value_half, logistic, normed_three, attn_w, 5 * channels // LANES, out_keep, out_send, stream_grad, stream2, norms, [other],
    )
    second_parts = reduce_core_pairs(
        [(keep, other), (conv_keep, core_other(conv_send))], "core_second"
    )
    came = plane_first(second_parts)
    gp, dk, dv, own_keys, *others = attn_back_keys(
        place, gb, attn_w, probs, keys, vals, query_u, size_t, [second_parts[1], block_out]
    )
    others = [swap(o, "tensor", m) for m, o in enumerate(others, 1)]
    second_parts = plane_second(second_parts, came, [own_keys], "plane_second")
    plane_done = second_parts[4:]
    second_parts = second_parts[:4]
    keeps, sends, own = attn_back_queries(
        gp, keys, positions, query_v, dk, dv, mixed, gb, normed_two, tokens, rel_rows, attn_w,
        taps_grad, plane_done,
    )
    attn_parts = reduce_core_pieces(keeps, sends, 16, "core_attn")
    came = plane_first(attn_parts)
    stream_grad, gb, norm_sums_1 = ffn1_branch_grad(
        sum_parts([own_keys, own, *others], "sum_normed"), stream_grad, stream1, norms,
        [],
    )
    input_grad, norm_rows, gb = ffn1_back_tokens(
        stream_grad, gb, stream0, norms, slope_one, first_w,
        [norm_sums_1, norm_sums_2, norm_sums_4], attn_parts[1:2],
    )
    gb_all = lax.all_gather(gb, "tensor", axis=0, tiled=True)
    attn_parts = plane_second(attn_parts, came, [gb_all], "plane_attn")
    plane_done, attn_parts = attn_parts[4:], attn_parts[:4]
    keep, send = ffn1_back_weights(gb_all, hidden, slope, normed_t, first_w, norm_rows, [*second_parts[1:3], *plane_done])
    first_parts = reduce_core_pairs([(keep, core_other(send))], "core_ffn1")
    core_done = first_parts[1:2]
    first_parts = plane_second(first_parts, plane_first(first_parts), name="plane_ffn1")[:4]
    widths = [units, units, 2 * part, part]
    second_cuts = reduce_split(second_parts, widths, after=core_done, name="split_second")
    flat, square = (shard, part), (shard, units)

    def pick(total):
        wide, out, pair, conv = cut_columns(total, widths)
        return [wide, out, pair[:, :part], pair[:, part:], conv]

    second_in_grad, second_out_grad, values_grad, gates_grad, outs_grad = finish(
        second_cuts, [square, square, flat, flat, flat], pick, "finish_second"
    )
    first_sum = first_parts[0] + sum(p.astype(F32) for p in first_parts[1:3])
    first_in_grad, first_out_grad, norm_cols = cut_columns(first_sum, [units, units, LANES])
    attn_cuts = reduce_split(attn_parts, [part] * 5, norm_cols, name="split_attn")

    def pick(total):
        columns = cut_columns(total, [part] * 5 + [LANES])
        norms = columns[5][:shard].T
        taps = jnp.concatenate([columns[0][shard:], columns[1][shard:]], 0)
        grads = [c[:shard] for c in columns[:5]]
        return grads + [norms[0:5], norms[5:10], taps[:ker], columns[2][shard : shard + 2]]

    query_grad, key_grad, value_grad, pos_grad, attn_grad, gain_grad, beta_grad, taps_grad, bias_grad = finish(
        attn_cuts, [flat] * 5 + [(5, shard), (5, shard), (ker, part), (2, part)], pick, "finish_attn"
    )

    input_grad = dot(input_grad, order.astype(F32), ((1,), (1,)), precision=HIGHEST)
    return (
        block_out[None],
        input_grad[None],
        gain_grad,
        beta_grad,
        first_in_grad,
        first_out_grad.T,
        query_grad,
        key_grad,
        value_grad,
        pos_grad,
        attn_grad.T,
        bias_grad,
        values_grad,
        gates_grad,
        taps_grad,
        totals[1, :part],
        totals[0, :part],
        outs_grad.T,
        second_in_grad,
        second_out_grad.T,
    )


def solution(mesh):
    return jax.shard_map(
        on_device,
        mesh=mesh,
        in_specs=(
            P("dp", "tensor", None),
            P("dp"),
            P(),
            P("dp", "tensor", None),
            P(None, "dp"),
            P(None, "dp"),
            P("dp", "tensor"),
            P("tensor", "dp"),
            P("dp", "tensor"),
            P("dp", "tensor"),
            P("dp", "tensor"),
            P("dp", "tensor"),
            P("tensor", "dp"),
            P(None, "tensor"),
            P("dp", "tensor"),
            P("dp", "tensor"),
            P(None, "tensor"),
            P("tensor"),
            P("tensor"),
            P("tensor", "dp"),
            P("dp", "tensor"),
            P("tensor", "dp"),
        ),
        out_specs=(
            P("dp", "tensor", None),
            P("dp", "tensor", None),
            P(None, "dp"),
            P(None, "dp"),
            P("dp", "tensor"),
            P("tensor", "dp"),
            P("dp", "tensor"),
            P("dp", "tensor"),
            P("dp", "tensor"),
            P("dp", "tensor"),
            P("tensor", "dp"),
            P(None, "tensor"),
            P("dp", "tensor"),
            P("dp", "tensor"),
            P(None, "tensor"),
            P("tensor"),
            P("tensor"),
            P("tensor", "dp"),
            P("dp", "tensor"),
            P("tensor", "dp"),
        ),
        check_vma=False,
    )
```
